32 devices in a mesh: grp: 4 (over z), rep: 8 (over y, x, core).
Axes of the slice: x: 2, y: 2, z: 4, core: 2. Of those that a mesh axis runs over, the one named last changes fastest.
Arguments:
- tokens: bfloat16 [64, 512, 768], P(('grp', 'rep')), may hold values from -6 to 6
- lengths: int32 [64], P(('grp', 'rep')), may hold values from 1 to 512, 19660 in all
- cotangent: bfloat16 [64, 512, 768], P(('grp', 'rep')), may hold values from -6 to 6
- query_weight: bfloat16 [768, 768], P('grp'), may hold values from -0.21875 to 0.21875
- query_bias: bfloat16 [768], P('grp'), may hold values from -1.75 to 1.75
- key_weight: bfloat16 [768, 768], P('grp'), may hold values from -0.21875 to 0.21875
- value_weight: bfloat16 [768, 768], P('grp'), may hold values from -0.21875 to 0.21875
- value_bias: bfloat16 [768], P('grp'), may hold values from -1.75 to 1.75
- out_weight: bfloat16 [768, 768], P('grp'), may hold values from -1.75 to 1.75
- out_bias: bfloat16 [768], P('grp'), may hold values from -1.75 to 1.75
- norm_gain: bfloat16 [768], P('grp'), may hold values from 0.5 to 1.5
- norm_shift: bfloat16 [768], P('grp'), may hold values from -1.75 to 1.75
- up_weight: bfloat16 [768, 3072], P('grp'), may hold values from -0.21875 to 0.21875
- up_bias: bfloat16 [3072], P('grp'), may hold values from -3 to 3
- down_weight: bfloat16 [3072, 768], P('grp'), may hold values from -0.109375 to 0.109375
- down_bias: bfloat16 [768], P('grp'), may hold values from -1.75 to 1.75
- final_gain: bfloat16 [768], P('grp'), may hold values from 0.5 to 1.5
- final_shift: bfloat16 [768], P('grp'), may hold values from -1.75 to 1.75
Outputs:
- output: bfloat16 [64, 512, 768], P(('grp', 'rep'))
- grad_tokens: bfloat16 [64, 512, 768], P(('grp', 'rep'))
- grad_query_weight: float32 [768, 768], P('grp')
- grad_query_bias: float32 [768], P('grp')
- grad_key_weight: float32 [768, 768], P('grp')
- grad_value_weight: float32 [768, 768], P('grp')
- grad_value_bias: float32 [768], P('grp')
- grad_out_weight: float32 [768, 768], P('grp')
- grad_out_bias: float32 [768], P('grp')
- grad_norm_gain: float32 [768], P('grp')
- grad_norm_shift: float32 [768], P('grp')
- grad_up_weight: float32 [768, 3072], P('grp')
- grad_up_bias: float32 [3072], P('grp')
- grad_down_weight: float32 [3072, 768], P('grp')
- grad_down_bias: float32 [768], P('grp')
- grad_final_gain: float32 [768], P('grp')
- grad_final_shift: float32 [768], P('grp')
The draws below stay inside these ranges and needn't reach their ends.
Inputs may be any that keep to these rules, and one draw needn't show every extreme that they name: Every pair has at least one token; slots from lengths on are padding.
All inputs are finite; a program needn't handle non-finite values. No bound on the sum of `lengths` on one device may be relied on, other than what follows from the above.
Results may differ from the reference program's by a relative error of at most 0.017.
Values may be sent and summed in bfloat16 or wider, within the bound.
No kernel may reach another device: no remote copies, remote signals or barrier semaphores. Data moves between devices by JAX's collectives and lax.ppermute only.
A program may use at most 192 MiB of HBM per device.

```python
import math
import jax
import jax.numpy as jnp
import numpy as np
from jax import lax

D = 768
H = 12
HD = 64
FF = 3072
SEQ = 512
PAIRS = 64


def steps_of(key, shape, split, smallest, largest):
    factor_of, own = 1.0, jax.random.fold_in(key, 6)
    for axis_at, parts in split:
        heights = jnp.exp(jax.random.uniform(jax.random.fold_in(own, axis_at), (parts,), jnp.float32, smallest / len(split), largest / len(split)))
        factor_of = factor_of * jnp.repeat(heights, shape[axis_at] // parts).reshape([-1 if axis == axis_at else 1 for axis in range(len(shape))])
    return factor_of


def length_profile(number_of, total, bound, skew):
    weights = [(1 << 20) // math.isqrt(rank ** skew) + 1 for rank in range(2, number_of + 1)]
    spare, holding = total - bound - (number_of - 1), [1] * (number_of - 1)
    while spare > 0:
        candidates = [i for i in range(number_of - 1) if holding[i] < bound]
        pool, remaining = sum([weights[i] for i in candidates]), spare
        for i in candidates:
            addition = min(bound - holding[i], max(1, remaining * weights[i] // pool), spare)
            holding[i] = holding[i] + addition
            spare = spare - addition
    return np.array([bound] + holding)


def ragged(stream_key, count, total, bound, lean):
    if count == 2:
        one = jax.random.randint(stream_key, (), max(1, total - bound), min(bound, total - 1) + 1)
        return jnp.stack([one, total - one])
    tallies = jnp.asarray(length_profile(count, total, bound, lean), jnp.int32)
    pairs = (count - 1) // 2
    giver, taker = tallies[1:1 + 2 * pairs:2], tallies[2:2 + 2 * pairs:2]
    margin = jnp.minimum(giver - 1, bound - taker)
    passed = jax.random.randint(jax.random.fold_in(stream_key, 1), (pairs,), 0, 1 << 20) % (margin + 1)
    tallies = tallies.at[1:1 + 2 * pairs:2].set(giver - passed).at[2:2 + 2 * pairs:2].set(taker + passed)
    return tallies[jax.random.permutation(jax.random.fold_in(stream_key, 2), count)]


def normal_values(own_key, extent, deviation, reach, cuts=(), held_as=jnp.bfloat16):
    result = deviation * jax.random.normal(own_key, extent, jnp.float32)
    if cuts:
        result = result * steps_of(own_key, extent, cuts, -0.22, 0.18)
    return jnp.clip(result, -reach, reach).astype(held_as)


def setup_inputs(seed: int = 0) -> dict:
    splits = jax.random.split(jax.random.key(seed), 19)
    return {
        "tokens": normal_values(splits[0], (PAIRS, SEQ, D), 1.0, 6.0, ((0, 32),)),
        "lengths": ragged(splits[1], PAIRS, PAIRS * SEQ * 3 // 5, SEQ, 2).astype(jnp.int32),
        "cotangent": normal_values(splits[2], (PAIRS, SEQ, D), 1.0, 6.0, ((0, 32),)),
        "query_weight": normal_values(splits[3], (D, D), D ** -0.5, 0.21875, ((0, 4),)),
        "query_bias": normal_values(splits[4], (D,), 0.3, 1.75, ((0, 4),)),
        "key_weight": normal_values(splits[5], (D, D), D ** -0.5, 0.21875, ((0, 4),)),
        "value_weight": normal_values(splits[6], (D, D), D ** -0.5, 0.21875, ((0, 4),)),
        "value_bias": normal_values(splits[7], (D,), 0.3, 1.75, ((0, 4),)),
        "out_weight": normal_values(splits[8], (D, D), (D // 64) ** -0.5, 1.75, ((0, 4),)),
        "out_bias": normal_values(splits[9], (D,), 0.3, 1.75, ((0, 4),)),
        "norm_gain": jnp.clip(1.0 + 0.1 * jax.random.normal(splits[10], (D,), jnp.float32), 0.5, 1.5).astype(jnp.bfloat16),
        "norm_shift": normal_values(splits[11], (D,), 0.3, 1.75, ((0, 4),)),
        "up_weight": normal_values(splits[12], (D, FF), D ** -0.5, 0.21875, ((0, 4),)),
        "up_bias": normal_values(splits[13], (FF,), 0.5, 3.0, ((0, 4),)),
        "down_weight": normal_values(splits[14], (FF, D), FF ** -0.5, 0.109375, ((0, 4),)),
        "down_bias": normal_values(splits[15], (D,), 0.3, 1.75, ((0, 4),)),
        "final_gain": jnp.clip(1.0 + 0.1 * jax.random.normal(splits[16], (D,), jnp.float32), 0.5, 1.5).astype(jnp.bfloat16),
        "final_shift": normal_values(splits[17], (D,), 0.3, 1.75, ((0, 4),)),
    }


EPSILON = 1e-06

@jax.custom_vjp
def low(v):
    return lax.optimization_barrier(v.astype(jnp.bfloat16)).astype(jnp.float32)

@jax.custom_vjp
def low_back(v):
    return v

def low_keep(v):
    return (low(v), None)

def low_pass(kept, grad):
    return (grad,)

def back_keep(v):
    return (v, None)

def back_low(kept, grad):
    return (low(grad),)
low.defvjp(low_keep, low_pass)
low_back.defvjp(back_keep, back_low)

def exact(left, right):
    return jnp.dot(left, right, precision=lax.Precision.HIGHEST)

def layer_norm(values, gain, shift):
    centred = values - lax.optimization_barrier(jnp.mean(values, axis=-1, keepdims=True))
    spread = lax.optimization_barrier(jnp.mean(centred * centred, axis=-1, keepdims=True))
    return centred * lax.rsqrt(spread + EPSILON) * gain + shift

def one_pair(weights, inputs, usable):
    mat_query, bias_query, mat_key, mat_value, bias_value, mat_out, bias_out, gain_first, shift_first, mat_up, bias_up, mat_down, bias_down, gain_last, shift_last = weights
    seqlen = inputs.shape[0]
    scaling = HD ** (-0.5)
    inputs_low = low(inputs)
    queries = low(low_back(exact(inputs_low, mat_query) + bias_query)).reshape(seqlen, H, HD)
    key_rows = low(low_back(exact(inputs_low, mat_key))).reshape(seqlen, H, HD)
    values_all = low(low_back(exact(inputs_low, mat_value) + bias_value)).reshape(seqlen, H, HD)
    scores = jnp.einsum('qhd,khd->hqk', queries, key_rows, precision=lax.Precision.HIGHEST) * scaling
    scores = low_back(scores)
    scores = jnp.where(usable[None, None, :], scores, -1e+30)
    probs = low(jax.nn.softmax(scores, axis=-1))
    mixed = jnp.einsum('hqk,khd->qhd', probs, values_all, precision=lax.Precision.HIGHEST).reshape(seqlen, D)
    mixed = low(low_back(mixed))
    branch = low_back(exact(mixed, mat_out) + bias_out)
    hidden = layer_norm(inputs + branch, gain_first, shift_first)
    hidden_low = low(hidden)
    expanded = low_back(exact(hidden_low, mat_up) + bias_up)
    activated = low(jax.nn.gelu(expanded, approximate=False))
    second = hidden + low_back(exact(activated, mat_down) + bias_down)
    return layer_norm(second, gain_last, shift_last) * usable[:, None].astype(jnp.float32)

def reference(tokens, lengths, cotangent, query_weight, query_bias, key_weight, value_weight, value_bias, out_weight, out_bias, norm_gain, norm_shift, up_weight, up_bias, down_weight, down_bias, final_gain, final_shift):
    weights = tuple((array.astype(jnp.float32) for array in (query_weight, query_bias, key_weight, value_weight, value_bias, out_weight, out_bias, norm_gain, norm_shift, up_weight, up_bias, down_weight, down_bias, final_gain, final_shift)))
    slots = jnp.arange(SEQ, dtype=jnp.int32)
    usable = slots[None, :] < lengths[:, None].astype(jnp.int32)
    stepper = jax.checkpoint(one_pair)

    def forward(inputs, params):

        def run(operands):
            return stepper(params, operands[0], operands[1])
        return lax.map(run, (inputs, usable))
    outputs, pull = jax.vjp(forward, tokens.astype(jnp.float32), weights)
    grad_inputs, grads = pull(cotangent.astype(jnp.float32))
    return (outputs.astype(jnp.bfloat16), grad_inputs.astype(jnp.bfloat16), grads[0], grads[1], grads[2], grads[3], grads[4], grads[5], grads[6], grads[7], grads[8], grads[9], grads[10], grads[11], grads[12], grads[13], grads[14])
```

```python
import functools

import jax
import jax.numpy as jnp
from jax import lax
from jax.experimental import pallas as pl
from jax.experimental.pallas import tpu as pltpu
from jax.sharding import PartitionSpec as P

H = 12
HD = 64
EPSILON = 1e-06
MASKED = -1e30
DENSITY = 0.3989422804014327

f32 = jnp.float32
bf16 = jnp.bfloat16
VMEM = pl.BlockSpec(memory_space=pltpu.VMEM)
SMEM = pl.BlockSpec(memory_space=pltpu.SMEM)
ANY = pl.BlockSpec(memory_space=pl.ANY)
VMEM_LIMIT = 56 * 2**20
COLS = 384
LOCAL = 8


def dot(a, b):
    return jnp.dot(a, b, preferred_element_type=f32)


def nt(a, b):
    return lax.dot_general(a, b, (((1,), (1,)), ((), ())), preferred_element_type=f32)


def tn(a, b):
    return lax.dot_general(a, b, (((0,), (0,)), ((), ())), preferred_element_type=f32)


def shape(dims, dtype):
    return jax.ShapeDtypeStruct(dims, dtype)


def al(value, by):
    return pl.multiple_of(value, by)


def call(kernel, outs, args, specs, out_specs, scratch=(), grid=(), flops=0, moved=0):
    return pl.pallas_call(
        kernel,
        grid=grid,
        out_shape=outs,
        in_specs=specs,
        out_specs=out_specs,
        scratch_shapes=scratch,
        compiler_params=pltpu.CompilerParams(vmem_limit_bytes=VMEM_LIMIT),
        cost_estimate=pl.CostEstimate(flops=flops, bytes_accessed=moved, transcendentals=0),
    )(*args)


def to_rep(array, bit):
    size = lax.axis_size("rep")
    return lax.ppermute(array, "rep", [(i, i ^ bit) for i in range(size)])


def to_grp(array, step):
    size = lax.axis_size("grp")
    return lax.ppermute(array, "grp", [(i, (i + step) % size) for i in range(size)])


def position():
    z = lax.axis_index("grp").astype(jnp.int32)
    p = lax.axis_index("rep").astype(jnp.int32) % LOCAL
    return jnp.stack([z, (p // 2) % 2, p // 4, p % 2, p])


class Copies:
    def __init__(self, sems):
        self.sems, self.held = sems, []

    def add(self, src, dst):
        copy = pltpu.make_async_copy(src, dst, self.sems.at[len(self.held)])
        copy.start()
        self.held.append(copy)

    def wait(self):
        for copy in self.held:
            copy.wait()


def piece_refs(kind, ref, zone, p, depth):
    if kind == "tall":
        rows = depth // LOCAL
        start = al(zone * depth + p * rows, 16)
        return [
            (ref.at[pl.ds(start, rows), pl.ds(half * COLS, COLS)], rows) for half in range(2)
        ]
    if kind == "wide":
        rows = depth // 2
        start = al(zone * depth + (p % 2) * rows, 16)
        return [
            (
                ref.at[pl.ds(start, rows), pl.ds(al((p // 2) * 2 * COLS + half * COLS, 128), COLS)],
                rows,
            )
            for half in range(2)
        ]
    rows = depth // 4
    offset = int(kind)
    start = al(zone * depth + (p // 2) * rows, 16)
    return [(ref.at[pl.ds(start, rows), pl.ds(al(offset + (p % 2) * COLS, 128), COLS)], rows)]


def own_slab(ref, zone, depth, first=0, width=None):
    width = ref.shape[1] if width is None else width
    return ref.at[pl.ds(al(zone * depth, 16), depth), pl.ds(first, width)]


def fetch(copies, pos, parts, mine, sibling):
    zone, p = pos[0], pos[4]
    groups = lax.axis_size("grp")
    for sib, held in ((0, mine), (1, sibling)):
        for other in range(4):
            owner = p ^ (other * 2) ^ sib
            for step in range(1, groups):
                source = lax.rem(zone + groups - step, groups)
                total = sum(
                    rows for kind, ref, depth in parts for _, rows in piece_refs(kind, ref, 0, 0, depth)
                )
                at = (other * (groups - 1) + step - 1) * total
                for kind, ref, depth in parts:
                    for place, rows in piece_refs(kind, ref, source, owner, depth):
                        copies.add(held.at[pl.ds(at, rows), :], place)
                        at += rows


def emit(copies, pos, parts, send, keep):
    core = pos[3]
    groups = lax.axis_size("grp")
    for held, flip in ((send, 1), (keep, 0)):
        for zone in range(groups):
            for q in range(4):
                owner = q * 2 + (core ^ flip)
                at = 0
                for kind, ref, depth in parts:
                    for place, rows in piece_refs(kind, ref, zone, owner, depth):
                        copies.add(place, held.at[zone, q, pl.ds(at, rows), :])
                        at += rows


def spread(own, n):
    groups = lax.axis_size("grp")
    mine = jnp.concatenate([to_grp(own, step)[:n] for step in range(1, groups)], axis=0)
    total = mine.shape[0]
    cut = (total // 2 + 47) // 48 * 48
    from_x = to_rep(mine, 2)
    from_y = to_rep(mine, 4)
    corner_low = to_rep(from_x[:cut], 4)
    corner_high = to_rep(from_y[cut:], 2)
    held = jnp.concatenate([mine, from_x, from_y, corner_low, corner_high], axis=0)
    return held, to_rep(held, 1)


def add_first(pos, keep, got, sa, ka, sb, kb):
    x, y = pos[1], pos[2]
    half = keep.shape[0] // 2
    for zone in range(half):
        for j in range(2):
            for ref, q in ((sa, j * 2 + (1 - x)), (ka, j * 2 + x)):
                ref[zone, j] = (keep[zone, q].astype(f32) + got[zone, q].astype(f32)).astype(bf16)
            for ref, q in ((sb, (1 - y) * 2 + j), (kb, y * 2 + j)):
                ref[zone, j] = (
                    keep[half + zone, q].astype(f32) + got[half + zone, q].astype(f32)
                ).astype(bf16)


def add_second(pos, ka, ra, kb, rb, sa, ja, sb, jb):
    x, y = pos[1], pos[2]
    for zone in range(ka.shape[0]):
        for kept, got, send, hold, at in ((ka, ra, sa, ja, y), (kb, rb, sb, jb, x)):
            send[zone] = (kept[zone, 1 - at].astype(f32) + got[zone, 1 - at].astype(f32)).astype(bf16)
            hold[zone] = (kept[zone, at].astype(f32) + got[zone, at].astype(f32)).astype(bf16)


def add_third(pos, ka, ra, kb, rb, *rest):
    outs, total = rest[:-1], rest[-1]
    half = ka.shape[0]
    for zone in range(half):
        total[zone] = (ka[zone].astype(f32) + ra[zone].astype(f32)).astype(bf16)
        total[half + zone] = (kb[zone].astype(f32) + rb[zone].astype(f32)).astype(bf16)
    for step, out in enumerate(outs):
        out[...] = total[lax.rem(pos[0] + step, 2 * half)]


def add_fourth(*refs):
    total = refs[0][...].astype(f32)
    for ref in refs[1:-1]:
        total = total + ref[...].astype(f32)
    refs[-1][...] = total.astype(bf16)


def reduce_group(pos, send, keep):
    groups, _, n, _ = keep.shape
    half = groups // 2
    size = groups * 4 * n * COLS * 2
    got = to_rep(send, 1)
    quad = shape((half, 2, n, COLS), bf16)
    sa, ka, sb, kb = call(
        add_first, (quad,) * 4, (pos, keep, got), [SMEM, VMEM, VMEM], (VMEM,) * 4, moved=3 * size
    )
    ra, rb = to_rep(sa, 2), to_rep(sb, 4)
    pair = shape((half, n, COLS), bf16)
    sa, ka, sb, kb = call(
        add_second,
        (pair,) * 4,
        (pos, ka, ra, kb, rb),
        [SMEM] + [VMEM] * 4,
        (VMEM,) * 4,
        moved=3 * size // 2,
    )
    ra, rb = to_rep(sa, 4), to_rep(sb, 2)
    one = shape((n, COLS), bf16)
    blocks = call(
        add_third,
        (one,) * groups,
        (pos, ka, ra, kb, rb),
        [SMEM] + [VMEM] * 4,
        (VMEM,) * groups,
        scratch=[pltpu.VMEM((groups, n, COLS), bf16)],
        moved=3 * size // 4,
    )
    arrived = [to_grp(blocks[step], step) for step in range(1, groups)]
    total = call(
        add_fourth, one, (blocks[0], *arrived), [VMEM] * groups, VMEM, moved=size // 3
    )
    bit = LOCAL
    while bit < lax.axis_size("rep"):
        other = to_rep(total, bit)
        total = call(add_fourth, one, (total, other), [VMEM] * 2, VMEM, moved=size // 5)
        bit *= 2
    return total


def share_group(total):
    held = jnp.concatenate([total, to_rep(total, 2), to_rep(total, 4), to_rep(total, 6)], axis=0)
    return held, to_rep(held, 1)


def cut_weights(pos, wq, wk, wv, wo, wu, wd, vectors, first, second, third, sems):
    p = pos[4]
    copies = Copies(sems)
    depth = wq.shape[0]
    for out, parts in (
        (first, (("0", wq, depth), ("0", wk, depth), ("0", wv, depth))),
        (second, (("wide", wu, depth), ("0", wo, depth))),
        (third, (("tall", wd, wd.shape[0]),)),
    ):
        at = 0
        for kind, ref, rows_of in parts:
            for place, rows in piece_refs(kind, ref, 0, p, rows_of):
                copies.add(place, out.at[pl.ds(at, rows), :])
                at += rows
        if out is first:
            copies.add(vectors, out.at[pl.ds(at, vectors.shape[0]), :])
    copies.wait()


def layer_norm(values):
    centred = values - jnp.mean(values, axis=-1, keepdims=True)
    spread_of = jnp.mean(centred * centred, axis=-1, keepdims=True)
    inverse = lax.rsqrt(spread_of + EPSILON)
    return centred * inverse, inverse


def norm_back(upstream, normed, inverse, gain):
    scaled = upstream * gain
    return inverse * (
        scaled
        - jnp.mean(scaled, axis=-1, keepdims=True)
        - normed * jnp.mean(scaled * normed, axis=-1, keepdims=True)
    )


def attend(pos, lengths, x, wq, wk, wv, mine, sibling, vectors, q_out, k_out, v_out, mixed, logsum, w_out, weight, sems):
    pair = pl.program_id(0)
    depth = wq.shape[0]
    width = wq.shape[1]

    @pl.when(pair == 0)
    def _():
        copies = Copies(sems)
        for m, ref in enumerate((wq, wk, wv)):
            copies.add(ref, own_slab(weight, pos[0], depth, m * width, width))
        parts = [(str(m * width), weight, depth) for m in range(3)]
        fetch(copies, pos, parts, mine, sibling)
        copies.wait()

    write = pltpu.make_async_copy(weight, w_out, sems.at[sems.shape[0] - 1])

    @pl.when(pair == 0)
    def _():
        write.start()

    rows = x[...]
    scaling = HD ** (-0.5)
    q_out[...] = (
        (dot(rows, weight[:, :width]) + vectors[0:1, :]).astype(bf16).astype(f32) * scaling
    ).astype(bf16)
    k_out[...] = dot(rows, weight[:, width : 2 * width]).astype(bf16)
    v_out[...] = (dot(rows, weight[:, 2 * width :]) + vectors[1:2, :]).astype(bf16)
    slots = rows.shape[0]
    lane = lax.broadcasted_iota(jnp.int32, (slots, 128), 1)
    low = lane < HD
    slot = lax.broadcasted_iota(jnp.int32, (1, slots), 1)
    bias = jnp.where(slot < lengths[pair], 0.0, MASKED).astype(f32)

    def heads(h, sums):
        s = pl.ds(al(h * 128, 128), 128)
        q1, k1, v1 = q_out[:, s], k_out[:, s], v_out[:, s]
        results = []
        for e in range(2):
            mask = low if e == 0 else ~low
            scores = nt(jnp.where(mask, q1, 0).astype(bf16), k1) + bias
            peak = jnp.max(scores, axis=1, keepdims=True)
            expo = jnp.exp(scores - peak)
            total = jnp.sum(expo, axis=1, keepdims=True)
            results.append(dot(expo.astype(bf16), v1) * (1.0 / total))
            sums = jnp.where(lane == h * 2 + e, peak + jnp.log(total), sums)
        mixed[:, s] = jnp.where(low, results[0], results[1]).astype(bf16)
        return sums

    sums = lax.fori_loop(0, H // 2, heads, jnp.zeros((slots, 128), f32), unroll=2)
    logsum[0] = sums.T[:16]

    @pl.when(pair == pl.num_programs(0) - 1)
    def _():
        write.wait()


def expand(pos, x, mixed, wu, wo, mine, sibling, vectors, up_bias, act, slope, normed, inverse, wu_out, wo_out, up, out_w, sems):
    step = pl.program_id(0)
    depth = wo.shape[0]
    last = sems.shape[0]
    writes = [
        pltpu.make_async_copy(up, wu_out, sems.at[last - 1]),
        pltpu.make_async_copy(out_w, wo_out, sems.at[last - 2]),
    ]

    @pl.when(step == 0)
    def _():
        copies = Copies(sems)
        copies.add(wu, own_slab(up, pos[0], depth))
        copies.add(wo, own_slab(out_w, pos[0], depth))
        fetch(copies, pos, [("wide", up, depth), ("0", out_w, depth)], mine, sibling)
        copies.wait()
        for write in writes:
            write.start()

    first = x[...].astype(f32) + dot(mixed[...], out_w[...]) + vectors[2:3, :]
    normal, scale = layer_norm(first)
    normed[...] = normal
    inverse[...] = jnp.broadcast_to(scale, inverse.shape)
    hidden = (normal * vectors[3:4, :] + vectors[4:5, :]).astype(bf16)
    chunk = 768
    for j in range(up.shape[1] // chunk):
        s = slice(j * chunk, (j + 1) * chunk)
        u = dot(hidden, up[:, s]) + up_bias[:, s]
        cdf, pdf = gaussian(u)
        act[:, s] = (u * cdf).astype(bf16)
        slope[:, s] = (cdf + u * pdf).astype(bf16)

    @pl.when(step == pl.num_programs(0) - 1)
    def _():
        for write in writes:
            write.wait()


def gaussian(u):
    density = jnp.exp(-0.5 * u * u)
    t = 1.0 / (1.0 + (0.3275911 * 0.7071067811865476) * jnp.abs(u))
    series = t * (
        0.127414796
        + t * (-0.142248368 + t * (0.7107068705 + t * (-0.7265760135 + t * 0.5307027145)))
    )
    tail = series * density
    return jnp.where(u < 0, tail, 1.0 - tail), density * DENSITY


def contract(lengths, act, normed, cotangent, wd, mine, sibling, pos, vectors, output, grad_second, send, keep, sums, wd_out, down, acts, lows, grads, sems, act_sems, out_sems):
    step = pl.program_id(0)
    blocks = pl.num_programs(0) - 1
    depth = wd.shape[0]
    rows = normed.shape[0]
    write = pltpu.make_async_copy(down, wd_out, sems.at[sems.shape[0] - 1])

    def part(i):
        return pltpu.make_async_copy(
            act.at[pl.ds(al(i * rows, 16), rows), :],
            acts.at[pl.ds(al(i * rows, 16), rows), :],
            act_sems.at[i],
        )

    @pl.when(step == 0)
    def _():
        copies = Copies(sems)
        copies.add(wd, own_slab(down, pos[0], depth))
        fetch(copies, pos, [("tall", down, depth)], mine, sibling)
        for i in range(act_sems.shape[0]):
            part(i).start()
        copies.wait()
        write.start()
        sums[...] = jnp.zeros_like(sums)

    @pl.when(step < blocks)
    def _():
        part(step).wait()
        s = pl.ds(al(step * rows, 16), rows)
        per_pair = acts.shape[0] // lengths.shape[0] // rows
        slot = lax.broadcasted_iota(jnp.int32, (rows, 1), 0) + lax.rem(step, per_pair) * rows
        mask = (slot < lengths[step // per_pair]).astype(f32)
        hidden = normed[...] * vectors[3:4, :] + vectors[4:5, :]
        second = hidden + dot(acts[s, :], down[...]) + vectors[5:6, :]
        normal, scale = layer_norm(second)
        gain = vectors[6:7, :]
        output[...] = ((normal * gain + vectors[7:8, :]) * mask).astype(bf16)
        upstream = cotangent[...].astype(f32) * mask
        result = norm_back(upstream, normal, scale, gain)
        grad_second[...] = result
        low = result.astype(bf16)
        lows[s, :] = low
        sums[0:1, :] += jnp.sum(upstream * normal, axis=0, keepdims=True)
        sums[1:2, :] += jnp.sum(upstream, axis=0, keepdims=True)
        sums[2:3, :] += jnp.sum(low.astype(f32), axis=0, keepdims=True)

    @pl.when(step == blocks)
    def _():
        chunk = 768
        for j in range(grads.shape[0] // chunk):
            s = slice(j * chunk, (j + 1) * chunk)
            grads[s, :] = tn(acts[:, s], lows[...]).astype(bf16)
        copies = Copies(out_sems)
        emit(copies, pos, [("tall", grads, depth)], send, keep)
        copies.wait()
        write.wait()


def ffn_back(pos, grad_second, slope, normed, inverse, mixed, wd, wu, wo, vectors, grad_first, grad_mixed, send, keep, sums, up_sums, expos, hiddens, lows, grad_up, grad_out, out_sems):
    step = pl.program_id(0)
    blocks = pl.num_programs(0) - 1
    rows = normed.shape[0]

    @pl.when(step == 0)
    def _():
        sums[...] = jnp.zeros_like(sums)
        up_sums[...] = jnp.zeros_like(up_sums)

    @pl.when(step < blocks)
    def _():
        s = pl.ds(al(step * rows, 16), rows)
        upper = grad_second[...]
        low = upper.astype(bf16)
        chunk = 768
        for j in range(expos.shape[1] // chunk):
            c = slice(j * chunk, (j + 1) * chunk)
            grown = (nt(low, wd[c, :]) * slope[:, c].astype(f32)).astype(bf16)
            expos[s, c] = grown
            up_sums[0:1, c] += jnp.sum(grown.astype(f32), axis=0, keepdims=True)
        normal = normed[...]
        gain = vectors[3:4, :]
        hiddens[s, :] = (normal * gain + vectors[4:5, :]).astype(bf16)
        upstream = upper + nt(expos[s, :], wu[...])
        result = norm_back(upstream, normal, inverse[:, 0:1], gain)
        grad_first[...] = result
        low = result.astype(bf16)
        lows[s, :] = low
        grad_mixed[...] = nt(low, wo[...]).astype(bf16)
        sums[0:1, :] += jnp.sum(upstream * normal, axis=0, keepdims=True)
        sums[1:2, :] += jnp.sum(upstream, axis=0, keepdims=True)
        sums[2:3, :] += jnp.sum(low.astype(f32), axis=0, keepdims=True)

    @pl.when(step == blocks)
    def _():
        chunk = 768
        for j in range(grad_up.shape[1] // chunk):
            c = slice(j * chunk, (j + 1) * chunk)
            grad_up[:, c] = tn(hiddens[...], expos[:, c]).astype(bf16)
        grad_out[...] = tn(mixed[...], lows[...]).astype(bf16)
        copies = Copies(out_sems)
        depth = grad_out.shape[0] // lax.axis_size("grp")
        emit(copies, pos, [("wide", grad_up, depth), ("0", grad_out, depth)], send, keep)
        copies.wait()


def attend_back(pos, lengths, x, q, k, v, mixed, grad_mixed, logsum, last_sums, first_sums, up_sums, grads, send, keep, held, weight_grads, deltas, sums, blocks, out_sems):
    pair = pl.program_id(0)
    pairs = pl.num_programs(0) - 1
    width = q.shape[1]
    slots = q.shape[0]

    @pl.when(pair == 0)
    def _():
        sums[...] = jnp.zeros_like(sums)

    @pl.when(pair < pairs)
    def _():
        low = lax.broadcasted_iota(jnp.int32, (slots, 128), 1) < HD
        slot = lax.broadcasted_iota(jnp.int32, (slots, 1), 0)
        bias = jnp.where(slot < lengths[pair], 0.0, MASKED).astype(f32)
        product = mixed[...].astype(f32) * grad_mixed[...].astype(f32)
        select = (
            lax.broadcasted_iota(jnp.int32, (16, width), 1) // HD
            == lax.broadcasted_iota(jnp.int32, (16, width), 0)
        ).astype(bf16)
        high = product.astype(bf16)
        rest = (product - high.astype(f32)).astype(bf16)
        deltas[...] = nt(select, high) + nt(select, rest)
        here = pl.ds(al(pair * slots, 16), slots)
        scaling = HD ** (-0.5)

        def heads(h, carry):
            s = pl.ds(al(h * 128, 128), 128)
            q1, k1, v1, g1 = q[:, s], k[:, s], v[:, s], grad_mixed[:, s]
            probs, scores_back, qs, gs, ks = [], [], [], [], []
            for e in range(2):
                mask = low if e == 0 else ~low
                qm = jnp.where(mask, q1, 0).astype(bf16)
                gm = jnp.where(mask, g1, 0).astype(bf16)
                row = pl.ds(h * 2 + e, 1)
                prob = jnp.exp(nt(k1, qm) + bias - logsum[0, row, :])
                back = prob * (nt(v1, gm) - deltas[row, :])
                probs.append(prob.astype(bf16))
                scores_back.append(back.astype(bf16))
                qs.append(qm)
                gs.append(gm)
                ks.append(jnp.where(mask, k1, 0).astype(bf16))
            grad_v = dot(jnp.concatenate(probs, 1), jnp.concatenate(gs, 0))
            grad_k = dot(jnp.concatenate(scores_back, 1), jnp.concatenate(qs, 0))
            grad_q = tn(jnp.concatenate(scores_back, 0), jnp.concatenate(ks, 0)) * scaling
            for m, value in enumerate((grad_q, grad_k, grad_v)):
                value = value.astype(bf16)
                c = pl.ds(al(m * width + h * 128, 128), 128)
                held[here, c] = value
                sums[m : m + 1, s] += jnp.sum(value.astype(f32), axis=0, keepdims=True)
            return carry

        lax.fori_loop(0, H // 2, heads, 0, unroll=2)
        grads[...] = held[here, :]

    @pl.when(pair == pairs)
    def _():
        for m in range(3):
            c = slice(m * width, (m + 1) * width)
            weight_grads[:, c] = tn(x[...], held[:, c]).astype(bf16)
        blocks[...] = jnp.zeros_like(blocks)
        half = width // 2
        rows = (
            (sums[0:1, :], sums[2:3, :]),
            (first_sums[2:3, :], first_sums[0:1, :]),
            (first_sums[1:2, :], last_sums[2:3, :]),
            (last_sums[0:1, :], last_sums[1:2, :]),
            (up_sums[0:1, :width], up_sums[0:1, width : 2 * width]),
            (up_sums[0:1, 2 * width : 3 * width], up_sums[0:1, 3 * width :]),
        )
        for p, (a, b) in enumerate(rows):
            stacked = jnp.concatenate(
                [a[:, :half], a[:, half:], b[:, :half], b[:, half:], jnp.zeros((12, half), f32)], axis=0
            )
            blocks[p] = stacked.astype(bf16)
        copies = Copies(out_sems)
        depth = weight_grads.shape[0] // lax.axis_size("grp")
        emit(copies, pos, [(str(m * width), weight_grads, depth) for m in range(3)], send, keep)
        core = pos[3]
        base = 3 * depth // 4
        for held_ref, flip in ((send, 1), (keep, 0)):
            for zone in range(send.shape[0]):
                for q_at in range(4):
                    copies.add(
                        blocks.at[q_at * 2 + (core ^ flip)], held_ref.at[zone, q_at, pl.ds(base, 16), :]
                    )
        copies.wait()


def inputs_back(grad_first, grads, weight, out):
    out[...] = (grad_first[...] + nt(grads[...], weight[...])).astype(bf16)


def place_pieces(pos, t1, c1, t2, c2, t3, c3, gq, gk, gv, go, gu, gd, small):
    p = pos[4]
    depth = gq.shape[0]
    quarter, half, eighth = depth // 4, depth // 2, gd.shape[0] // LOCAL
    for sib, (first, second, third) in ((0, (t1, t2, t3)), (1, (c1, c2, c3))):
        for other in range(4):
            owner = p ^ (other * 2) ^ sib
            row4 = al((owner // 2) * quarter, 16)
            col2 = al((owner % 2) * COLS, 128)
            n = first.shape[0] // 4
            for m, out in enumerate((gq, gk, gv)):
                block = first[pl.ds(other * n + m * quarter, quarter), :]
                out[pl.ds(row4, quarter), pl.ds(col2, COLS)] = block.astype(f32)
            block = first[pl.ds(other * n + 3 * quarter, 16), :].astype(f32)
            small[pl.ds(al(owner * 8, 8), 8), :] = block[:8]
            n = second.shape[0] // 4
            for j in range(2):
                block = second[pl.ds(other * n + j * half, half), :]
                wide = al((owner // 2) * 2 * COLS + j * COLS, 128)
                gu[pl.ds(al((owner % 2) * half, 16), half), pl.ds(wide, COLS)] = block.astype(f32)
            block = second[pl.ds(other * n + 2 * half, quarter), :]
            go[pl.ds(row4, quarter), pl.ds(col2, COLS)] = block.astype(f32)
            n = third.shape[0] // 4
            for j in range(2):
                block = third[pl.ds(other * n + j * eighth, eighth), :]
                gd[pl.ds(al(owner * eighth, 16), eighth), pl.ds(j * COLS, COLS)] = block.astype(f32)


def shards(
    tokens,
    lengths,
    cotangent,
    query_weight,
    query_bias,
    key_weight,
    value_weight,
    value_bias,
    out_weight,
    out_bias,
    norm_gain,
    norm_shift,
    up_weight,
    up_bias,
    down_weight,
    down_bias,
    final_gain,
    final_shift,
):
    groups = lax.axis_size("grp")
    pairs, seqlen, width = tokens.shape
    rows = pairs * seqlen
    depth = width // groups
    wide = up_weight.shape[1]
    inputs = tokens.reshape(rows, width)
    upstream = cotangent.reshape(rows, width)
    pos = position()
    n1 = 3 * depth // 4
    n2 = depth + depth // 4
    n3 = depth

    small = jnp.concatenate(
        [query_bias, value_bias, out_bias, norm_gain, norm_shift, down_bias, final_gain, final_shift, up_bias]
    )
    count = small.shape[0] // COLS
    small_block = jnp.pad(small.reshape(count, COLS), ((0, 16 - count), (0, 0)))
    weights = (query_weight, key_weight, value_weight, out_weight, up_weight, down_weight)
    first, second, third = call(
        cut_weights,
        (shape((n1 + 16, COLS), bf16), shape((n2, COLS), bf16), shape((n3, COLS), bf16)),
        (pos, *weights, small_block),
        [SMEM] + [ANY] * 7,
        (ANY,) * 3,
        scratch=[pltpu.SemaphoreType.DMA((9,))],
        moved=2 * (n1 + n2 + n3) * COLS * 4,
    )
    blocks = [first] + [to_grp(first, step) for step in range(1, groups)]
    mine = jnp.concatenate([block[:n1] for block in blocks[1:]], axis=0)
    held1 = spread_rest(mine)
    held2 = spread_rest(jnp.concatenate([to_grp(second, step) for step in range(1, groups)], axis=0))
    held3 = spread_rest(jnp.concatenate([to_grp(third, step) for step in range(1, groups)], axis=0))
    order = [blocks[0]] + blocks[:0:-1]
    twice = jnp.stack([block[n1 : n1 + count].reshape(-1) for block in order] * 2)
    by_zone = lax.dynamic_slice_in_dim(twice, lax.rem(groups - pos[0], groups), groups, 0)
    by_zone = by_zone.astype(f32)
    vectors = by_zone[:, : 8 * depth].reshape(groups, 8, depth).transpose(1, 0, 2).reshape(8, width)
    up_vector = by_zone[:, 8 * depth :].reshape(1, wide)

    row_block = 256
    blocks_of = rows // row_block
    mat = shape((rows, width), bf16)
    mat32 = shape((rows, width), f32)
    dense = 2 * rows * width * width
    by_pair = pl.BlockSpec((seqlen, width), lambda i: (i, 0))
    q, k, v, mixed, logsum, w_all = call(
        attend,
        (mat, mat, mat, mat, shape((pairs, 16, seqlen), f32), shape((width, 3 * width), bf16)),
        (pos, lengths, inputs, query_weight, key_weight, value_weight, *held1, vectors),
        [SMEM, SMEM, by_pair, ANY, ANY, ANY, ANY, ANY, VMEM],
        (by_pair, by_pair, by_pair, by_pair, pl.BlockSpec((1, 16, seqlen), lambda i: (i, 0, 0)), ANY),
        scratch=[
            pltpu.VMEM((width, 3 * width), bf16),
            pltpu.SemaphoreType.DMA((4 + 8 * (groups - 1) * 3,)),
        ],
        grid=(pairs,),
        flops=12 * dense,
        moved=12 * rows * width,
    )

    by_row = pl.BlockSpec((row_block, width), lambda i: (i, 0))
    by_wide = pl.BlockSpec((row_block, wide), lambda i: (i, 0))
    by_lane = pl.BlockSpec((row_block, 128), lambda i: (i, 0))
    act, slope, normed, inverse, wu_all, wo_all = call(
        expand,
        (
            shape((rows, wide), bf16),
            shape((rows, wide), bf16),
            mat32,
            shape((rows, 128), f32),
            shape((width, wide), bf16),
            shape((width, width), bf16),
        ),
        (pos, inputs, mixed, up_weight, out_weight, *held2, vectors, up_vector),
        [SMEM, by_row, by_row, ANY, ANY, ANY, ANY, VMEM, VMEM],
        (by_wide, by_wide, by_row, by_lane, ANY, ANY),
        scratch=[
            pltpu.VMEM((width, wide), bf16),
            pltpu.VMEM((width, width), bf16),
            pltpu.SemaphoreType.DMA((4 + 8 * (groups - 1) * 3,)),
        ],
        grid=(blocks_of,),
        flops=8 * dense,
        moved=18 * rows * width,
    )

    stay = lambda i: (jnp.minimum(i, blocks_of - 1), 0)
    by_row = pl.BlockSpec((row_block, width), stay)
    by_wide = pl.BlockSpec((row_block, wide), stay)
    by_lane = pl.BlockSpec((row_block, 128), stay)
    vec_out = pl.BlockSpec((8, width), lambda i: (0, 0))
    output, grad_second, send3, keep3, last_sums, wd_all = call(
        contract,
        (
            mat,
            mat32,
            shape((groups, 4, n3, COLS), bf16),
            shape((groups, 4, n3, COLS), bf16),
            shape((8, width), f32),
            shape((wide, width), bf16),
        ),
        (lengths, act, normed, upstream, down_weight, *held3, pos, vectors),
        [SMEM, ANY, by_row, by_row, ANY, ANY, ANY, SMEM, VMEM],
        (by_row, by_row, ANY, ANY, vec_out, ANY),
        scratch=[
            pltpu.VMEM((wide, width), bf16),
            pltpu.VMEM((rows, wide), bf16),
            pltpu.VMEM((rows, width), bf16),
            pltpu.VMEM((wide, width), bf16),
            pltpu.SemaphoreType.DMA((2 + 8 * (groups - 1) * 2,)),
            pltpu.SemaphoreType.DMA((blocks_of,)),
            pltpu.SemaphoreType.DMA((groups * 4 * 2 * 2,)),
        ],
        grid=(blocks_of + 1,),
        flops=8 * dense,
        moved=16 * rows * width,
    )
    total3 = reduce_group(pos, send3, keep3)

    whole = lambda dims: pl.BlockSpec(dims, lambda i: (0,) * len(dims))
    grad_first, grad_mixed, send2, keep2, first_sums, up_sums = call(
        ffn_back,
        (
            mat32,
            mat,
            shape((groups, 4, n2, COLS), bf16),
            shape((groups, 4, n2, COLS), bf16),
            shape((8, width), f32),
            shape((8, wide), f32),
        ),
        (pos, grad_second, slope, normed, inverse, mixed, wd_all, wu_all, wo_all, vectors),
        [SMEM, by_row, by_wide, by_row, by_lane, VMEM, VMEM, VMEM, VMEM, VMEM],
        (by_row, by_row, ANY, ANY, vec_out, whole((8, wide))),
        scratch=[
            pltpu.VMEM((rows, wide), bf16),
            pltpu.VMEM((rows, width), bf16),
            pltpu.VMEM((rows, width), bf16),
            pltpu.VMEM((width, wide), bf16),
            pltpu.VMEM((width, width), bf16),
            pltpu.SemaphoreType.DMA((groups * 4 * 2 * 3,)),
        ],
        grid=(blocks_of + 1,),
        flops=14 * dense,
        moved=30 * rows * width,
    )
    total2 = reduce_group(pos, send2, keep2)

    stay_pair = lambda i: (jnp.minimum(i, pairs - 1), 0)
    by_pair = pl.BlockSpec((seqlen, width), stay_pair)
    grads, send1, keep1 = call(
        attend_back,
        (
            shape((rows, 3 * width), bf16),
            shape((groups, 4, n1 + 16, COLS), bf16),
            shape((groups, 4, n1 + 16, COLS), bf16),
        ),
        (pos, lengths, inputs, q, k, v, mixed, grad_mixed, logsum, last_sums, first_sums, up_sums),
        [SMEM, SMEM, VMEM]
        + [by_pair] * 5
        + [pl.BlockSpec((1, 16, seqlen), lambda i: (jnp.minimum(i, pairs - 1), 0, 0)), VMEM, VMEM, VMEM],
        (pl.BlockSpec((seqlen, 3 * width), stay_pair), ANY, ANY),
        scratch=[
            pltpu.VMEM((rows, 3 * width), bf16),
            pltpu.VMEM((width, 3 * width), bf16),
            pltpu.VMEM((16, seqlen), f32),
            pltpu.VMEM((8, width), f32),
            pltpu.VMEM((LOCAL, 16, COLS), bf16),
            pltpu.SemaphoreType.DMA((groups * 4 * 2 * 4,)),
        ],
        grid=(pairs + 1,),
        flops=24 * dense,
        moved=24 * rows * width,
    )
    total1 = reduce_group(pos, send1, keep1)
    by_row = pl.BlockSpec((row_block, width), lambda i: (i, 0))
    grad_inputs = call(
        inputs_back,
        mat,
        (grad_first, grads, w_all),
        [by_row, pl.BlockSpec((row_block, 3 * width), lambda i: (i, 0)), VMEM],
        by_row,
        grid=(blocks_of,),
        flops=3 * dense,
        moved=16 * rows * width,
    )
    square = shape((depth, width), f32)
    gq, gk, gv, go, gu, gd, rest = call(
        place_pieces,
        (
            square,
            square,
            square,
            square,
            shape((depth, wide), f32),
            shape((wide // groups, width), f32),
            shape((LOCAL * 8, COLS), f32),
        ),
        (pos, *share_group(total1), *share_group(total2), *share_group(total3)),
        [SMEM] + [VMEM] * 6,
        (VMEM,) * 7,
        moved=24 * depth * width,
    )
    rest = rest.reshape(LOCAL, 8, COLS)[:, :4].reshape(LOCAL * 2, width)

    def part(i):
        return lax.dynamic_slice_in_dim(rest[i], pos[0] * depth, depth, 0)

    bq, bv, bo, g1, s1, bd, g2, s2 = (part(i) for i in range(8))
    bu = lax.dynamic_slice_in_dim(rest[8:12].reshape(-1), pos[0] * width, width, 0)
    return (
        output.reshape(pairs, seqlen, width),
        grad_inputs.reshape(pairs, seqlen, width),
        gq,
        bq,
        gk,
        gv,
        bv,
        go,
        bo,
        g1,
        s1,
        gu,
        bu,
        gd,
        bd,
        g2,
        s2,
    )


def spread_rest(mine):
    cut = (mine.shape[0] // 2 + 47) // 48 * 48
    from_x = to_rep(mine, 2)
    from_y = to_rep(mine, 4)
    corner_low = to_rep(from_x[:cut], 4)
    corner_high = to_rep(from_y[cut:], 2)
    held = jnp.concatenate([mine, from_x, from_y, corner_low, corner_high], axis=0)
    return held, to_rep(held, 1)


def solution(mesh):
    pairs = P(("grp", "rep"), None, None)
    matrix = P("grp", None)
    vector = P("grp")
    placed = (pairs, P(("grp", "rep")), pairs, matrix, vector, matrix, matrix, vector, matrix, vector)
    placed += (vector, vector, matrix, vector, matrix, vector, vector, vector)
    results = (pairs, pairs, matrix, vector, matrix, matrix, vector, matrix, vector, vector, vector)
    results += (matrix, vector, matrix, vector, vector, vector)
    return jax.shard_map(shards, mesh=mesh, in_specs=placed, out_specs=results, check_vma=False)
```

```python
import functools

import jax
import jax.numpy as jnp
from jax import lax
from jax.experimental import pallas as pl
from jax.experimental.pallas import tpu as pltpu
from jax.sharding import PartitionSpec as P

H = 12
HD = 64
EPSILON = 1e-06
MASKED = -1e30
DENSITY = 0.3989422804014327
ROOT_HALF = 0.7071067811865476

f32 = jnp.float32
bf16 = jnp.bfloat16
VMEM = pl.BlockSpec(memory_space=pltpu.VMEM)
SMEM = pl.BlockSpec(memory_space=pltpu.SMEM)
ANY = pl.BlockSpec(memory_space=pl.ANY)
VMEM_LIMIT = 56 * 2**20
COLS = 384
WEIGHT = 20
LOCAL = 8


def dot(a, b):
    return jnp.dot(a, b, preferred_element_type=f32)


def nt(a, b):
    return lax.dot_general(a, b, (((1,), (1,)), ((), ())), preferred_element_type=f32)


def tn(a, b):
    return lax.dot_general(a, b, (((0,), (0,)), ((), ())), preferred_element_type=f32)


def shape(dims, dtype):
    return jax.ShapeDtypeStruct(dims, dtype)


def al(value, by):
    return pl.multiple_of(value, by)


def call(kernel, outs, args, specs, out_specs, scratch=(), grid=(), flops=0, moved=0, aliases=None, **fixed):
    return pl.pallas_call(
        functools.partial(kernel, **fixed) if fixed else kernel,
        grid=grid,
        out_shape=outs,
        in_specs=specs,
        out_specs=out_specs,
        scratch_shapes=scratch,
        input_output_aliases=aliases or {},
        compiler_params=pltpu.CompilerParams(vmem_limit_bytes=VMEM_LIMIT),
        cost_estimate=pl.CostEstimate(
            flops=WEIGHT * flops, bytes_accessed=WEIGHT * moved, transcendentals=0
        ),
        name=kernel.__name__,
    )(*args)


def after(values, *events):
    return lax.optimization_barrier((values, events))[0]


def to_rep(array, bit):
    size = lax.axis_size("rep")
    return lax.ppermute(array, "rep", [(i, i ^ bit) for i in range(size)])


def to_grp(array, bit):
    size = lax.axis_size("grp")
    return lax.ppermute(array, "grp", [(i, i ^ bit) for i in range(size)])


def position():
    z = lax.axis_index("grp").astype(jnp.int32)
    p = lax.axis_index("rep").astype(jnp.int32) % LOCAL
    return jnp.stack([z, (p // 2) % 2, p // 4, p % 2, p])


class Copies:
    def __init__(self, sems):
        self.sems, self.held = sems, []

    def add(self, src, dst):
        copy = pltpu.make_async_copy(src, dst, self.sems.at[len(self.held)])
        copy.start()
        self.held.append(copy)

    def wait(self):
        for copy in self.held:
            copy.wait()


def piece_refs(kind, ref, zone, p, depth):
    if kind == "tall":
        rows = depth // LOCAL
        start = al(zone * depth + p * rows, 16)
        return [
            (ref.at[pl.ds(start, rows), pl.ds(half * COLS, COLS)], rows) for half in range(2)
        ]
    if kind == "wide":
        rows = depth // 2
        start = al(zone * depth + (p % 2) * rows, 16)
        return [
            (
                ref.at[pl.ds(start, rows), pl.ds(al((p // 2) * 2 * COLS + half * COLS, 128), COLS)],
                rows,
            )
            for half in range(2)
        ]
    if kind == "half":
        rows = depth // 2
        start = al(zone * depth + (p % 2) * rows, 16)
        return [(ref.at[pl.ds(start, rows), pl.ds(al((p // 2) * COLS, 128), COLS)], rows)]
    rows = depth // 4
    offset = int(kind)
    start = al(zone * depth + (p // 2) * rows, 16)
    return [(ref.at[pl.ds(start, rows), pl.ds(al(offset + (p % 2) * COLS, 128), COLS)], rows)]


def own_slab(ref, zone, depth, first=0, width=None):
    width = ref.shape[1] if width is None else width
    return ref.at[pl.ds(al(zone * depth, 16), depth), pl.ds(first, width)]


def block_rows(parts):
    return sum(rows for kind, ref, depth in parts for _, rows in piece_refs(kind, ref, 0, 0, depth))


def fetch(copies, pos, parts, held):
    zone, p = pos[0], pos[4]
    groups = lax.axis_size("grp")
    n = held[0].shape[0] // (groups - 1)
    side = len(held) // 2
    for sib in range(2):
        for other in range(4):
            owner = p ^ (other * 2) ^ sib
            part = held[side * sib + other]
            cut = part.shape[0]
            for step in range(1, groups):
                source = zone ^ step
                at = (step - 1) * n
                for kind, ref, depth in parts:
                    for place, rows in piece_refs(kind, ref, source, owner, depth):
                        first = max(0, min(cut - at, rows))
                        if first:
                            copies.add(part.at[pl.ds(at, first), :], place.at[pl.ds(0, first), :])
                        if first < rows:
                            copies.add(
                                held[side * sib + 4].at[pl.ds(at + first - cut, rows - first), :],
                                place.at[pl.ds(first, rows - first), :],
                            )
                        at += rows


def emit(copies, pos, parts, send, keep, quads=range(4)):
    core = pos[3]
    groups = lax.axis_size("grp")
    for held, flip in ((send, 1), (keep, 0)):
        for zone in range(groups):
            for q in quads:
                owner = q * 2 + (core ^ flip)
                at = 0
                for kind, ref, depth in parts:
                    for place, rows in piece_refs(kind, ref, zone, owner, depth):
                        copies.add(place, held.at[zone, q, pl.ds(at, rows), :])
                        at += rows


def add_first(pos, keep, got, sa, ka, sb, kb):
    x, y = pos[1], pos[2]
    half = keep.shape[0] // 2
    for zone in range(half):
        for j in range(2):
            for ref, q in ((sa, j * 2 + (1 - x)), (ka, j * 2 + x)):
                ref[zone, j] = keep[zone, q] + got[zone, q]
            for ref, q in ((sb, (1 - y) * 2 + j), (kb, y * 2 + j)):
                ref[zone, j] = keep[half + zone, q] + got[half + zone, q]


def add_second(pos, ka, ra, kb, rb, sa, ja, sb, jb):
    x, y = pos[1], pos[2]
    for zone in range(ka.shape[0]):
        for kept, got, send, hold, at in ((ka, ra, sa, ja, y), (kb, rb, sb, jb, x)):
            send[zone] = kept[zone, 1 - at] + got[zone, 1 - at]
            hold[zone] = kept[zone, at] + got[zone, at]


def add_third(pos, ka, ra, kb, rb, *rest):
    outs, total = rest[:-1], rest[-1]
    half = ka.shape[0]
    for zone in range(half):
        total[zone] = ka[zone] + ra[zone]
        total[half + zone] = kb[zone] + rb[zone]
    for step, out in enumerate(outs):
        out[...] = total[pos[0] ^ step]


def add_direct(pos, keep, got, *outs):
    q = pos[2] * 2 + pos[1]
    for zone in range(keep.shape[0]):
        for i, out in enumerate(outs):
            out[zone] = keep[zone, q ^ i] + got[zone, q ^ i]


def add_third_with(pos, ka, ra, kb, rb, mine, a, b, c, *rest):
    outs, total = rest[:-1], rest[-1]
    half, n = ka.shape[:2]
    for zone in range(half):
        total[zone, :n] = ka[zone] + ra[zone]
        total[half + zone, :n] = kb[zone] + rb[zone]
    for zone in range(2 * half):
        sums = mine[zone].astype(f32) + a[zone].astype(f32)
        total[zone, n:] = (sums + (b[zone].astype(f32) + c[zone].astype(f32))).astype(bf16)
    for step, out in enumerate(outs):
        out[...] = total[pos[0] ^ step]


def add_zones(ka, ra, kb, rb, other, out):
    half, n = ka.shape[0], other.shape[1]
    out[:, :n] = other[...]
    out[:half, n:] = ka[...] + ra[...]
    out[half:, n:] = kb[...] + rb[...]


def add_fourth(*refs):
    total = refs[0][...].astype(f32)
    for ref in refs[1:-1]:
        total = total + ref[...].astype(f32)
    refs[-1][...] = total.astype(bf16)


def over_blocks(total):
    bit = LOCAL
    while bit < lax.axis_size("rep"):
        other = to_rep(total, bit)
        total = call(add_fourth, shape(total.shape, bf16), (total, other), [VMEM] * 2, VMEM)
        bit *= 2
    return total


class Reduce:
    def __init__(self, pos, send, keep):
        self.pos, self.keep = pos, keep
        self.n = keep.shape[2]
        self.size = keep.shape[0] * 4 * self.n * COLS * 2
        self.got = to_rep(send, 1)

    def one(self, *events):
        groups = self.keep.shape[0]
        quad = shape((groups // 2, 2, self.n, COLS), bf16)
        got = after(self.got, *events)
        sa, self.ka, sb, self.kb = call(
            add_first,
            (quad,) * 4,
            (self.pos, self.keep, got),
            [SMEM, VMEM, VMEM],
            (VMEM,) * 4,
            moved=3 * self.size,
        )
        self.ra, self.rb = to_rep(sa, 2), to_rep(sb, 4)
        return self.ka

    def two(self, *events):
        pair = shape((self.ka.shape[0], self.n, COLS), bf16)
        ra, rb = after((self.ra, self.rb), *events)
        sa, self.ja, sb, self.jb = call(
            add_second,
            (pair,) * 4,
            (self.pos, self.ka, ra, self.kb, rb),
            [SMEM] + [VMEM] * 4,
            (VMEM,) * 4,
            moved=3 * self.size // 2,
        )
        self.ra, self.rb = to_rep(sa, 4), to_rep(sb, 2)
        return self.ja

    def zones(self, other, *events):
        ra, rb = after((self.ra, self.rb), *events)
        groups, n, _ = other.shape
        return call(
            add_zones,
            shape((groups, n + self.n, COLS), bf16),
            (self.ja, ra, self.jb, rb, other),
            [VMEM] * 5,
            VMEM,
            moved=3 * self.size // 4,
        )

    def three(self, *events):
        groups = self.keep.shape[0]
        ra, rb = after((self.ra, self.rb), *events)
        self.blocks = call(
            add_third,
            (shape((self.n, COLS), bf16),) * groups,
            (self.pos, self.ja, ra, self.jb, rb),
            [SMEM] + [VMEM] * 4,
            (VMEM,) * groups,
            scratch=[pltpu.VMEM((groups, self.n, COLS), bf16)],
            moved=3 * self.size // 4,
        )
        self.arrived = [to_grp(self.blocks[step], step) for step in range(1, groups)]
        return self.blocks[0]

    def direct(self, *events):
        groups = self.keep.shape[0]
        got = after(self.got, *events)
        self.mine, *sends = call(
            add_direct,
            (shape((groups, self.n, COLS), bf16),) * 4,
            (self.pos, self.keep, got),
            [SMEM, VMEM, VMEM],
            (VMEM,) * 4,
            moved=3 * self.size,
        )
        self.near = [to_rep(send, 2 * (i + 1)) for i, send in enumerate(sends)]
        return self.mine

    def three_with(self, small, *events):
        groups = self.keep.shape[0]
        ra, rb, near = after((self.ra, self.rb, small.near), *events)
        self.n += small.n
        self.blocks = call(
            add_third_with,
            (shape((self.n, COLS), bf16),) * groups,
            (self.pos, self.ja, ra, self.jb, rb, small.mine, *near),
            [SMEM] + [VMEM] * 8,
            (VMEM,) * groups,
            scratch=[pltpu.VMEM((groups, self.n, COLS), bf16)],
            moved=self.size,
        )
        self.arrived = [to_grp(self.blocks[step], step) for step in range(1, groups)]
        return self.blocks[0]

    def four(self, *events):
        arrived = after(self.arrived, *events)
        one = shape((self.n, COLS), bf16)
        total = call(
            add_fourth,
            one,
            (self.blocks[0], *arrived),
            [VMEM] * (1 + len(arrived)),
            VMEM,
            moved=self.size // 3,
        )
        self.total = over_blocks(total)
        return self.total

    def around(self):
        self.near = [to_rep(self.total, bit) for bit in (2, 4, 6)]

    def five(self, *events):
        near = after(self.near, *events)
        held = jnp.concatenate([self.total, *near], axis=0)
        self.both = held, to_rep(held, 1)
        return held


def cut_first(pos, wq, wk, wv, first):
    quarter = wq.shape[0]
    for m, ref in enumerate((wq, wk, wv)):
        first[m * quarter : (m + 1) * quarter, :] = ref[...]


def cut_more(pos, wo, wu, wd, small, second, third):
    half, quarter = wu.shape[0], wo.shape[0]
    for j in range(2):
        second[j * half : (j + 1) * half, :] = wu[:, j * COLS : (j + 1) * COLS]
        third[j * half : (j + 1) * half, :] = wd[:, j * COLS : (j + 1) * COLS]
    second[2 * half : 2 * half + quarter, :] = wo[...]
    second[2 * half + quarter :, :] = small[...]


def layer_norm(values):
    centred = values - jnp.mean(values, axis=-1, keepdims=True)
    spread_of = jnp.mean(centred * centred, axis=-1, keepdims=True)
    inverse = lax.rsqrt(spread_of + EPSILON)
    return centred * inverse, inverse


def norm_back(upstream, normed, inverse, gain):
    scaled = upstream * gain
    return inverse * (
        scaled
        - jnp.mean(scaled, axis=-1, keepdims=True)
        - normed * jnp.mean(scaled * normed, axis=-1, keepdims=True)
    )


def attend_heads(lengths, x, vectors, weight, q_out, k_out, v_out, mixed, logsum, pair):
    width = x.shape[1]
    rows = x[...]
    scaling = HD ** (-0.5)
    q_out[...] = (
        (dot(rows, weight[:, :width]) + vectors[0:1, :]).astype(bf16).astype(f32) * scaling
    ).astype(bf16)
    k_out[...] = dot(rows, weight[:, width : 2 * width]).astype(bf16)
    v_out[...] = (dot(rows, weight[:, 2 * width :]) + vectors[1:2, :]).astype(bf16)
    slots = rows.shape[0]
    lane = lax.broadcasted_iota(jnp.int32, (slots, 128), 1)
    low = lane < HD
    slot = lax.broadcasted_iota(jnp.int32, (1, slots), 1)
    bias = jnp.where(slot < lengths[pair], 0.0, MASKED).astype(f32)

    def heads(h, sums):
        s = pl.ds(al(h * 128, 128), 128)
        q1, k1, v1 = q_out[:, s], k_out[:, s], v_out[:, s]
        results, peaks = [], []
        for e in range(2):
            mask = low if e == 0 else ~low
            scores = nt(jnp.where(mask, q1, 0).astype(bf16), k1) + bias
            peak = jnp.max(scores, axis=1, keepdims=True)
            expo = jnp.exp(scores - peak).astype(bf16)
            results.append(dot(expo, jnp.where(mask, v1, 1).astype(bf16)))
            peaks.append(peak)
        total = pltpu.roll(jnp.where(low, results[1], results[0]), HD, 1)
        mixed[:, s] = (jnp.where(low, results[0], results[1]) / total).astype(bf16)
        sums = jnp.where(lane % HD == h, jnp.where(low, peaks[0], peaks[1]) + jnp.log(total), sums)
        return sums

    sums = lax.fori_loop(0, H // 2, heads, jnp.zeros((slots, 128), f32), unroll=True)
    turned = sums.T
    logsum[0, :8] = turned[:8]
    logsum[0, 8:] = turned[HD : HD + 8]


def attend(pos, lengths, x, wq, wk, wv, vectors, *rest):
    held, (q_out, k_out, v_out, mixed, logsum, w_out, weight, sems) = rest[:10], rest[10:]
    depth, width = wq.shape
    pair = pl.program_id(0)
    write = pltpu.make_async_copy(weight, w_out, sems.at[sems.shape[0] - 1])

    @pl.when(pair == 0)
    def _():
        copies = Copies(sems)
        for m, ref in enumerate((wq, wk, wv)):
            copies.add(ref, own_slab(weight, pos[0], depth, m * width, width))
        fetch(copies, pos, [(str(m * width), weight, depth) for m in range(3)], held)
        copies.wait()
        write.start()

    attend_heads(lengths, x, vectors, weight, q_out, k_out, v_out, mixed, logsum, pair)

    @pl.when(pair == pl.num_programs(0) - 1)
    def _():
        write.wait()


def expand_rows(x, mixed, vectors, up_bias, up, out_w, act, slope, normed, inverse):
    first = x[...].astype(f32) + dot(mixed[...], out_w[...]) + vectors[2:3, :]
    normal, scale = layer_norm(first)
    normed[...] = normal
    inverse[...] = jnp.broadcast_to(scale, inverse.shape)
    hidden = (normal * vectors[3:4, :] + vectors[4:5, :]).astype(bf16)
    chunk = 768
    for j in range(up.shape[1] // chunk):
        s = slice(j * chunk, (j + 1) * chunk)
        u = dot(hidden, up[:, s]) + up_bias[:, s]
        cdf, pdf = gaussian(u)
        act[:, s] = (u * cdf).astype(bf16)
        slope[:, s] = (cdf + u * pdf).astype(bf16)


def expand(pos, x, mixed, wu, wo, vectors, up_bias, *rest):
    held, (act, slope, normed, inverse, wu_out, wo_out, up, out_w, sems) = rest[:8], rest[8:]
    step = pl.program_id(0)
    depth = wo.shape[0]
    last = sems.shape[0]
    writes = [
        pltpu.make_async_copy(up, wu_out, sems.at[last - 1]),
        pltpu.make_async_copy(out_w, wo_out, sems.at[last - 2]),
    ]

    @pl.when(step == 0)
    def _():
        copies = Copies(sems)
        copies.add(wu, own_slab(up, pos[0], depth))
        copies.add(wo, own_slab(out_w, pos[0], depth))
        fetch(copies, pos, [("wide", up, depth), ("0", out_w, depth)], held)
        copies.wait()
        for write in writes:
            write.start()

    expand_rows(x, mixed, vectors, up_bias, up, out_w, act, slope, normed, inverse)

    @pl.when(step == pl.num_programs(0) - 1)
    def _():
        for write in writes:
            write.wait()


def gaussian(u):
    return 0.5 + 0.5 * lax.erf(u * ROOT_HALF), jnp.exp(-0.5 * u * u) * DENSITY


def contract(pos, lengths, act, normed, cotangent, wd, vectors, *rest):
    held, rest = rest[:8], rest[8:]
    output, grad_second, send, sums, wd_out, down, acts, lows, grads, sems, act_sems, out_sems = rest
    step = pl.program_id(0)
    blocks = pl.num_programs(0) - 1
    depth = wd.shape[0]
    rows = normed.shape[0]
    write = pltpu.make_async_copy(down, wd_out, sems.at[sems.shape[0] - 1])

    def part(i):
        return pltpu.make_async_copy(
            act.at[pl.ds(al(i * rows, 16), rows), :],
            acts.at[pl.ds(al(i * rows, 16), rows), :],
            act_sems.at[i],
        )

    @pl.when(step == 0)
    def _():
        copies = Copies(sems)
        copies.add(wd, own_slab(down, pos[0], depth))
        fetch(copies, pos, [("tall", down, depth)], held)
        for i in range(act_sems.shape[0]):
            part(i).start()
        copies.wait()
        write.start()
        sums[...] = jnp.zeros_like(sums)

    @pl.when(step < blocks)
    def _():
        part(step).wait()
        s = pl.ds(al(step * rows, 16), rows)
        per_pair = acts.shape[0] // lengths.shape[0] // rows
        slot = lax.broadcasted_iota(jnp.int32, (rows, 1), 0) + lax.rem(step, per_pair) * rows
        mask = (slot < lengths[step // per_pair]).astype(f32)
        hidden = normed[...] * vectors[3:4, :] + vectors[4:5, :]
        second = hidden + dot(acts[s, :], down[...]) + vectors[5:6, :]
        normal, scale = layer_norm(second)
        gain = vectors[6:7, :]
        output[...] = ((normal * gain + vectors[7:8, :]) * mask).astype(bf16)
        upstream = cotangent[...].astype(f32) * mask
        result = norm_back(upstream, normal, scale, gain)
        grad_second[...] = result
        low = result.astype(bf16)
        lows[s, :] = low
        sums[0:1, :] += jnp.sum(upstream * normal, axis=0, keepdims=True)
        sums[1:2, :] += jnp.sum(upstream, axis=0, keepdims=True)
        sums[2:3, :] += jnp.sum(low.astype(f32), axis=0, keepdims=True)

    @pl.when(step == blocks)
    def _():
        copies = Copies(out_sems)
        for zone in range(grads.shape[0] // depth):
            s = slice(zone * depth, (zone + 1) * depth)
            grads[s, :] = tn(acts[:, s], lows[...]).astype(bf16)
            for p in range(LOCAL):
                at = 0
                for place, rows in piece_refs("tall", grads, zone, p, depth):
                    copies.add(place, send.at[p, zone, pl.ds(at, rows), :])
                    at += rows
        copies.wait()
        write.wait()


def vector_blocks(blocks, rows):
    blocks[...] = jnp.zeros_like(blocks)
    for p, row in enumerate(rows):
        half = row.shape[1] // 2
        stacked = jnp.concatenate([row[:, :half], row[:, half:], jnp.zeros((14, half), f32)], axis=0)
        blocks[p] = stacked.astype(bf16)


def emit_vectors(copies, pos, blocks, base, send, keep):
    for held, flip in ((send, 1), (keep, 0)):
        for zone in range(send.shape[0]):
            for q in range(4):
                owner = q * 2 + (pos[3] ^ flip)
                copies.add(blocks.at[owner], held.at[zone, q, pl.ds(base, 16), :])


def up_back(pos, grad_second, slope, normed, wd, vectors, last_sums, expo_out, send, keep, expos, hiddens, grad_up, up_sums, blocks, out_sems):
    step = pl.program_id(0)
    steps = pl.num_programs(0) - 1
    rows = normed.shape[0]
    width = normed.shape[1]

    @pl.when(step == 0)
    def _():
        up_sums[...] = jnp.zeros_like(up_sums)

    @pl.when(step < steps)
    def _():
        s = pl.ds(al(step * rows, 16), rows)
        low = grad_second[...].astype(bf16)
        chunk = 768
        for j in range(expos.shape[1] // chunk):
            c = slice(j * chunk, (j + 1) * chunk)
            grown = (nt(low, wd[c, :]) * slope[:, c].astype(f32)).astype(bf16)
            expos[s, c] = grown
            expo_out[:, c] = grown
            up_sums[0:1, c] += jnp.sum(grown.astype(f32), axis=0, keepdims=True)
        hiddens[s, :] = (normed[...] * vectors[3:4, :] + vectors[4:5, :]).astype(bf16)

    @pl.when(step == steps)
    def _():
        copies = Copies(out_sems)
        depth = grad_up.shape[0] // lax.axis_size("grp")
        chunk = 2 * COLS
        for j in range(grad_up.shape[1] // chunk):
            c = slice(j * chunk, (j + 1) * chunk)
            grad_up[:, c] = tn(hiddens[...], expos[:, c]).astype(bf16)
            emit(copies, pos, [("wide", grad_up, depth)], send, keep, (j,))
        rows_of = [last_sums[i : i + 1, :] for i in range(3)]
        rows_of += [up_sums[0:1, j * width : (j + 1) * width] for j in range(4)]
        vector_blocks(blocks, rows_of)
        emit_vectors(copies, pos, blocks, depth, send, keep)
        copies.wait()


def hidden_back(grad_second, expos, normed, inverse, mixed, wu, wo, vectors, grad_first, grad_mixed, sums, grad_out, lows):
    step = pl.program_id(0)
    steps = pl.num_programs(0) - 1
    rows = normed.shape[0]

    @pl.when(step == 0)
    def _():
        sums[...] = jnp.zeros_like(sums)

    @pl.when(step < steps)
    def _():
        s = pl.ds(al(step * rows, 16), rows)
        normal = normed[...]
        upstream = grad_second[...] + nt(expos[...], wu[...])
        result = norm_back(upstream, normal, inverse[:, 0:1], vectors[3:4, :])
        grad_first[...] = result
        low = result.astype(bf16)
        lows[s, :] = low
        grad_mixed[...] = nt(low, wo[...]).astype(bf16)
        sums[0:1, :] += jnp.sum(upstream * normal, axis=0, keepdims=True)
        sums[1:2, :] += jnp.sum(upstream, axis=0, keepdims=True)
        sums[2:3, :] += jnp.sum(low.astype(f32), axis=0, keepdims=True)

    @pl.when(step == steps)
    def _():
        grad_out[...] = tn(mixed[...], lows[...]).astype(bf16)


def heads_back(lengths, q, k, v, mixed, grad_mixed, logsum, held, deltas, sums, pair, first, count, width):
    slots = q.shape[0]
    span = q.shape[1]
    low = lax.broadcasted_iota(jnp.int32, (slots, 128), 1) < HD
    slot = lax.broadcasted_iota(jnp.int32, (slots, 1), 0)
    bias = jnp.where(slot < lengths[pair], 0.0, MASKED).astype(f32)
    product = mixed[...].astype(f32) * grad_mixed[...].astype(f32)
    select = (
        lax.broadcasted_iota(jnp.int32, (16, span), 1) // HD
        == lax.broadcasted_iota(jnp.int32, (16, span), 0)
    ).astype(bf16)
    high = product.astype(bf16)
    rest = (product - high.astype(f32)).astype(bf16)
    deltas[...] = nt(select, high) + nt(select, rest)
    here = pl.ds(al(pair * slots, 16), slots)
    scaling = HD ** (-0.5)

    def heads(h, carry):
        s = pl.ds(al(h * 128, 128), 128)
        q1, k1, v1, g1 = q[:, s], k[:, s], v[:, s], grad_mixed[:, s]
        probs, scores_back, qs, gs, ks = [], [], [], [], []
        for e in range(2):
            mask = low if e == 0 else ~low
            qm = jnp.where(mask, q1, 0).astype(bf16)
            gm = jnp.where(mask, g1, 0).astype(bf16)
            prob = jnp.exp(nt(k1, qm) + bias - logsum[0, pl.ds(first + h + 8 * e, 1), :])
            back = prob * (nt(v1, gm) - deltas[pl.ds(h * 2 + e, 1), :])
            probs.append(prob.astype(bf16))
            scores_back.append(back.astype(bf16))
            qs.append(qm)
            gs.append(gm)
            ks.append(jnp.where(mask, k1, 0).astype(bf16))
        grad_v = dot(jnp.concatenate(probs, 1), jnp.concatenate(gs, 0))
        grad_k = dot(jnp.concatenate(scores_back, 1), jnp.concatenate(qs, 0))
        grad_q = tn(jnp.concatenate(scores_back, 0), jnp.concatenate(ks, 0)) * scaling
        for m, value in enumerate((grad_q, grad_k, grad_v)):
            value = value.astype(bf16)
            held[here, pl.ds(al(m * span + h * 128, 128), 128)] = value
            if m != 1:
                sums[m : m + 1, pl.ds(al((first + h) * 128, 128), 128)] += jnp.sum(
                    value.astype(f32), axis=0, keepdims=True
                )
        return carry

    lax.fori_loop(0, count, heads, 0, unroll=True)


def attend_back(pos, lengths, x, q, k, v, mixed, grad_mixed, logsum, *rest, first, count):
    pair = pl.program_id(0)
    pairs = pl.num_programs(0) - 1
    if first == 0:
        grad_out, first_sums = rest[:2]
        grads, send, keep, sums, held, weight_grads, deltas, blocks, out_sems = rest[2:]
    else:
        old_sums = rest[0]
        grads, send, keep, held, weight_grads, deltas, sums, blocks, out_sems = rest[1:]

    @pl.when(pair == 0)
    def _():
        sums[...] = jnp.zeros_like(sums)

    @pl.when(pair < pairs)
    def _():
        heads_back(
            lengths, q, k, v, mixed, grad_mixed, logsum, held, deltas, sums, pair, first, count, x.shape[1]
        )
        slots = q.shape[0]
        grads[...] = held[pl.ds(al(pair * slots, 16), slots), :]

    @pl.when(pair == pairs)
    def _():
        span = q.shape[1]
        for m in range(3):
            c = slice(m * span, (m + 1) * span)
            weight_grads[:, c] = tn(x[...], held[:, c]).astype(bf16)
        copies = Copies(out_sems)
        depth = weight_grads.shape[0] // lax.axis_size("grp")
        if first == 0:
            parts = [("half", weight_grads, depth), ("0", grad_out, depth)]
            vectors = [first_sums[i : i + 1, :] for i in range(3)]
        else:
            parts = [("0", weight_grads, depth)]
            vectors = [sums[m : m + 1, :] + old_sums[m : m + 1, :] for m in (0, 2)]
        vector_blocks(blocks, vectors)
        emit(copies, pos, parts, send, keep)
        emit_vectors(copies, pos, blocks, block_rows(parts), send, keep)
        copies.wait()


def inputs_back(sofar, grads, weight, out, first):
    width = out.shape[1]
    total = sofar[...]
    span = grads.shape[1] // 3
    for m in range(3):
        c = slice(m * width + first, m * width + first + span)
        total = total + nt(grads[:, m * span : (m + 1) * span], weight[:, c])
    out[...] = total.astype(out.dtype)


def place_ffn(pos, shared, gd, gu, g2, s2, bd, bu):
    tall, half = gd.shape[0] // LOCAL, gu.shape[0] // 2
    n = shared.shape[0] // LOCAL
    for p in range(LOCAL):
        for j in range(2):
            at = p * n + j * tall
            gd[p * tall : (p + 1) * tall, j * COLS : (j + 1) * COLS] = shared[at : at + tall, :].astype(f32)
            at = p * n + 2 * tall + j * half
            first = (p // 2) * 2 * COLS + j * COLS
            rows = slice((p % 2) * half, (p % 2 + 1) * half)
            gu[rows, first : first + COLS] = shared[at : at + half, :].astype(f32)

    def vector(p):
        at = p * n + 2 * tall + 2 * half
        block = shared[at : at + 16, :].astype(f32)
        return jnp.concatenate([block[0:1, :], block[1:2, :]], axis=1)

    for p, out in enumerate((g2, s2, bd)):
        out[...] = own_part(pos, vector(p), out.shape[1])
    total = jnp.zeros(bu.shape, f32)
    for zone in range(4):
        total = jnp.where(pos[0] == zone, vector(3 + zone), total)
    bu[...] = total


def own_part(pos, row, size):
    total = row[:, :size]
    for zone in range(1, row.shape[1] // size):
        total = jnp.where(pos[0] == zone, row[:, zone * size : (zone + 1) * size], total)
    return total


def place_heads(pos, mine, sibling, gq, gk, gv, go, g1, s1, bo, bq, bv, cols_a, cols_b, small):
    depth = gq.shape[0]
    quarter, half = depth // 4, depth // 2
    n = mine.shape[0] // 4
    for sib, held in ((0, mine), (1, sibling)):
        for other in range(4):
            owner = pos[4] ^ (other * 2) ^ sib
            row4 = pl.ds(al((owner // 2) * quarter, 16), quarter)
            col2 = pl.ds(al((owner % 2) * COLS, 128), COLS)
            at = other * n
            cols_a[pl.ds(al((owner % 2) * half, 16), half), pl.ds(al((owner // 2) * COLS, 128), COLS)] = held[
                at : at + half, :
            ].astype(f32)
            at += half
            go[row4, col2] = held[at : at + quarter, :].astype(f32)
            at += quarter
            small[0, owner] = held[at : at + 16, :].astype(f32)[:8]
            at += 16
            cols_b[row4, col2] = held[at : at + quarter, :].astype(f32)
            at += quarter
            small[1, owner] = held[at : at + 16, :].astype(f32)[:8]
    for m, out in enumerate((gq, gk, gv)):
        span = cols_a.shape[1] // 3
        out[:, :span] = cols_a[:, m * span : (m + 1) * span]
        rest = cols_b.shape[1] // 3
        out[:, span:] = cols_b[:, m * rest : (m + 1) * rest]
    for out, which, p in ((g1, 0, 0), (s1, 0, 1), (bo, 0, 2), (bq, 1, 0), (bv, 1, 1)):
        block = small[which, p]
        row = jnp.concatenate([block[0:1, :], block[1:2, :]], axis=1)
        out[...] = own_part(pos, row, out.shape[1])


def shards(
    tokens,
    lengths,
    cotangent,
    query_weight,
    query_bias,
    key_weight,
    value_weight,
    value_bias,
    out_weight,
    out_bias,
    norm_gain,
    norm_shift,
    up_weight,
    up_bias,
    down_weight,
    down_bias,
    final_gain,
    final_shift,
):
    groups = lax.axis_size("grp")
    pairs, seqlen, width = tokens.shape
    rows = pairs * seqlen
    depth = width // groups
    wide = up_weight.shape[1]
    inputs = tokens.reshape(rows, width)
    upstream = cotangent.reshape(rows, width)
    pos = position()
    n1 = 3 * depth // 4
    n2 = depth + depth // 4
    n3 = depth

    def cut(kernel, sizes, args, specs):
        return pl.pallas_call(
            kernel,
            grid_spec=pltpu.PrefetchScalarGridSpec(
                num_scalar_prefetch=1,
                grid=(1,),
                in_specs=specs,
                out_specs=[pl.BlockSpec((n, COLS), lambda i, at: (0, 0)) for n in sizes],
            ),
            out_shape=[shape((n, COLS), bf16) for n in sizes],
            name=kernel.__name__,
        )(pos, *args)

    square = pl.BlockSpec((depth // 4, COLS), lambda i, at: (at[4] // 2, at[4] % 2))
    (first,) = cut(cut_first, (n1,), (query_weight, key_weight, value_weight), [square] * 3)
    z1 = [to_grp(first, step) for step in range(1, groups)]
    small = jnp.concatenate(
        after(
            [
                query_bias,
                value_bias,
                out_bias,
                norm_gain,
                norm_shift,
                down_bias,
                final_gain,
                final_shift,
                up_bias,
            ],
            first,
        )
    )
    count = small.shape[0] // COLS
    small = jnp.pad(small.reshape(count, COLS), ((0, 16 - count), (0, 0)))
    second, third = cut(
        cut_more,
        (n2 + 16, n3),
        (out_weight, up_weight, down_weight, small),
        [
            square,
            pl.BlockSpec((depth // 2, 2 * COLS), lambda i, at: (at[4] % 2, at[4] // 2)),
            pl.BlockSpec((down_weight.shape[0] // LOCAL, width), lambda i, at: (at[4], 0)),
            pl.BlockSpec((16, COLS), lambda i, at: (0, 0)),
        ],
    )

    def near(mine):
        return [mine, *(to_rep(mine, bit) for bit in (2, 4, 6))]

    def other_core(held):
        return [to_rep(part, 1) for part in held]

    def doubled(own):
        near_zone = to_grp(own, 1)
        pair = jnp.concatenate([own, near_zone], axis=0)
        return near_zone, to_grp(pair, 2)

    mine1 = jnp.concatenate(z1, axis=0)
    held1 = [mine1, to_rep(mine1, 2), to_rep(mine1, 4)]
    cut_at = (mine1.shape[0] // 2 + 47) // 48 * 48
    second = after(second, z1)
    parts = [second] + [to_grp(second, step) for step in range(1, groups)]
    held1 += [to_rep(held1[1][:cut_at], 4), to_rep(held1[2][cut_at:], 2)]
    held1 += other_core(held1)
    flat = jnp.stack([part[n2 : n2 + count].reshape(-1) for part in parts])
    by_zone = jnp.stack([flat[pos[0] ^ zone] for zone in range(groups)]).astype(f32)
    vectors = by_zone[:, : 8 * depth].reshape(groups, 8, depth).transpose(1, 0, 2).reshape(8, width)
    up_vector = by_zone[:, 8 * depth :].reshape(1, wide)
    mine2 = after(jnp.concatenate([part[:n2] for part in parts[1:]], axis=0), held1[:5])
    held2 = near(mine2)
    held2 += other_core(held2[:1])
    one, two = doubled(after(third, parts[1:]))

    row_block = 256
    blocks_of = rows // row_block
    mat = shape((rows, width), bf16)
    mat32 = shape((rows, width), f32)
    dense = 2 * rows * width * width
    by_pair = pl.BlockSpec((seqlen, width), lambda i: (i, 0))
    q, k, v, mixed, logsum, w_all = call(
        attend,
        (mat, mat, mat, mat, shape((pairs, 16, seqlen), f32), shape((width, 3 * width), bf16)),
        (pos, lengths, after(inputs, (mine2, one)), query_weight, key_weight, value_weight, vectors, *held1),
        [SMEM, SMEM, by_pair, ANY, ANY, ANY, VMEM] + [ANY] * 10,
        (by_pair,) * 4 + (pl.BlockSpec((1, 16, seqlen), lambda i: (i, 0, 0)), ANY),
        scratch=[
            pltpu.VMEM((width, 3 * width), bf16),
            pltpu.SemaphoreType.DMA((4 + 8 * (groups - 1) * 3,)),
        ],
        grid=(pairs,),
        flops=12 * dense,
        moved=12 * rows * width,
    )
    held2 += other_core(after(held2[1:4], (w_all, two)))
    held3 = near(jnp.concatenate([one, two], axis=0))
    held3 += other_core(held3[:1])
    by_row = pl.BlockSpec((row_block, width), lambda i: (i, 0))
    by_wide = pl.BlockSpec((row_block, wide), lambda i: (i, 0))
    by_lane = pl.BlockSpec((row_block, 128), lambda i: (i, 0))
    act, slope, normed, inverse, wu_all, wo_all = call(
        expand,
        (
            shape((rows, wide), bf16),
            shape((rows, wide), bf16),
            mat32,
            shape((rows, 128), f32),
            shape((width, wide), bf16),
            shape((width, width), bf16),
        ),
        (pos, after(inputs, held3[0]), mixed, up_weight, out_weight, vectors, up_vector, *held2),
        [SMEM, by_row, by_row, ANY, ANY, VMEM, VMEM] + [ANY] * 8,
        (by_wide, by_wide, by_row, by_lane, ANY, ANY),
        scratch=[
            pltpu.VMEM((width, wide), bf16),
            pltpu.VMEM((width, width), bf16),
            pltpu.SemaphoreType.DMA((4 + 8 * (groups - 1) * 3,)),
        ],
        grid=(blocks_of,),
        flops=8 * dense,
        moved=18 * rows * width,
    )
    held3 = after(held3, wo_all)
    held3 += other_core(held3[1:4])

    stay = lambda i: (jnp.minimum(i, blocks_of - 1), 0)
    by_row = pl.BlockSpec((row_block, width), stay)
    by_wide = pl.BlockSpec((row_block, wide), stay)
    by_lane = pl.BlockSpec((row_block, 128), stay)
    vec = shape((8, width), f32)
    vec_out = pl.BlockSpec((8, width), lambda i: (0, 0))

    def travelling(n):
        return (shape((groups, 4, n, COLS), bf16),) * 2

    output, grad_second, send, last_sums, wd_all = call(
        contract,
        (mat, mat32, shape((LOCAL, groups, n3, COLS), bf16), vec, shape((wide, width), bf16)),
        (pos, lengths, act, normed, upstream, down_weight, vectors, *held3),
        [SMEM, SMEM, ANY, by_row, by_row, ANY, VMEM] + [ANY] * 8,
        (by_row, by_row, ANY, vec_out, ANY),
        scratch=[
            pltpu.VMEM((wide, width), bf16),
            pltpu.VMEM((rows, wide), bf16),
            pltpu.VMEM((rows, width), bf16),
            pltpu.VMEM((wide, width), bf16),
            pltpu.SemaphoreType.DMA((4 + 8 * (groups - 1) * 2,)),
            pltpu.SemaphoreType.DMA((blocks_of,)),
            pltpu.SemaphoreType.DMA((groups * 4 * 2 * 2,)),
        ],
        grid=(blocks_of + 1,),
        flops=8 * dense,
        moved=16 * rows * width,
    )
    ring = lax.axis_size("rep")
    circles = [list(range(i, i + LOCAL)) for i in range(0, ring, LOCAL)] if ring > LOCAL else None
    down = lax.psum_scatter(
        send.reshape(LOCAL * groups * n3, COLS),
        "rep",
        scatter_dimension=0,
        tiled=True,
        axis_index_groups=circles,
    )

    n_up = depth + 16
    expos, send, keep = call(
        up_back,
        (shape((rows, wide), bf16), *travelling(n_up)),
        (pos, grad_second, slope, normed, wd_all, vectors, last_sums),
        [SMEM, by_row, by_wide, by_row, VMEM, VMEM, VMEM],
        (by_wide, ANY, ANY),
        scratch=[
            pltpu.VMEM((rows, wide), bf16),
            pltpu.VMEM((rows, width), bf16),
            pltpu.VMEM((width, wide), bf16),
            pltpu.VMEM((8, wide), f32),
            pltpu.VMEM((LOCAL, 16, COLS), bf16),
            pltpu.SemaphoreType.DMA((groups * 4 * 2 * 3,)),
        ],
        grid=(blocks_of + 1,),
        flops=8 * dense,
        moved=30 * rows * width,
    )
    up = Reduce(pos, send, keep)

    grad_first, grad_mixed, first_sums, grad_out = call(
        hidden_back,
        (mat32, mat, vec, shape((width, width), bf16)),
        (grad_second, expos, normed, inverse, mixed, wu_all, wo_all, vectors),
        [by_row, by_wide, by_row, by_lane, VMEM, VMEM, VMEM, VMEM],
        (by_row, by_row, vec_out, pl.BlockSpec((width, width), lambda i: (0, 0))),
        scratch=[pltpu.VMEM((rows, width), bf16)],
        grid=(blocks_of + 1,),
        flops=6 * dense,
        moved=30 * rows * width,
    )
    done = up.one(grad_mixed)

    def heads_call(first, count, n, extra, extra_specs, done, sums_out):
        span = count * 128
        part = lambda i: (jnp.minimum(i, pairs - 1), first * 128 // span)
        by_pair = pl.BlockSpec((seqlen, span), part)
        outs = (shape((rows, 3 * span), bf16), *travelling(n)) + ((vec,) if sums_out else ())
        out_specs = (
            pl.BlockSpec((seqlen, 3 * span), lambda i: (jnp.minimum(i, pairs - 1), 0)),
            ANY,
            ANY,
        ) + ((vec_out,) if sums_out else ())
        scratch = [
            pltpu.VMEM((rows, 3 * span), bf16),
            pltpu.VMEM((width, 3 * span), bf16),
            pltpu.VMEM((16, seqlen), f32),
        ]
        scratch += [] if sums_out else [pltpu.VMEM((8, width), f32)]
        scratch += [
            pltpu.VMEM((LOCAL, 16, COLS), bf16),
            pltpu.SemaphoreType.DMA((groups * 4 * 2 * 3,)),
        ]
        return call(
            attend_back,
            outs,
            (pos, lengths, after(inputs, done), q, k, v, mixed, grad_mixed, logsum, *extra),
            [SMEM, SMEM, VMEM]
            + [by_pair] * 5
            + [pl.BlockSpec((1, 16, seqlen), lambda i: (jnp.minimum(i, pairs - 1), 0, 0))]
            + extra_specs,
            out_specs,
            scratch=scratch,
            grid=(pairs + 1,),
            flops=4 * dense * count,
            moved=4 * rows * width * count,
            first=first,
            count=count,
        )

    grads_a, send, keep, sums = heads_call(
        0, 4, depth // 2 + depth // 4 + 16, (grad_out, first_sums), [VMEM, VMEM], done, True
    )
    part_a = Reduce(pos, send, keep)
    by_row = pl.BlockSpec((row_block, width), lambda i: (i, 0))

    def inputs_call(sofar, grads, first, last, dtype):
        return call(
            inputs_back,
            shape((rows, width), dtype),
            (sofar, grads, w_all),
            [by_row, pl.BlockSpec((row_block, grads.shape[1]), lambda i: (i, 0)), VMEM],
            by_row,
            grid=(blocks_of,),
            flops=dense * grads.shape[1] // width,
            moved=16 * rows * width,
            first=first,
        )

    done = up.two(grads_a)
    sofar = inputs_call(after(grad_first, done), grads_a, 0, False, f32)
    done = part_a.one(sofar)
    grads_b, send, keep = heads_call(4, 2, depth // 4 + 16, (sums,), [VMEM], done, False)
    part_b = Reduce(pos, send, keep)
    total = up.zones(down.reshape(groups, n3, COLS), grads_b)
    total = lax.psum_scatter(total.reshape(-1, COLS), "grp", scatter_dimension=0, tiled=True)
    done = (part_a.two(grads_b), part_b.direct(grads_b))
    grad_inputs = inputs_call(after(sofar, done), grads_b, grads_a.shape[1] // 3, True, bf16)
    done = part_a.three_with(part_b, grad_inputs)
    shared = lax.all_gather(
        over_blocks(after(total, done)), "rep", axis=0, tiled=True, axis_index_groups=circles
    )
    part_a.four()
    part_a.around()
    part_a.five()
    vector = shape((1, depth), f32)
    gd, gu, g2, s2, bd, bu = call(
        place_ffn,
        (shape((wide // groups, width), f32), shape((depth, wide), f32), vector, vector, vector)
        + (shape((1, wide // groups), f32),),
        (pos, shared),
        [SMEM, VMEM],
        (VMEM,) * 6,
        moved=24 * depth * width,
    )
    square = shape((depth, width), f32)
    gq, gk, gv, go, g1, s1, bo, bq, bv = call(
        place_heads,
        (square,) * 4 + (vector,) * 5,
        (pos, *part_a.both),
        [SMEM] + [VMEM] * 2,
        (VMEM,) * 9,
        scratch=[
            pltpu.VMEM((depth, 2 * width), f32),
            pltpu.VMEM((depth, width), f32),
            pltpu.VMEM((2, LOCAL, 8, COLS), f32),
        ],
        moved=24 * depth * width,
    )
    bq, bv, bo, g1, s1, bu, bd, g2, s2 = (
        row.reshape(-1) for row in (bq, bv, bo, g1, s1, bu, bd, g2, s2)
    )
    return (
        output.reshape(pairs, seqlen, width),
        grad_inputs.reshape(pairs, seqlen, width),
        gq,
        bq,
        gk,
        gv,
        bv,
        go,
        bo,
        g1,
        s1,
        gu,
        bu,
        gd,
        bd,
        g2,
        s2,
    )


def solution(mesh):
    pairs = P(("grp", "rep"), None, None)
    matrix = P("grp", None)
    vector = P("grp")
    placed = (pairs, P(("grp", "rep")), pairs, matrix, vector, matrix, matrix, vector, matrix, vector)
    placed += (vector, vector, matrix, vector, matrix, vector, vector, vector)
    results = (pairs, pairs, matrix, vector, matrix, matrix, vector, matrix, vector, vector, vector)
    results += (matrix, vector, matrix, vector, vector, vector)
    return jax.shard_map(shards, mesh=mesh, in_specs=placed, out_specs=results, check_vma=False)
```

```python
import functools

import jax
import jax.numpy as jnp
from jax import lax
from jax.experimental import pallas as pl
from jax.experimental.pallas import tpu as pltpu
from jax.sharding import PartitionSpec as P

H = 12
HD = 64
EPSILON = 1e-06
MASKED = -1e30
DENSITY = 0.3989422804014327
ROOT_HALF = 0.7071067811865476

f32 = jnp.float32
bf16 = jnp.bfloat16
VMEM = pl.BlockSpec(memory_space=pltpu.VMEM)
SMEM = pl.BlockSpec(memory_space=pltpu.SMEM)
ANY = pl.BlockSpec(memory_space=pl.ANY)
VMEM_LIMIT = 63 * 2**20
COLS = 384
WEIGHT = 20
LOCAL = 8


def dot(a, b):
    return jnp.dot(a, b, preferred_element_type=f32)


def nt(a, b):
    return lax.dot_general(a, b, (((1,), (1,)), ((), ())), preferred_element_type=f32)


def tn(a, b):
    return lax.dot_general(a, b, (((0,), (0,)), ((), ())), preferred_element_type=f32)


def shape(dims, dtype):
    return jax.ShapeDtypeStruct(dims, dtype)


def al(value, by):
    return pl.multiple_of(value, by)


def call(kernel, outs, args, specs, out_specs, scratch=(), grid=(), flops=0, moved=0, aliases=None, **fixed):
    return pl.pallas_call(
        functools.partial(kernel, **fixed) if fixed else kernel,
        grid=grid,
        out_shape=outs,
        in_specs=specs,
        out_specs=out_specs,
        scratch_shapes=scratch,
        input_output_aliases=aliases or {},
        compiler_params=pltpu.CompilerParams(vmem_limit_bytes=VMEM_LIMIT),
        cost_estimate=pl.CostEstimate(
            flops=WEIGHT * flops, bytes_accessed=WEIGHT * moved, transcendentals=0
        ),
        name=kernel.__name__,
    )(*args)


def after(values, *events):
    return lax.optimization_barrier((values, events))[0]


def to_rep(array, bit):
    size = lax.axis_size("rep")
    return lax.ppermute(array, "rep", [(i, i ^ bit) for i in range(size)])


def to_grp(array, bit):
    size = lax.axis_size("grp")
    return lax.ppermute(array, "grp", [(i, i ^ bit) for i in range(size)])


def position():
    z = lax.axis_index("grp").astype(jnp.int32)
    p = lax.axis_index("rep").astype(jnp.int32) % LOCAL
    return jnp.stack([z, (p // 2) % 2, p // 4, p % 2, p])


class Copies:
    def __init__(self, sems):
        self.sems, self.held = sems, []

    def add(self, src, dst):
        copy = pltpu.make_async_copy(src, dst, self.sems.at[len(self.held)])
        copy.start()
        self.held.append(copy)

    def wait(self):
        for copy in self.held:
            copy.wait()


def piece_refs(kind, ref, zone, p, depth):
    if kind == "tall":
        rows = depth // LOCAL
        start = al(zone * depth + p * rows, 16)
        return [
            (ref.at[pl.ds(start, rows), pl.ds(half * COLS, COLS)], rows) for half in range(2)
        ]
    if kind == "wide":
        rows = depth // 2
        start = al(zone * depth + (p % 2) * rows, 16)
        return [
            (
                ref.at[pl.ds(start, rows), pl.ds(al((p // 2) * 2 * COLS + half * COLS, 128), COLS)],
                rows,
            )
            for half in range(2)
        ]
    if kind == "half":
        rows = depth // 2
        start = al(zone * depth + (p % 2) * rows, 16)
        return [(ref.at[pl.ds(start, rows), pl.ds(al((p // 2) * COLS, 128), COLS)], rows)]
    rows = depth // 4
    offset = int(kind)
    start = al(zone * depth + (p // 2) * rows, 16)
    return [(ref.at[pl.ds(start, rows), pl.ds(al(offset + (p % 2) * COLS, 128), COLS)], rows)]


def own_slab(ref, zone, depth, first=0, width=None):
    width = ref.shape[1] if width is None else width
    return ref.at[pl.ds(al(zone * depth, 16), depth), pl.ds(first, width)]


def block_rows(parts):
    return sum(rows for kind, ref, depth in parts for _, rows in piece_refs(kind, ref, 0, 0, depth))


def fetch(copies, pos, parts, held):
    zone, p = pos[0], pos[4]
    groups = lax.axis_size("grp")
    side = len(held) // 2
    n = held[0].shape[0] // (groups - 1) // (4 // side)
    for sib in range(2):
        for other in range(4):
            owner = p ^ (other * 2) ^ sib
            part = held[side * sib + other % side]
            at = 0 if side == 4 else other * (groups - 1) * n
            for step in range(1, groups):
                source = zone ^ step
                skip = at + n
                for kind, ref, depth in parts:
                    for place, rows in piece_refs(kind, ref, source, owner, depth):
                        copies.add(part.at[pl.ds(at, rows), :], place)
                        at += rows
                at = skip


def emit(copies, pos, parts, send, keep, quads=range(4), base=0, zones=None):
    core = pos[3]
    zones = range(lax.axis_size("grp")) if zones is None else zones
    for held, flip in ((send, 1), (keep, 0)):
        for zone in zones:
            for q in quads:
                owner = q * 2 + (core ^ flip)
                at = base
                for kind, ref, depth in parts:
                    for place, rows in piece_refs(kind, ref, zone, owner, depth):
                        copies.add(place, held.at[zone, q, pl.ds(at, rows), :])
                        at += rows


def add_first(pos, keep, got, sa, ka, sb, kb, kept, gotten, oa, pa, ob, pb, sems, out_sems):
    x, y = pos[1], pos[2]
    groups = keep.shape[0]
    half = groups // 2
    loads = [Copies(sems.at[zone]) for zone in range(groups)]
    for zone, load in enumerate(loads):
        load.add(keep.at[zone], kept.at[zone])
        load.add(got.at[zone], gotten.at[zone])
    stores = Copies(out_sems)
    for zone, load in enumerate(loads):
        load.wait()
        if zone < half:
            places = [(oa, j, j * 2 + (1 - x)) for j in range(2)] + [(pa, j, j * 2 + x) for j in range(2)]
            pairs = ((oa, sa), (pa, ka))
        else:
            places = [(ob, j, (1 - y) * 2 + j) for j in range(2)] + [(pb, j, y * 2 + j) for j in range(2)]
            pairs = ((ob, sb), (pb, kb))
        at = zone % half
        for ref, j, q in places:
            ref[at, j] = kept[zone, q] + gotten[zone, q]
        for ref, out in pairs:
            stores.add(ref.at[at], out.at[at])
    stores.wait()


def add_second(pos, ka, ra, kb, rb, sa, ja, sb, jb):
    x, y = pos[1], pos[2]
    for zone in range(ka.shape[0]):
        for kept, got, send, hold, at in ((ka, ra, sa, ja, y), (kb, rb, sb, jb, x)):
            send[zone] = kept[zone, 1 - at] + got[zone, 1 - at]
            hold[zone] = kept[zone, at] + got[zone, at]


def add_third(pos, ka, ra, kb, rb, *rest):
    outs, total = rest[:-1], rest[-1]
    half = ka.shape[0]
    for zone in range(half):
        total[zone] = ka[zone] + ra[zone]
        total[half + zone] = kb[zone] + rb[zone]
    for step, out in enumerate(outs):
        out[...] = total[pos[0] ^ step]


def add_fourth(*refs):
    total = refs[0][...].astype(f32)
    for ref in refs[1:-1]:
        total = total + ref[...].astype(f32)
    refs[-1][...] = total.astype(bf16)


def over_blocks(total):
    bit = LOCAL
    while bit < lax.axis_size("rep"):
        other = to_rep(total, bit)
        total = call(add_fourth, shape(total.shape, bf16), (total, other), [VMEM] * 2, VMEM)
        bit *= 2
    return total


class Reduce:
    def __init__(self, pos, send, keep):
        self.pos, self.keep = pos, keep
        self.n = keep.shape[2]
        self.size = keep.shape[0] * 4 * self.n * COLS * 2
        self.got = to_rep(send, 1)

    def one(self, *events):
        groups = self.keep.shape[0]
        quad = shape((groups // 2, 2, self.n, COLS), bf16)
        got = after(self.got, *events)
        block = pltpu.VMEM(self.keep.shape, bf16)
        part = pltpu.VMEM(quad.shape, bf16)
        sa, self.ka, sb, self.kb = call(
            add_first,
            (quad,) * 4,
            (self.pos, self.keep, got),
            [SMEM, ANY, ANY],
            (ANY,) * 4,
            scratch=[block, block, part, part, part, part]
            + [pltpu.SemaphoreType.DMA((groups, 2)), pltpu.SemaphoreType.DMA((2 * groups,))],
            moved=3 * self.size,
        )
        self.ra, self.rb = to_rep(sa, 2), to_rep(sb, 4)
        return self.ka

    def two(self, *events):
        pair = shape((self.ka.shape[0], self.n, COLS), bf16)
        ra, rb = after((self.ra, self.rb), *events)
        sa, self.ja, sb, self.jb = call(
            add_second,
            (pair,) * 4,
            (self.pos, self.ka, ra, self.kb, rb),
            [SMEM] + [VMEM] * 4,
            (VMEM,) * 4,
            moved=3 * self.size // 2,
        )
        self.ra, self.rb = to_rep(sa, 4), to_rep(sb, 2)
        return self.ja

    def three(self, *events):
        groups = self.keep.shape[0]
        ra, rb = after((self.ra, self.rb), *events)
        self.blocks = call(
            add_third,
            (shape((self.n, COLS), bf16),) * groups,
            (self.pos, self.ja, ra, self.jb, rb),
            [SMEM] + [VMEM] * 4,
            (VMEM,) * groups,
            scratch=[pltpu.VMEM((groups, self.n, COLS), bf16)],
            moved=3 * self.size // 4,
        )
        self.arrived = [to_grp(self.blocks[step], step) for step in range(1, groups)]
        return self.blocks[0]

    def four(self, *events):
        arrived = after(self.arrived, *events)
        total = call(
            add_fourth,
            shape((self.n, COLS), bf16),
            (self.blocks[0], *arrived),
            [VMEM] * (1 + len(arrived)),
            VMEM,
            moved=self.size // 3,
        )
        self.total = over_blocks(total)
        return self.total

    def around(self):
        self.near = [to_rep(self.total, bit) for bit in (2, 4, 6)]

    def five(self, *events):
        near = after(self.near, *events)
        held = jnp.concatenate([self.total, *near], axis=0)
        self.both = held, to_rep(held, 1)
        return held


def cut_first(pos, wq, wk, wv, wd, first, third):
    quarter, tall = wq.shape[0], wd.shape[0]
    for m, ref in enumerate((wq, wk, wv)):
        first[m * quarter : (m + 1) * quarter, :] = ref[...]
    for j in range(2):
        third[j * tall : (j + 1) * tall, :] = wd[:, j * COLS : (j + 1) * COLS]


def cut_more(pos, wo, wu, small, second):
    half, quarter = wu.shape[0], wo.shape[0]
    for j in range(2):
        second[j * half : (j + 1) * half, :] = wu[:, j * COLS : (j + 1) * COLS]
    second[2 * half : 2 * half + quarter, :] = wo[...]
    second[2 * half + quarter :, :] = small[...]


def join(*refs, counts):
    first = 0
    for count, out in zip(counts, refs[-len(counts) :]):
        at = 0
        for ref in refs[first : first + count]:
            out[at : at + ref.shape[0], :] = ref[...]
            at += ref.shape[0]
        first += count


def joined(*lists):
    blocks = [block for one in lists for block in one]
    return call(
        join,
        tuple(shape((sum(block.shape[0] for block in one), COLS), bf16) for one in lists),
        blocks,
        [VMEM] * len(blocks),
        (VMEM,) * len(lists),
        moved=sum(block.shape[0] for block in blocks) * COLS * 4,
        counts=tuple(len(one) for one in lists),
    )


def layer_norm(values):
    centred = values - jnp.mean(values, axis=-1, keepdims=True)
    spread_of = jnp.mean(centred * centred, axis=-1, keepdims=True)
    inverse = lax.rsqrt(spread_of + EPSILON)
    return centred * inverse, inverse


def norm_back(upstream, normed, inverse, gain):
    scaled = upstream * gain
    return inverse * (
        scaled
        - jnp.mean(scaled, axis=-1, keepdims=True)
        - normed * jnp.mean(scaled * normed, axis=-1, keepdims=True)
    )


def attend_heads(lengths, x, vectors, weight, q_out, k_out, v_out, mixed, logsum, pair):
    width = x.shape[1]
    rows = x[...]
    scaling = HD ** (-0.5)
    q_out[...] = (
        (dot(rows, weight[:, :width]) + vectors[0:1, :]).astype(bf16).astype(f32) * scaling
    ).astype(bf16)
    k_out[...] = dot(rows, weight[:, width : 2 * width]).astype(bf16)
    v_out[...] = (dot(rows, weight[:, 2 * width :]) + vectors[1:2, :]).astype(bf16)
    slots = rows.shape[0]
    lane = lax.broadcasted_iota(jnp.int32, (slots, 128), 1)
    low = lane < HD
    slot = lax.broadcasted_iota(jnp.int32, (1, slots), 1)
    bias = jnp.where(slot < lengths[pair], 0.0, MASKED).astype(f32)

    def heads(h, sums):
        s = pl.ds(al(h * 128, 128), 128)
        q1, k1, v1 = q_out[:, s], k_out[:, s], v_out[:, s]
        results, peaks = [], []
        for e in range(2):
            mask = low if e == 0 else ~low
            scores = nt(jnp.where(mask, q1, 0).astype(bf16), k1) + bias
            peak = jnp.max(scores, axis=1, keepdims=True)
            expo = jnp.exp(scores - peak).astype(bf16)
            results.append(dot(expo, jnp.where(mask, v1, 1).astype(bf16)))
            peaks.append(peak)
        total = pltpu.roll(jnp.where(low, results[1], results[0]), HD, 1)
        mixed[:, s] = (jnp.where(low, results[0], results[1]) / total).astype(bf16)
        sums = jnp.where(lane % HD == h, jnp.where(low, peaks[0], peaks[1]) + jnp.log(total), sums)
        return sums

    sums = lax.fori_loop(0, H // 2, heads, jnp.zeros((slots, 128), f32), unroll=True)
    turned = sums.T
    logsum[0, :8] = turned[:8]
    logsum[0, 8:] = turned[HD : HD + 8]


def attend(pos, lengths, x, wq, wk, wv, vectors, *rest):
    held, (q_out, k_out, v_out, mixed, logsum, w_out, weight, sems) = rest[:2], rest[2:]
    depth, width = wq.shape
    pair = pl.program_id(0)
    write = pltpu.make_async_copy(weight, w_out, sems.at[sems.shape[0] - 1])

    @pl.when(pair == 0)
    def _():
        copies = Copies(sems)
        for m, ref in enumerate((wq, wk, wv)):
            copies.add(ref, own_slab(weight, pos[0], depth, m * width, width))
        fetch(copies, pos, [(str(m * width), weight, depth) for m in range(3)], held)
        copies.wait()
        write.start()

    attend_heads(lengths, x, vectors, weight, q_out, k_out, v_out, mixed, logsum, pair)

    @pl.when(pair == pl.num_programs(0) - 1)
    def _():
        write.wait()


def expand_rows(x, mixed, vectors, up_bias, up, out_w, act, slope, normed, inverse):
    first = x[...].astype(f32) + dot(mixed[...], out_w[...]) + vectors[2:3, :]
    normal, scale = layer_norm(first)
    normed[...] = normal
    inverse[...] = jnp.broadcast_to(scale, inverse.shape)
    hidden = (normal * vectors[3:4, :] + vectors[4:5, :]).astype(bf16)
    chunk = 768
    for j in range(up.shape[1] // chunk):
        s = slice(j * chunk, (j + 1) * chunk)
        u = dot(hidden, up[:, s]) + up_bias[:, s]
        cdf, pdf = gaussian(u)
        act[:, s] = (u * cdf).astype(bf16)
        slope[:, s] = (cdf + u * pdf).astype(bf16)


def expand(pos, x, mixed, wu, wo, vectors, up_bias, *rest):
    held, (act, slope, normed, inverse, wu_out, wo_out, up, out_w, sems) = rest[:8], rest[8:]
    step = pl.program_id(0)
    depth = wo.shape[0]
    last = sems.shape[0]
    writes = [
        pltpu.make_async_copy(up, wu_out, sems.at[last - 1]),
        pltpu.make_async_copy(out_w, wo_out, sems.at[last - 2]),
    ]

    @pl.when(step == 0)
    def _():
        copies = Copies(sems)
        copies.add(wu, own_slab(up, pos[0], depth))
        copies.add(wo, own_slab(out_w, pos[0], depth))
        fetch(copies, pos, [("wide", up, depth), ("0", out_w, depth)], held)
        copies.wait()
        for write in writes:
            write.start()

    expand_rows(x, mixed, vectors, up_bias, up, out_w, act, slope, normed, inverse)

    @pl.when(step == pl.num_programs(0) - 1)
    def _():
        for write in writes:
            write.wait()


def gaussian(u):
    return 0.5 + 0.5 * lax.erf(u * ROOT_HALF), jnp.exp(-0.5 * u * u) * DENSITY


def feed_forward(pos, lengths, act, slope, normed, inverse, cotangent, mixed, wd, wu, wo, vectors, *rest):
    held, rest = rest[:8], rest[8:]
    output, grad_first, grad_mixed, down_send, down_keep, send, keep = rest[:7]
    down, acts, expos, hiddens, lows, lows_first, grad_out, last_sums, first_sums, up_sums, blocks = rest[7:18]
    up, out_w, mixes, sems, act_sems, out_sems, late_sems = rest[18:]
    step = pl.program_id(0)
    steps = pl.num_programs(0) - 1
    depth = wd.shape[0]
    rows, width = normed.shape

    def part(i):
        return pltpu.make_async_copy(
            act.at[pl.ds(al(i * rows, 16), rows), :],
            acts.at[pl.ds(al(i * rows, 16), rows), :],
            act_sems.at[i],
        )

    def late(i):
        return pltpu.make_async_copy((wu, wo, mixed)[i], (up, out_w, mixes)[i], late_sems.at[i])

    @pl.when(step == 0)
    def _():
        copies = Copies(sems)
        copies.add(wd, own_slab(down, pos[0], depth))
        fetch(copies, pos, [("tall", down, depth)], held)
        for i in range(act_sems.shape[0]):
            part(i).start()
        for i in range(3):
            late(i).start()
        copies.wait()
        late(0).wait()
        late(1).wait()
        last_sums[...] = jnp.zeros_like(last_sums)
        first_sums[...] = jnp.zeros_like(first_sums)
        up_sums[...] = jnp.zeros_like(up_sums)

    @pl.when(step < steps)
    def _():
        part(step).wait()
        s = pl.ds(al(step * rows, 16), rows)
        per_pair = acts.shape[0] // lengths.shape[0] // rows
        slot = lax.broadcasted_iota(jnp.int32, (rows, 1), 0) + lax.rem(step, per_pair) * rows
        mask = (slot < lengths[step // per_pair]).astype(f32)
        first_normal = normed[...]
        first_gain = vectors[3:4, :]
        hidden = first_normal * first_gain + vectors[4:5, :]
        hiddens[s, :] = hidden.astype(bf16)
        second = hidden + dot(acts[s, :], down[...]) + vectors[5:6, :]
        normal, scale = layer_norm(second)
        gain = vectors[6:7, :]
        output[...] = ((normal * gain + vectors[7:8, :]) * mask).astype(bf16)
        upstream = cotangent[...].astype(f32) * mask
        grad_second = norm_back(upstream, normal, scale, gain)
        low = grad_second.astype(bf16)
        lows[s, :] = low
        last_sums[0:1, :] += jnp.sum(upstream * normal, axis=0, keepdims=True)
        last_sums[1:2, :] += jnp.sum(upstream, axis=0, keepdims=True)
        last_sums[2:3, :] += jnp.sum(low.astype(f32), axis=0, keepdims=True)
        chunk = 768
        for j in range(expos.shape[1] // chunk):
            c = slice(j * chunk, (j + 1) * chunk)
            grown = (nt(low, down[c, :]) * slope[:, c].astype(f32)).astype(bf16)
            expos[s, c] = grown
            up_sums[0:1, c] += jnp.sum(grown.astype(f32), axis=0, keepdims=True)
        upstream = grad_second + nt(expos[s, :], up[...])
        result = norm_back(upstream, first_normal, inverse[:, 0:1], first_gain)
        grad_first[...] = result
        low = result.astype(bf16)
        lows_first[s, :] = low
        grad_mixed[...] = nt(low, out_w[...]).astype(bf16)
        first_sums[0:1, :] += jnp.sum(upstream * first_normal, axis=0, keepdims=True)
        first_sums[1:2, :] += jnp.sum(upstream, axis=0, keepdims=True)
        first_sums[2:3, :] += jnp.sum(low.astype(f32), axis=0, keepdims=True)

    @pl.when(step == steps)
    def _():
        copies = Copies(out_sems)
        for zone in range(down.shape[0] // depth):
            s = slice(zone * depth, (zone + 1) * depth)
            down[s, :] = tn(acts[:, s], lows[...]).astype(bf16)
            emit(copies, pos, [("tall", down, depth)], down_send, down_keep, zones=(zone,))
        grad_up = acts.at[pl.ds(0, width), :]
        up_depth = width // lax.axis_size("grp")
        chunk = 2 * COLS
        for j in range(acts.shape[1] // chunk):
            c = slice(j * chunk, (j + 1) * chunk)
            acts[:width, c] = tn(hiddens[...], expos[:, c]).astype(bf16)
            emit(copies, pos, [("wide", grad_up, up_depth)], send, keep, (j,))
        late(2).wait()
        grad_out[...] = tn(mixes[...], lows_first[...]).astype(bf16)
        emit(copies, pos, [("0", grad_out, up_depth)], send, keep, base=up_depth)
        vector_blocks(
            blocks,
            [last_sums[i : i + 1, :] for i in range(3)]
            + [up_sums[0:1, j * width : (j + 1) * width] for j in range(4)]
            + [first_sums[i : i + 1, :] for i in range(3)],
        )
        emit_vectors(copies, pos, blocks, up_depth + up_depth // 4, send, keep)
        copies.wait()


def vector_blocks(blocks, rows):
    blocks[...] = jnp.zeros_like(blocks)
    for p in range(min(LOCAL, len(rows))):
        here = rows[p::LOCAL]
        half = here[0].shape[1] // 2
        stacked = [part for row in here for part in (row[:, :half], row[:, half:])]
        stacked.append(jnp.zeros((16 - 2 * len(here), half), f32))
        blocks[p] = jnp.concatenate(stacked, axis=0).astype(bf16)


def vector_of(block, i):
    at = 2 * (i // LOCAL)
    return jnp.concatenate([block[at : at + 1, :], block[at + 1 : at + 2, :]], axis=1)


def emit_vectors(copies, pos, blocks, base, send, keep):
    for held, flip in ((send, 1), (keep, 0)):
        for zone in range(send.shape[0]):
            for q in range(4):
                owner = q * 2 + (pos[3] ^ flip)
                copies.add(blocks.at[owner], held.at[zone, q, pl.ds(base, 16), :])


def pair_back(lengths, q, k, v, mixed, grad_mixed, logsum, *rest, pair):
    if pair:
        old_sums, rest = rest[0], rest[2:]
    grads, sums, rows_of, held, deltas, in_sems, out_sem = rest
    slots, width = held.shape[0], q.shape[1]
    here = pl.ds(pair * slots, slots)
    copies = Copies(in_sems)
    for i, ref in enumerate((mixed, grad_mixed, q, k, v)):
        copies.add(ref.at[here, :], rows_of.at[i])
    sums[...] = old_sums[...] if pair else jnp.zeros_like(sums)
    low = lax.broadcasted_iota(jnp.int32, (slots, 128), 1) < HD
    slot = lax.broadcasted_iota(jnp.int32, (slots, 1), 0)
    select = (
        lax.broadcasted_iota(jnp.int32, (16, width), 1) // HD
        == lax.broadcasted_iota(jnp.int32, (16, width), 0)
    ).astype(bf16)
    scaling = HD ** (-0.5)
    bias = jnp.where(slot < lengths[pair], 0.0, MASKED).astype(f32)
    copies.wait()
    product = rows_of[0].astype(f32) * rows_of[1].astype(f32)
    high = product.astype(bf16)
    rest_of = (product - high.astype(f32)).astype(bf16)
    deltas[...] = nt(select, high) + nt(select, rest_of)

    def heads(h, carry):
        s = pl.ds(al(h * 128, 128), 128)
        g1, q1, k1, v1 = (rows_of[i, :, s] for i in (1, 2, 3, 4))
        probs, scores_back, qs, gs, ks = [], [], [], [], []
        for e in range(2):
            mask = low if e == 0 else ~low
            qm = jnp.where(mask, q1, 0).astype(bf16)
            gm = jnp.where(mask, g1, 0).astype(bf16)
            prob = jnp.exp(nt(k1, qm) + bias - logsum[pair, pl.ds(h + 8 * e, 1), :])
            back = prob * (nt(v1, gm) - deltas[pl.ds(h * 2 + e, 1), :])
            probs.append(prob.astype(bf16))
            scores_back.append(back.astype(bf16))
            qs.append(qm)
            gs.append(gm)
            ks.append(jnp.where(mask, k1, 0).astype(bf16))
        grad_v = dot(jnp.concatenate(probs, 1), jnp.concatenate(gs, 0))
        grad_k = dot(jnp.concatenate(scores_back, 1), jnp.concatenate(qs, 0))
        grad_q = tn(jnp.concatenate(scores_back, 0), jnp.concatenate(ks, 0)) * scaling
        for m, value in enumerate((grad_q, grad_k, grad_v)):
            value = value.astype(bf16)
            held[:, pl.ds(al(m * width + h * 128, 128), 128)] = value
            if m != 1:
                sums[m : m + 1, s] += jnp.sum(value.astype(f32), axis=0, keepdims=True)
        return carry

    lax.fori_loop(0, H // 2, heads, 0, unroll=True)
    store = pltpu.make_async_copy(held, grads.at[here, :], out_sem.at[0])
    store.start()
    store.wait()


def heads_weights(pos, x, grads, sums, send, keep, xs, held, weight_grads, blocks, sems, out_sems):
    width = xs.shape[1]
    depth = width // lax.axis_size("grp")
    copies = Copies(sems)
    copies.add(x, xs)
    for m in range(3):
        c = pl.ds(m * width, width)
        copies.add(grads.at[:, c], held.at[:, c])
    copies.held[0].wait()
    stores = Copies(out_sems)
    vector_blocks(blocks, [sums[m : m + 1, :] for m in (0, 2)])
    emit_vectors(stores, pos, blocks, 3 * depth // 4, send, keep)
    for m in range(3):
        c = slice(m * width, (m + 1) * width)
        copies.held[1 + m].wait()
        weight_grads[:, c] = tn(xs[...], held[:, c]).astype(bf16)
        emit(stores, pos, [(str(m * width), weight_grads, depth)], send, keep, base=m * depth // 4)
    stores.wait()


def inputs_back(grad_first, grads, weight, out):
    out[...] = (grad_first[...] + nt(grads[...], weight[...])).astype(bf16)


def place_ffn(pos, mine, sibling, gd, gu, go, g2, s2, bd, bu, g1, s1, bo, small):
    tall, half, quarter = gd.shape[0] // LOCAL, gu.shape[0] // 2, go.shape[0] // 4
    n = mine.shape[0] // 4 - 2 * tall
    for sib, held in ((0, mine), (1, sibling)):
        for other in range(4):
            owner = pos[4] ^ (other * 2) ^ sib
            at = other * 2 * tall
            for j in range(2):
                gd[pl.ds(al(owner * tall, 16), tall), j * COLS : (j + 1) * COLS] = held[
                    at : at + tall, :
                ].astype(f32)
                at += tall
            at = 8 * tall + (0, 2, 1, 3)[other] * n
            for j in range(2):
                first = pl.ds(al((owner // 2) * 2 * COLS + j * COLS, 128), COLS)
                gu[pl.ds(al((owner % 2) * half, 16), half), first] = held[at : at + half, :].astype(f32)
                at += half
            rows = pl.ds(al((owner // 2) * quarter, 16), quarter)
            go[rows, pl.ds(al((owner % 2) * COLS, 128), COLS)] = held[at : at + quarter, :].astype(f32)
            at += quarter
            small[owner] = held[at : at + 16, :].astype(f32)

    for i, out in ((0, g2), (1, s2), (2, bd), (7, g1), (8, s1), (9, bo)):
        out[...] = own_part(pos, vector_of(small[i % LOCAL], i), out.shape[1])
    total = jnp.zeros(bu.shape, f32)
    for zone in range(4):
        total = jnp.where(pos[0] == zone, vector_of(small[3 + zone], 3 + zone), total)
    bu[...] = total


def own_part(pos, row, size):
    total = row[:, :size]
    for zone in range(1, row.shape[1] // size):
        total = jnp.where(pos[0] == zone, row[:, zone * size : (zone + 1) * size], total)
    return total


def place_heads(pos, mine, sibling, gq, gk, gv, bq, bv, small):
    quarter = gq.shape[0] // 4
    n = mine.shape[0] // 4
    for sib, held in ((0, mine), (1, sibling)):
        for other in range(4):
            owner = pos[4] ^ (other * 2) ^ sib
            row4 = pl.ds(al((owner // 2) * quarter, 16), quarter)
            col2 = pl.ds(al((owner % 2) * COLS, 128), COLS)
            at = other * n
            for out in (gq, gk, gv):
                out[row4, col2] = held[at : at + quarter, :].astype(f32)
                at += quarter
            small[owner] = held[at : at + 16, :].astype(f32)[:8]
    for i, out in enumerate((bq, bv)):
        out[...] = own_part(pos, vector_of(small[i], i), out.shape[1])


def shards(
    tokens,
    lengths,
    cotangent,
    query_weight,
    query_bias,
    key_weight,
    value_weight,
    value_bias,
    out_weight,
    out_bias,
    norm_gain,
    norm_shift,
    up_weight,
    up_bias,
    down_weight,
    down_bias,
    final_gain,
    final_shift,
):
    groups = lax.axis_size("grp")
    pairs, seqlen, width = tokens.shape
    rows = pairs * seqlen
    depth = width // groups
    wide = up_weight.shape[1]
    inputs = tokens.reshape(rows, width)
    upstream = cotangent.reshape(rows, width)
    pos = position()
    n1 = 3 * depth // 4
    n2 = depth + depth // 4
    n3 = depth

    def cut(kernel, sizes, args, specs):
        return pl.pallas_call(
            kernel,
            grid_spec=pltpu.PrefetchScalarGridSpec(
                num_scalar_prefetch=1,
                grid=(1,),
                in_specs=specs,
                out_specs=[pl.BlockSpec((n, COLS), lambda i, at: (0, 0)) for n in sizes],
            ),
            out_shape=[shape((n, COLS), bf16) for n in sizes],
            name=kernel.__name__,
        )(pos, *args)

    square = pl.BlockSpec((depth // 4, COLS), lambda i, at: (at[4] // 2, at[4] % 2))
    tall = pl.BlockSpec((down_weight.shape[0] // LOCAL, width), lambda i, at: (at[4], 0))
    first, third = cut(
        cut_first,
        (n1, n3),
        (query_weight, key_weight, value_weight, down_weight),
        [square] * 3 + [tall],
    )
    z1 = [to_grp(first, step) for step in range(1, groups)]
    close = to_grp(third, 1)
    small = jnp.concatenate(
        after(
            [
                query_bias,
                value_bias,
                out_bias,
                norm_gain,
                norm_shift,
                down_bias,
                final_gain,
                final_shift,
                up_bias,
            ],
            first,
        )
    )
    count = small.shape[0] // COLS
    small = jnp.pad(small.reshape(count, COLS), ((0, 16 - count), (0, 0)))
    (second,) = cut(
        cut_more,
        (n2 + 16,),
        (out_weight, up_weight, small),
        [
            square,
            pl.BlockSpec((depth // 2, 2 * COLS), lambda i, at: (at[4] % 2, at[4] // 2)),
            pl.BlockSpec((16, COLS), lambda i, at: (0, 0)),
        ],
    )
    z1 = after(z1, second)

    def near(mine):
        return [mine, *(to_rep(mine, bit) for bit in (2, 4, 6))]

    def other_core(held):
        return [to_rep(part, 1) for part in held]

    mine1 = jnp.concatenate(z1, axis=0)
    from_x, from_y = to_rep(mine1, 2), to_rep(mine1, 4)
    second = after(second, z1)
    far = [to_grp(second, 2), to_grp(second, 3)]
    cut_at = (mine1.shape[0] // 2 + 47) // 48 * 48
    low, high = to_rep(from_x[:cut_at], 4), to_rep(from_y[cut_at:], 2)
    parts = [second, to_grp(after(second, (from_x, from_y)), 1), *far]
    parts[1:] = after(parts[1:], (low, high))
    mine2 = jnp.concatenate([part[:n2] for part in parts[1:]], axis=0)
    held2 = near(mine2)
    held1 = jnp.concatenate([mine1, from_x, from_y, low, high], axis=0)
    held1 = [held1, to_rep(held1, 1)]
    flat = jnp.stack([part[n2 : n2 + count].reshape(-1) for part in parts])
    by_zone = jnp.stack([flat[pos[0] ^ zone] for zone in range(groups)]).astype(f32)
    vectors = by_zone[:, : 8 * depth].reshape(groups, 8, depth).transpose(1, 0, 2).reshape(8, width)
    up_vector = by_zone[:, 8 * depth :].reshape(1, wide)
    third, close = after((third, close), mine2)
    far = [to_grp(third, 2), to_grp(third, 3)]

    row_block = 256
    blocks_of = rows // row_block
    mat = shape((rows, width), bf16)
    mat32 = shape((rows, width), f32)
    dense = 2 * rows * width * width
    by_pair = pl.BlockSpec((seqlen, width), lambda i: (i, 0))
    q, k, v, mixed, logsum, w_all = call(
        attend,
        (mat, mat, mat, mat, shape((pairs, 16, seqlen), f32), shape((width, 3 * width), bf16)),
        (pos, lengths, after(inputs, (mine2, close)), query_weight, key_weight, value_weight, vectors, *held1),
        [SMEM, SMEM, by_pair, ANY, ANY, ANY, VMEM] + [ANY] * 2,
        (by_pair,) * 4 + (pl.BlockSpec((1, 16, seqlen), lambda i: (i, 0, 0)), ANY),
        scratch=[
            pltpu.VMEM((width, 3 * width), bf16),
            pltpu.SemaphoreType.DMA((4 + 8 * (groups - 1) * 3,)),
        ],
        grid=(pairs,),
        flops=12 * dense,
        moved=12 * rows * width,
    )
    held2, far = after((held2, far), w_all)
    held2 += other_core(held2)
    (mine3,) = joined((close, *far))
    held3 = near(mine3)
    held3 += other_core(held3[:1])
    by_row = pl.BlockSpec((row_block, width), lambda i: (i, 0))
    by_wide = pl.BlockSpec((row_block, wide), lambda i: (i, 0))
    by_lane = pl.BlockSpec((row_block, 128), lambda i: (i, 0))
    act, slope, normed, inverse, wu_all, wo_all = call(
        expand,
        (
            shape((rows, wide), bf16),
            shape((rows, wide), bf16),
            mat32,
            shape((rows, 128), f32),
            shape((width, wide), bf16),
            shape((width, width), bf16),
        ),
        (pos, after(inputs, held3[0]), mixed, up_weight, out_weight, vectors, up_vector, *held2),
        [SMEM, by_row, by_row, ANY, ANY, VMEM, VMEM] + [ANY] * 8,
        (by_wide, by_wide, by_row, by_lane, ANY, ANY),
        scratch=[
            pltpu.VMEM((width, wide), bf16),
            pltpu.VMEM((width, width), bf16),
            pltpu.SemaphoreType.DMA((4 + 8 * (groups - 1) * 3,)),
        ],
        grid=(blocks_of,),
        flops=8 * dense,
        moved=18 * rows * width,
    )
    held3 = after(held3, wo_all)
    held3 += other_core(held3[1:4])

    stay = lambda i: (jnp.minimum(i, blocks_of - 1), 0)
    by_row = pl.BlockSpec((row_block, width), stay)
    by_wide = pl.BlockSpec((row_block, wide), stay)
    by_lane = pl.BlockSpec((row_block, 128), stay)
    vec = shape((8, width), f32)
    vec_out = pl.BlockSpec((8, width), lambda i: (0, 0))

    def travelling(n):
        return (shape((groups, 4, n, COLS), bf16),) * 2

    n_up = depth + depth // 4 + 16
    output, grad_first, grad_mixed, down_send, down_keep, send, keep = call(
        feed_forward,
        (mat, mat32, mat, *travelling(n3), *travelling(n_up)),
        (pos, lengths, act, slope, normed, inverse, upstream, mixed, down_weight, wu_all, wo_all, vectors)
        + tuple(held3),
        [SMEM, SMEM, ANY, by_wide, by_row, by_lane, by_row, ANY, ANY, ANY, ANY, VMEM] + [ANY] * 8,
        (by_row, by_row, by_row, ANY, ANY, ANY, ANY),
        scratch=[
            pltpu.VMEM((wide, width), bf16),
            pltpu.VMEM((rows, wide), bf16),
            pltpu.VMEM((rows, wide), bf16),
            pltpu.VMEM((rows, width), bf16),
            pltpu.VMEM((rows, width), bf16),
            pltpu.VMEM((rows, width), bf16),
            pltpu.VMEM((width, width), bf16),
            pltpu.VMEM((8, width), f32),
            pltpu.VMEM((8, width), f32),
            pltpu.VMEM((8, wide), f32),
            pltpu.VMEM((LOCAL, 16, COLS), bf16),
            pltpu.VMEM((width, wide), bf16),
            pltpu.VMEM((width, width), bf16),
            pltpu.VMEM((rows, width), bf16),
            pltpu.SemaphoreType.DMA((4 + 8 * (groups - 1) * 2,)),
            pltpu.SemaphoreType.DMA((blocks_of,)),
            pltpu.SemaphoreType.DMA((groups * 4 * 2 * 6,)),
            pltpu.SemaphoreType.DMA((3,)),
        ],
        grid=(blocks_of + 1,),
        flops=22 * dense,
        moved=50 * rows * width,
    )
    down = Reduce(pos, down_send, down_keep)
    up = Reduce(pos, after(send, down.got), keep)
    done = down.one()
    done = up.one(done)

    n_heads = n1 + 16
    grads = sums = None
    for pair in range(pairs):
        grads, sums = call(
            pair_back,
            (shape((rows, 3 * width), bf16), vec),
            (lengths, q, k, v, mixed, grad_mixed, after(logsum, done))
            + ((sums, grads) if pair else ()),
            [SMEM] + [ANY] * 5 + [VMEM] + ([VMEM, ANY] if pair else []),
            (ANY, VMEM),
            scratch=[
                pltpu.VMEM((5, seqlen, width), bf16),
                pltpu.VMEM((seqlen, 3 * width), bf16),
                pltpu.VMEM((16, seqlen), f32),
                pltpu.SemaphoreType.DMA((5,)),
                pltpu.SemaphoreType.DMA((1,)),
            ],
            flops=12 * dense // pairs,
            moved=12 * rows * width,
            aliases={8: 0} if pair else None,
            pair=pair,
        )
        if pair == 0:
            done = down.two(grads)
    done = up.two(grads)
    done = down.three(done)
    send, keep = call(
        heads_weights,
        travelling(n_heads),
        (pos, after(inputs, done), grads, sums),
        [SMEM, ANY, ANY, VMEM],
        (ANY, ANY),
        scratch=[
            pltpu.VMEM((rows, width), bf16),
            pltpu.VMEM((rows, 3 * width), bf16),
            pltpu.VMEM((width, 3 * width), bf16),
            pltpu.VMEM((LOCAL, 16, COLS), bf16),
            pltpu.SemaphoreType.DMA((4,)),
            pltpu.SemaphoreType.DMA((groups * 4 * 2 * 4,)),
        ],
        flops=3 * dense,
        moved=12 * rows * width,
    )
    heads = Reduce(pos, after(send, (up.ra, up.rb, down.arrived)), keep)
    done = up.three(down.arrived)
    done = heads.one(done)
    by_row = pl.BlockSpec((row_block, width), lambda i: (i, 0))
    grad_inputs = call(
        inputs_back,
        mat,
        (after(grad_first, done), grads, w_all),
        [by_row, pl.BlockSpec((row_block, 3 * width), lambda i: (i, 0)), VMEM],
        by_row,
        grid=(blocks_of,),
        flops=3 * dense,
        moved=16 * rows * width,
    )
    done = heads.two(grad_inputs, up.arrived)
    down_total = down.four(done)
    up_total = up.four(down_total)
    down_total, up_total = after((down_total, up_total), (heads.ra, heads.rb))
    heads.three()
    near_down, near_up = after((to_rep(down_total, 2), to_rep(up_total, 4)), heads.blocks[0])
    down_pair, up_pair = joined((down_total, near_down), (up_total, near_up))
    (both,) = joined((down_pair, to_rep(down_pair, 4), up_pair, to_rep(up_pair, 2)))
    heads.four()
    heads.around()
    both = both, to_rep(after(both, heads.arrived), 1)
    vector = shape((1, depth), f32)
    square = shape((depth, width), f32)
    gd, gu, go, g2, s2, bd, bu, g1, s1, bo = call(
        place_ffn,
        (shape((wide // groups, width), f32), shape((depth, wide), f32), square)
        + (vector,) * 3
        + (shape((1, wide // groups), f32),)
        + (vector,) * 3,
        (pos, *both),
        [SMEM, VMEM, VMEM],
        (VMEM,) * 10,
        scratch=[pltpu.VMEM((LOCAL, 16, COLS), f32)],
        moved=24 * depth * width,
    )
    heads.five(gd)
    gq, gk, gv, bq, bv = call(
        place_heads,
        (square,) * 3 + (vector,) * 2,
        (pos, *heads.both),
        [SMEM] + [VMEM] * 2,
        (VMEM,) * 5,
        scratch=[pltpu.VMEM((LOCAL, 8, COLS), f32)],
        moved=24 * depth * width,
    )
    bq, bv, bo, g1, s1, bu, bd, g2, s2 = (
        row.reshape(-1) for row in (bq, bv, bo, g1, s1, bu, bd, g2, s2)
    )
    return (
        output.reshape(pairs, seqlen, width),
        grad_inputs.reshape(pairs, seqlen, width),
        gq,
        bq,
        gk,
        gv,
        bv,
        go,
        bo,
        g1,
        s1,
        gu,
        bu,
        gd,
        bd,
        g2,
        s2,
    )


def solution(mesh):
    pairs = P(("grp", "rep"), None, None)
    matrix = P("grp", None)
    vector = P("grp")
    placed = (pairs, P(("grp", "rep")), pairs, matrix, vector, matrix, matrix, vector, matrix, vector)
    placed += (vector, vector, matrix, vector, matrix, vector, vector, vector)
    results = (pairs, pairs, matrix, vector, matrix, matrix, vector, matrix, vector, vector, vector)
    results += (matrix, vector, matrix, vector, vector, vector)
    return jax.shard_map(shards, mesh=mesh, in_specs=placed, out_specs=results, check_vma=False)
```

```python
import functools

import jax
import jax.numpy as jnp
from jax import lax
from jax.experimental import pallas as pl
from jax.experimental.pallas import tpu as pltpu
from jax.sharding import PartitionSpec as P

H = 12
HD = 64
EPSILON = 1e-06
MASKED = -1e30
DENSITY = 0.3989422804014327
ROOT_HALF = 0.7071067811865476

f32 = jnp.float32
bf16 = jnp.bfloat16
VMEM = pl.BlockSpec(memory_space=pltpu.VMEM)
SMEM = pl.BlockSpec(memory_space=pltpu.SMEM)
ANY = pl.BlockSpec(memory_space=pl.ANY)
VMEM_LIMIT = 63 * 2**20
MIDDLE_LIMIT = 36 * 2**20
SMALL_LIMIT = 20 * 2**20
COLS = 384
WEIGHT = 20
LOCAL = 8


def dot(a, b):
    return jnp.dot(a, b, preferred_element_type=f32)


def nt(a, b):
    return lax.dot_general(a, b, (((1,), (1,)), ((), ())), preferred_element_type=f32)


def tn(a, b):
    return lax.dot_general(a, b, (((0,), (0,)), ((), ())), preferred_element_type=f32)


def shape(dims, dtype):
    return jax.ShapeDtypeStruct(dims, dtype)


def al(value, by):
    return pl.multiple_of(value, by)


def call(
    kernel, outs, args, specs, out_specs, scratch=(), grid=(), flops=0, moved=0, aliases=None, near=None, limit=VMEM_LIMIT, **fixed
):
    if near is not None:
        limit = SMALL_LIMIT
        if near[0]:
            args = [
                pltpu.with_memory_space_constraint(arg, pltpu.VMEM) if spec is VMEM else arg
                for arg, spec in zip(args, specs)
            ]
        if near[1]:
            outs = jax.tree.map(lambda out: pltpu.VMEM(out.shape, out.dtype), outs)
    return pl.pallas_call(
        functools.partial(kernel, **fixed) if fixed else kernel,
        grid=grid,
        out_shape=outs,
        in_specs=specs,
        out_specs=out_specs,
        scratch_shapes=scratch,
        input_output_aliases=aliases or {},
        compiler_params=pltpu.CompilerParams(vmem_limit_bytes=limit),
        cost_estimate=pl.CostEstimate(
            flops=WEIGHT * flops, bytes_accessed=WEIGHT * moved, transcendentals=0
        ),
        name=kernel.__name__,
    )(*args)


def after(values, *events):
    return lax.optimization_barrier((values, events))[0]


def to_rep(array, bit):
    size = lax.axis_size("rep")
    return lax.ppermute(array, "rep", [(i, i ^ bit) for i in range(size)])


def to_grp(array, bit):
    size = lax.axis_size("grp")
    return lax.ppermute(array, "grp", [(i, i ^ bit) for i in range(size)])


def position():
    z = lax.axis_index("grp").astype(jnp.int32)
    p = lax.axis_index("rep").astype(jnp.int32) % LOCAL
    return jnp.stack([z, (p // 2) % 2, p // 4, p % 2, p])


class Copies:
    def __init__(self, sems):
        self.sems, self.held = sems, []

    def add(self, src, dst):
        copy = pltpu.make_async_copy(src, dst, self.sems.at[len(self.held)])
        copy.start()
        self.held.append(copy)

    def wait(self):
        for copy in self.held:
            copy.wait()


def piece_refs(kind, ref, zone, p, depth):
    if kind == "slab":
        rows = depth // LOCAL
        return [(ref.at[pl.ds(al(zone * depth + p * rows, 16), rows), :], rows)]
    if kind == "halves":
        rows, cols = depth // 4, ref.shape[1] // 2
        start = al(zone * depth + (p // 2) * rows, 16)
        return [(ref.at[pl.ds(start, rows), pl.ds(al((p % 2) * cols, 128), cols)], rows)]
    if kind == "tall":
        rows = depth // LOCAL
        start = al(zone * depth + p * rows, 16)
        return [
            (ref.at[pl.ds(start, rows), pl.ds(half * COLS, COLS)], rows) for half in range(2)
        ]
    if kind == "wide":
        rows = depth // 2
        start = al(zone * depth + (p % 2) * rows, 16)
        return [
            (
                ref.at[pl.ds(start, rows), pl.ds(al((p // 2) * 2 * COLS + half * COLS, 128), COLS)],
                rows,
            )
            for half in range(2)
        ]
    if kind == "half":
        rows = depth // 2
        start = al(zone * depth + (p % 2) * rows, 16)
        return [(ref.at[pl.ds(start, rows), pl.ds(al((p // 2) * COLS, 128), COLS)], rows)]
    rows = depth // 4
    offset = int(kind)
    start = al(zone * depth + (p // 2) * rows, 16)
    return [(ref.at[pl.ds(start, rows), pl.ds(al(offset + (p % 2) * COLS, 128), COLS)], rows)]


def own_slab(ref, zone, depth, first=0, width=None):
    width = ref.shape[1] if width is None else width
    return ref.at[pl.ds(al(zone * depth, 16), depth), pl.ds(first, width)]


def block_rows(parts):
    return sum(rows for kind, ref, depth in parts for _, rows in piece_refs(kind, ref, 0, 0, depth))


def fetch(copies, pos, parts, held, only=None):
    zone, p = pos[0], pos[4]
    groups = lax.axis_size("grp")
    side = len(held) // 2
    n = held[0].shape[0] // (groups - 1) // (4 // side)
    for sib in range(2):
        for other in range(4):
            owner = p ^ (other * 2) ^ sib
            part = held[side * sib + other % side]
            at = 0 if side == 4 else other * (groups - 1) * n
            for step in range(1, groups):
                source = zone ^ step
                skip = at + n
                for index, (kind, ref, depth) in enumerate(parts):
                    for place, rows in piece_refs(kind, ref, source, owner, depth):
                        if only in (None, index):
                            copies.add(part.at[pl.ds(at, rows), :], place)
                        at += rows
                at = skip


def emit(copies, pos, parts, send, keep, quads=range(4), base=0, zones=None):
    core = pos[3]
    zones = range(lax.axis_size("grp")) if zones is None else zones
    for held, flip in ((send, 1), (keep, 0)):
        for zone in zones:
            for q in quads:
                owner = q * 2 + (core ^ flip)
                at = base
                for kind, ref, depth in parts:
                    for place, rows in piece_refs(kind, ref, zone, owner, depth):
                        copies.add(place, held.at[zone, q, pl.ds(at, rows), :])
                        at += rows


def add_first(pos, keep, got, sa, ka, sb, kb, kept, sems):
    x, y = pos[1], pos[2]
    groups = keep.shape[0]
    half = groups // 2
    loads = Copies(sems)
    for zone in range(groups):
        loads.add(keep.at[zone], kept.at[zone])
    for zone in range(groups):
        loads.held[zone].wait()
        if zone < half:
            places = [(sa, j, j * 2 + (1 - x)) for j in range(2)] + [(ka, j, j * 2 + x) for j in range(2)]
        else:
            places = [(sb, j, (1 - y) * 2 + j) for j in range(2)] + [(kb, j, y * 2 + j) for j in range(2)]
        for ref, j, q in places:
            ref[zone % half, j] = kept[zone, q] + got[zone, q]


def add_second(pos, ka, ra, kb, rb, sa, ja, sb, jb):
    x, y = pos[1], pos[2]
    for zone in range(ka.shape[0]):
        for kept, got, send, hold, at in ((ka, ra, sa, ja, y), (kb, rb, sb, jb, x)):
            send[zone] = kept[zone, 1 - at] + got[zone, 1 - at]
            hold[zone] = kept[zone, at] + got[zone, at]


def add_third(pos, ka, ra, kb, rb, *rest):
    outs, total = rest[:-1], rest[-1]
    half = ka.shape[0]
    for zone in range(half):
        total[zone] = ka[zone] + ra[zone]
        total[half + zone] = kb[zone] + rb[zone]
    for step, out in enumerate(outs):
        out[...] = total[pos[0] ^ step]


def add_fourth(*refs):
    total = refs[0][...].astype(f32)
    for ref in refs[1:-1]:
        total = total + ref[...].astype(f32)
    refs[-1][...] = total.astype(bf16)


def over_blocks(total):
    bit = LOCAL
    while bit < lax.axis_size("rep"):
        other = to_rep(total, bit)
        total = call(add_fourth, shape(total.shape, bf16), (total, other), [VMEM] * 2, VMEM)
        bit *= 2
    return total


class Reduce:
    def __init__(self, pos, send, keep):
        self.pos, self.keep = pos, keep
        self.n = keep.shape[2]
        self.size = keep.shape[0] * 4 * self.n * COLS * 2
        self.got = to_rep(send, 1)

    def one(self, *events):
        groups = self.keep.shape[0]
        quad = shape((groups // 2, 2, self.n, COLS), bf16)
        got = after(self.got, *events)
        sa, self.ka, sb, self.kb = call(
            add_first,
            (quad,) * 4,
            (self.pos, self.keep, got),
            [SMEM, ANY, VMEM],
            (VMEM,) * 4,
            scratch=[pltpu.VMEM(self.keep.shape, bf16), pltpu.SemaphoreType.DMA((groups,))],
            moved=3 * self.size,
            near=(True, True),
        )
        self.ra, self.rb = to_rep(sa, 2), to_rep(sb, 4)
        return self.ka

    def two(self, *events, near=None):
        pair = shape((self.ka.shape[0], self.n, COLS), bf16)
        ra, rb = after((self.ra, self.rb), *events)
        sa, self.ja, sb, self.jb = call(
            add_second,
            (pair,) * 4,
            (self.pos, self.ka, ra, self.kb, rb),
            [SMEM] + [VMEM] * 4,
            (VMEM,) * 4,
            moved=3 * self.size // 2,
            near=near,
        )
        self.ra, self.rb = to_rep(sa, 4), to_rep(sb, 2)
        return self.ja

    def three(self, *events, near=None):
        groups = self.keep.shape[0]
        ra, rb = after((self.ra, self.rb), *events)
        self.blocks = call(
            add_third,
            (shape((self.n, COLS), bf16),) * groups,
            (self.pos, self.ja, ra, self.jb, rb),
            [SMEM] + [VMEM] * 4,
            (VMEM,) * groups,
            scratch=[pltpu.VMEM((groups, self.n, COLS), bf16)],
            moved=3 * self.size // 4,
            near=near,
        )
        self.arrived = [to_grp(self.blocks[step], step) for step in range(1, groups)]
        return self.blocks[0]

    def four(self, *events, near=None):
        arrived = after(self.arrived, *events)
        total = call(
            add_fourth,
            shape((self.n, COLS), bf16),
            (self.blocks[0], *arrived),
            [VMEM] * (1 + len(arrived)),
            VMEM,
            moved=self.size // 3,
            near=near,
        )
        self.total = over_blocks(total)
        return self.total

    def around(self):
        self.near = [to_rep(self.total, bit) for bit in (2, 4, 6)]

    def five(self, *events):
        near = after(self.near, *events)
        held = jnp.concatenate([self.total, *near], axis=0)
        self.both = held, to_rep(held, 1)
        return held


def cut_first(pos, wq, wk, wv, wd, first, third):
    for m, ref in enumerate((wq, wk, wv)):
        first[:, m * COLS : (m + 1) * COLS] = ref[...]
    third[...] = wd[...]


def cut_more(pos, wo, wu, small, second):
    half, quarter = wu.shape[0], wo.shape[0]
    for j in range(2):
        second[j * half : (j + 1) * half, :] = wu[:, j * COLS : (j + 1) * COLS]
    second[2 * half : 2 * half + quarter, :] = wo[...]
    second[2 * half + quarter :, :] = small[...]


def join(*refs, counts):
    first = 0
    for count, out in zip(counts, refs[-len(counts) :]):
        at = 0
        for ref in refs[first : first + count]:
            out[at : at + ref.shape[0], :] = ref[...]
            at += ref.shape[0]
        first += count


def joined(*lists, near=None):
    blocks = [block for one in lists for block in one]
    return call(
        join,
        tuple(shape((sum(block.shape[0] for block in one), one[0].shape[1]), bf16) for one in lists),
        blocks,
        [VMEM] * len(blocks),
        (VMEM,) * len(lists),
        moved=sum(block.shape[0] for block in blocks) * COLS * 4,
        counts=tuple(len(one) for one in lists),
        near=near,
    )


def layer_norm(values):
    centred = values - jnp.mean(values, axis=-1, keepdims=True)
    spread_of = jnp.mean(centred * centred, axis=-1, keepdims=True)
    inverse = lax.rsqrt(spread_of + EPSILON)
    return centred * inverse, inverse


def norm_back(upstream, normed, inverse, gain):
    scaled = upstream * gain
    return inverse * (
        scaled
        - jnp.mean(scaled, axis=-1, keepdims=True)
        - normed * jnp.mean(scaled * normed, axis=-1, keepdims=True)
    )


def attend_heads(lengths, x, vectors, weight, q_out, k_out, v_out, mixed, logsum, pair):
    width = x.shape[1]
    rows = x[...]
    scaling = HD ** (-0.5)
    for half in range(2):
        c = slice(half * COLS, (half + 1) * COLS)
        part = dot(rows, weight[:, half * 3 * COLS : (half + 1) * 3 * COLS])
        q_out[:, c] = (
            (part[:, :COLS] + vectors[0:1, c]).astype(bf16).astype(f32) * scaling
        ).astype(bf16)
        k_out[:, c] = part[:, COLS : 2 * COLS].astype(bf16)
        v_out[:, c] = (part[:, 2 * COLS :] + vectors[1:2, c]).astype(bf16)
    slots = rows.shape[0]
    lane = lax.broadcasted_iota(jnp.int32, (slots, 128), 1)
    low = lane < HD
    slot = lax.broadcasted_iota(jnp.int32, (1, slots), 1)
    bias = jnp.where(slot < lengths[pair], 0.0, MASKED).astype(f32)

    def heads(h, sums):
        s = pl.ds(al(h * 128, 128), 128)
        q1, k1, v1 = q_out[:, s], k_out[:, s], v_out[:, s]
        results, peaks = [], []
        for e in range(2):
            mask = low if e == 0 else ~low
            scores = nt(jnp.where(mask, q1, 0).astype(bf16), k1) + bias
            peak = jnp.max(scores, axis=1, keepdims=True)
            expo = jnp.exp(scores - peak).astype(bf16)
            results.append(dot(expo, jnp.where(mask, v1, 1).astype(bf16)))
            peaks.append(peak)
        total = pltpu.roll(jnp.where(low, results[1], results[0]), HD, 1)
        mixed[:, s] = (jnp.where(low, results[0], results[1]) / total).astype(bf16)
        sums = jnp.where(lane % HD == h, jnp.where(low, peaks[0], peaks[1]) + jnp.log(total), sums)
        return sums

    sums = lax.fori_loop(0, H // 2, heads, jnp.zeros((slots, 128), f32), unroll=True)
    turned = sums.T
    logsum[0, :8] = turned[:8]
    logsum[0, 8:] = turned[HD : HD + 8]


def attend(pos, lengths, x, wq, wk, wv, vectors, *rest):
    held, (q_out, k_out, v_out, mixed, logsum, w_out, weight, sems) = rest[:2], rest[2:]
    depth, width = wq.shape
    pair = pl.program_id(0)
    places = [
        (weight.at[:, pl.ds((half * 3 + m) * COLS, COLS)], pl.ds(m * width + half * COLS, COLS))
        for half in range(2)
        for m in range(3)
    ]
    writes = [
        pltpu.make_async_copy(place, w_out.at[:, c], sems.at[sems.shape[0] - 1 - i])
        for i, (place, c) in enumerate(places)
    ]

    @pl.when(pair == 0)
    def _():
        copies = Copies(sems)
        for half in range(2):
            for m, ref in enumerate((wq, wk, wv)):
                copies.add(
                    ref.at[:, pl.ds(half * COLS, COLS)],
                    own_slab(weight, pos[0], depth, (half * 3 + m) * COLS, COLS),
                )
        fetch(copies, pos, [("halves", weight, depth)], held)
        copies.wait()
        for write in writes:
            write.start()

    attend_heads(lengths, x, vectors, weight, q_out, k_out, v_out, mixed, logsum, pair)

    @pl.when(pair == pl.num_programs(0) - 1)
    def _():
        for write in writes:
            write.wait()


def expand(pos, x, mixed, wu, wo, vectors, up_bias, *rest):
    held, rest = rest[:8], rest[8:]
    act, slope, normed, inverse, wu_out, wo_out, up, out_w, xs, mixes, acts, slopes, normals, scales = rest[:14]
    row_sems, near_sems, far_sems, store_sems = rest[14:]
    depth = wo.shape[0]
    count = row_sems.shape[0]
    rows = xs.shape[0] // count
    chunk = 768
    loads = [Copies(row_sems.at[i]) for i in range(count)]
    near, far, stores = Copies(near_sems), Copies(far_sems), Copies(store_sems)
    parts = [("wide", up, depth), ("0", out_w, depth)]
    for i, load in enumerate(loads):
        s = pl.ds(i * rows, rows)
        load.add(mixed.at[s, :], mixes.at[s, :])
        load.add(x.at[s, :], xs.at[s, :])
        if i == 0:
            near.add(wo, own_slab(out_w, pos[0], depth))
            fetch(near, pos, parts, held, 1)
    far.add(wu, own_slab(up, pos[0], depth))
    fetch(far, pos, parts, held, 0)
    near.wait()
    hidden = []
    for i, load in enumerate(loads):
        load.wait()
        s = pl.ds(i * rows, rows)
        first = xs[s, :].astype(f32) + dot(mixes[s, :], out_w[...]) + vectors[2:3, :]
        normal, scale = layer_norm(first)
        normals[s, :] = normal
        scales[s, :] = jnp.broadcast_to(scale, (rows, scales.shape[1]))
        stores.add(normals.at[s, :], normed.at[s, :])
        stores.add(scales.at[s, :], inverse.at[s, :])
        hidden.append((normal * vectors[3:4, :] + vectors[4:5, :]).astype(bf16))
    far.wait()
    stores.add(up, wu_out)
    stores.add(out_w, wo_out)
    for j in range(up.shape[1] // chunk):
        c = slice(j * chunk, (j + 1) * chunk)
        for i in range(count):
            s = pl.ds(i * rows, rows)
            u = dot(hidden[i], up[:, c]) + up_bias[:, c]
            cdf, pdf = gaussian(u)
            acts[s, c] = (u * cdf).astype(bf16)
            slopes[s, c] = (cdf + u * pdf).astype(bf16)
            stores.add(acts.at[s, c], act.at[s, c])
            stores.add(slopes.at[s, c], slope.at[s, c])
    stores.wait()


def gaussian(u):
    return 0.5 + 0.5 * lax.erf(u * ROOT_HALF), jnp.exp(-0.5 * u * u) * DENSITY


def feed_forward(pos, lengths, act, slope, normed, inverse, cotangent, mixed, wd, wu, wo, vectors, *rest):
    held, rest = rest[:8], rest[8:]
    output, grad_first, grad_mixed, down_send, down_keep, send, keep = rest[:7]
    down, up, out_w, acts, slopes, normals, scales, cots, mixes, hiddens, lows, lows_first = rest[7:19]
    mixed_grads, grad_out, blocks, sems, block_sems, late_sems, store_sems, out_sems = rest[19:]
    total, width = mixes.shape
    wide = acts.shape[1]
    depth = wd.shape[0]
    count = block_sems.shape[1]
    rows = total // count
    chunk = 768

    def at(i):
        return pl.ds(i * rows, rows)

    def load(k, i):
        source, held_at = ((act, acts), (normed, normals), (cotangent, cots), (slope, slopes))[k]
        return pltpu.make_async_copy(source.at[at(i), :], held_at.at[at(i), :], block_sems.at[k, i])

    weights = Copies(sems)
    weights.add(wd, own_slab(down, pos[0], depth))
    fetch(weights, pos, [("slab", down, depth)], held)
    for k in range(4):
        load(k, 0).start()
    late = Copies(late_sems)
    weights.wait()
    stores = Copies(store_sems)
    sums = [jnp.zeros((1, width), f32)] * 6
    up_sums = [jnp.zeros((1, chunk), f32)] * (wide // chunk)
    first_gain, gain = vectors[3:4, :], vectors[6:7, :]

    def column_sums(values):
        return jnp.sum(values, axis=0, keepdims=True)

    def begin(i):
        for k in range(4):
            load(k, i).wait()
        if i == 0:
            for source, place in ((wu, up), (wo, out_w), (inverse, scales)):
                late.add(source, place)
        if i + 1 < count:
            for k in range(4):
                load(k, i + 1).start()
        else:
            late.add(mixed, mixes)
        return dot(acts[at(i), :], down[...])

    def middle(i, product):
        s = at(i)
        per_pair = count // lengths.shape[0]
        slot = lax.broadcasted_iota(jnp.int32, (rows, 1), 0) + (i % per_pair) * rows
        mask = (slot < lengths[i // per_pair]).astype(f32)
        hidden = normals[s, :] * first_gain + vectors[4:5, :]
        hiddens[s, :] = hidden.astype(bf16)
        normal, scale = layer_norm(hidden + product + vectors[5:6, :])
        upstream = cots[s, :].astype(f32) * mask
        cots[s, :] = ((normal * gain + vectors[7:8, :]) * mask).astype(bf16)
        stores.add(cots.at[s, :], output.at[s, :])
        grad_second = norm_back(upstream, normal, scale, gain)
        low = grad_second.astype(bf16)
        lows[s, :] = low
        for k, value in enumerate((upstream * normal, upstream, low.astype(f32))):
            sums[k] = sums[k] + column_sums(value)
        return grad_second, low

    def grow(i, low):
        s = at(i)
        for j in range(wide // chunk):
            c = slice(j * chunk, (j + 1) * chunk)
            grown = (nt(low, down[c, :]) * slopes[s, c].astype(f32)).astype(bf16)
            slopes[s, c] = grown
            up_sums[j] = up_sums[j] + column_sums(grown.astype(f32))

    def shrink(i):
        if i == 0:
            for copy in late.held[:3]:
                copy.wait()
        return nt(slopes[at(i), :], up[...])

    def end(i, grad_second, product):
        s = at(i)
        normal = normals[s, :]
        upstream = grad_second + product
        result = norm_back(upstream, normal, scales[s, 0:1], first_gain)
        normals[s, :] = result
        stores.add(normals.at[s, :], grad_first.at[s, :])
        low = result.astype(bf16)
        lows_first[s, :] = low
        mixed_grads[s, :] = nt(low, out_w[...]).astype(bf16)
        stores.add(mixed_grads.at[s, :], grad_mixed.at[s, :])
        for k, value in enumerate((upstream * normal, upstream, low.astype(f32))):
            sums[3 + k] = sums[3 + k] + column_sums(value)

    pieces = Copies(out_sems)

    def down_zone(zone):
        s = slice(zone * depth, (zone + 1) * depth)
        down[s, :] = tn(acts[:, s], lows[...]).astype(bf16)
        emit(pieces, pos, [("tall", down, depth)], down_send, down_keep, zones=(zone,))

    for a in range(0, count, 2):
        b = a + 1
        product_a = begin(a)
        second_a, low_a = middle(a, product_a)
        product_b = begin(b)
        grow(a, low_a)
        second_b, low_b = middle(b, product_b)
        grow(b, low_b)
        product_a = shrink(a)
        product_b = shrink(b)
        end(a, second_a, product_a)
        if b == count - 1:
            down_zone(0)
        end(b, second_b, product_b)
    for zone in range(1, wide // depth):
        down_zone(zone)
    up_depth = width // lax.axis_size("grp")
    grad_up = acts.at[pl.ds(0, width), :]
    for j in range(wide // chunk):
        c = slice(j * chunk, (j + 1) * chunk)
        acts[:width, c] = tn(hiddens[...], slopes[:, c]).astype(bf16)
        emit(pieces, pos, [("wide", grad_up, up_depth)], send, keep, (j,))
    late.held[3].wait()
    grad_out[...] = tn(mixes[...], lows_first[...]).astype(bf16)
    emit(pieces, pos, [("0", grad_out, up_depth)], send, keep, base=up_depth)
    vector_blocks(blocks, sums[:3] + up_sums + sums[3:])
    emit_vectors(pieces, pos, blocks, up_depth + up_depth // 4, send, keep)
    stores.wait()
    pieces.wait()


def vector_blocks(blocks, rows):
    blocks[...] = jnp.zeros_like(blocks)
    for p in range(min(LOCAL, len(rows))):
        here = rows[p::LOCAL]
        half = here[0].shape[1] // 2
        stacked = [part for row in here for part in (row[:, :half], row[:, half:])]
        stacked.append(jnp.zeros((16 - 2 * len(here), half), f32))
        blocks[p] = jnp.concatenate(stacked, axis=0).astype(bf16)


def vector_of(block, i):
    at = 2 * (i // LOCAL)
    return jnp.concatenate([block[at : at + 1, :], block[at + 1 : at + 2, :]], axis=1)


def emit_vectors(copies, pos, blocks, base, send, keep):
    for held, flip in ((send, 1), (keep, 0)):
        for zone in range(send.shape[0]):
            for q in range(4):
                owner = q * 2 + (pos[3] ^ flip)
                copies.add(blocks.at[owner], held.at[zone, q, pl.ds(base, 16), :])


def pair_back(lengths, q, k, v, mixed, grad_mixed, logsum, *rest, pair):
    if pair:
        old_sums, rest = rest[0], rest[2:]
    grads, sums, rows_of, held, deltas, in_sems, out_sem = rest
    slots, width = held.shape[0], q.shape[1]
    here = pl.ds(pair * slots, slots)
    spans = 2
    span = width // spans
    loads = [Copies(in_sems.at[i]) for i in range(spans)]
    for part, load in enumerate(loads):
        c = pl.ds(part * span, span)
        for i, ref in enumerate((mixed, grad_mixed, q, k, v)):
            load.add(ref.at[here, c], rows_of.at[i, :, c])
    stores = Copies(out_sem)
    sums[...] = old_sums[...] if pair else jnp.zeros_like(sums)
    low = lax.broadcasted_iota(jnp.int32, (slots, 128), 1) < HD
    slot = lax.broadcasted_iota(jnp.int32, (slots, 1), 0)
    scaling = HD ** (-0.5)
    bias = jnp.where(slot < lengths[pair], 0.0, MASKED).astype(f32)

    def heads(h, carry):
        s = pl.ds(al(h * 128, 128), 128)
        g1, q1, k1, v1 = (rows_of[i, :, s] for i in (1, 2, 3, 4))
        probs, scores_back, qs, gs, ks = [], [], [], [], []
        for e in range(2):
            mask = low if e == 0 else ~low
            qm = jnp.where(mask, q1, 0).astype(bf16)
            gm = jnp.where(mask, g1, 0).astype(bf16)
            prob = jnp.exp(nt(k1, qm) + bias - logsum[pair, pl.ds(h + 8 * e, 1), :])
            back = prob * (nt(v1, gm) - deltas[pl.ds(h * 2 + e, 1), :])
            probs.append(prob.astype(bf16))
            scores_back.append(back.astype(bf16))
            qs.append(qm)
            gs.append(gm)
            ks.append(jnp.where(mask, k1, 0).astype(bf16))
        grad_v = dot(jnp.concatenate(probs, 1), jnp.concatenate(gs, 0))
        grad_k = dot(jnp.concatenate(scores_back, 1), jnp.concatenate(qs, 0))
        grad_q = tn(jnp.concatenate(scores_back, 0), jnp.concatenate(ks, 0)) * scaling
        for m, value in enumerate((grad_q, grad_k, grad_v)):
            value = value.astype(bf16)
            held[:, pl.ds(al(m * width + h * 128, 128), 128)] = value
            if m != 1:
                sums[m : m + 1, s] += jnp.sum(value.astype(f32), axis=0, keepdims=True)
        return carry

    for part, load in enumerate(loads):
        load.wait()
        c = pl.ds(part * span, span)
        select = (
            lax.broadcasted_iota(jnp.int32, (16, span), 1) // HD + part * span // HD
            == lax.broadcasted_iota(jnp.int32, (16, span), 0)
        ).astype(bf16)
        product = rows_of[0, :, c].astype(f32) * rows_of[1, :, c].astype(f32)
        high = product.astype(bf16)
        rest_of = (product - high.astype(f32)).astype(bf16)
        delta = nt(select, high) + nt(select, rest_of)
        deltas[...] = delta if part == 0 else deltas[...] + delta
        lax.fori_loop(part * span // 128, (part + 1) * span // 128, heads, 0, unroll=True)
        for m in range(3):
            here_m = pl.ds(m * width + part * span, span)
            stores.add(held.at[:, here_m], grads.at[here, here_m])
    stores.wait()


def heads_weights(pos, x, grads, sums, send, keep, xs, held, weight_grads, blocks, sems, out_sems):
    width = xs.shape[1]
    depth = width // lax.axis_size("grp")
    copies = Copies(sems)

    def add(m):
        c = pl.ds(m * width, width)
        copies.add(grads.at[:, c], held.at[:, c])

    copies.add(x, xs)
    add(0)
    copies.wait()
    add(1)
    stores = Copies(out_sems)
    vector_blocks(blocks, [sums[m : m + 1, :] for m in (0, 2)])
    emit_vectors(stores, pos, blocks, 3 * depth // 4, send, keep)
    for m in range(3):
        c = slice(m * width, (m + 1) * width)
        if m:
            copies.held[1 + m].wait()
        if m == 1:
            add(2)
        weight_grads[:, c] = tn(xs[...], held[:, c]).astype(bf16)
        emit(stores, pos, [(str(m * width), weight_grads, depth)], send, keep, base=m * depth // 4)
    stores.wait()


def inputs_back(grad_first, grads, weight, out):
    out[...] = (grad_first[...] + nt(grads[...], weight[...])).astype(bf16)


def place_ffn(pos, mine, sibling, gd, gu, go, g2, s2, bd, bu, g1, s1, bo, small):
    tall, half, quarter = gd.shape[0] // LOCAL, gu.shape[0] // 2, go.shape[0] // 4
    n = mine.shape[0] // 4 - 2 * tall
    for sib, held in ((0, mine), (1, sibling)):
        for other in range(4):
            owner = pos[4] ^ (other * 2) ^ sib
            at = other * 2 * tall
            for j in range(2):
                gd[pl.ds(al(owner * tall, 16), tall), j * COLS : (j + 1) * COLS] = held[
                    at : at + tall, :
                ].astype(f32)
                at += tall
            at = 8 * tall + (0, 2, 1, 3)[other] * n
            for j in range(2):
                first = pl.ds(al((owner // 2) * 2 * COLS + j * COLS, 128), COLS)
                gu[pl.ds(al((owner % 2) * half, 16), half), first] = held[at : at + half, :].astype(f32)
                at += half
            rows = pl.ds(al((owner // 2) * quarter, 16), quarter)
            go[rows, pl.ds(al((owner % 2) * COLS, 128), COLS)] = held[at : at + quarter, :].astype(f32)
            at += quarter
            small[owner] = held[at : at + 16, :].astype(f32)

    for i, out in ((0, g2), (1, s2), (2, bd), (7, g1), (8, s1), (9, bo)):
        out[...] = own_part(pos, vector_of(small[i % LOCAL], i), out.shape[1])
    total = jnp.zeros(bu.shape, f32)
    for zone in range(4):
        total = jnp.where(pos[0] == zone, vector_of(small[3 + zone], 3 + zone), total)
    bu[...] = total


def own_part(pos, row, size):
    total = row[:, :size]
    for zone in range(1, row.shape[1] // size):
        total = jnp.where(pos[0] == zone, row[:, zone * size : (zone + 1) * size], total)
    return total


def place_heads(pos, mine, sibling, gq, gk, gv, bq, bv, small):
    quarter = gq.shape[0] // 4
    n = mine.shape[0] // 4
    for sib, held in ((0, mine), (1, sibling)):
        for other in range(4):
            owner = pos[4] ^ (other * 2) ^ sib
            row4 = pl.ds(al((owner // 2) * quarter, 16), quarter)
            col2 = pl.ds(al((owner % 2) * COLS, 128), COLS)
            at = other * n
            for out in (gq, gk, gv):
                out[row4, col2] = held[at : at + quarter, :].astype(f32)
                at += quarter
            small[owner] = held[at : at + 16, :].astype(f32)[:8]
    for i, out in enumerate((bq, bv)):
        out[...] = own_part(pos, vector_of(small[i], i), out.shape[1])


def shards(
    tokens,
    lengths,
    cotangent,
    query_weight,
    query_bias,
    key_weight,
    value_weight,
    value_bias,
    out_weight,
    out_bias,
    norm_gain,
    norm_shift,
    up_weight,
    up_bias,
    down_weight,
    down_bias,
    final_gain,
    final_shift,
):
    groups = lax.axis_size("grp")
    pairs, seqlen, width = tokens.shape
    rows = pairs * seqlen
    depth = width // groups
    wide = up_weight.shape[1]
    inputs = tokens.reshape(rows, width)
    upstream = cotangent.reshape(rows, width)
    pos = position()
    n1 = 3 * depth // 4
    n2 = depth + depth // 4
    n3 = depth

    def cut(kernel, sizes, args, specs):
        return pl.pallas_call(
            kernel,
            grid_spec=pltpu.PrefetchScalarGridSpec(
                num_scalar_prefetch=1,
                grid=(1,),
                in_specs=specs,
                out_specs=[pl.BlockSpec(size, lambda i, at: (0, 0)) for size in sizes],
            ),
            out_shape=[shape(size, bf16) for size in sizes],
            name=kernel.__name__,
        )(pos, *args)

    square = pl.BlockSpec((depth // 4, COLS), lambda i, at: (at[4] // 2, at[4] % 2))
    tall = pl.BlockSpec((down_weight.shape[0] // LOCAL, width), lambda i, at: (at[4], 0))
    first, third = cut(
        cut_first,
        ((depth // 4, 3 * COLS), (n3 // 2, width)),
        (query_weight, key_weight, value_weight, down_weight),
        [square] * 3 + [tall],
    )
    z1 = [to_grp(first, step) for step in range(1, groups)]
    close = to_grp(third, 1)
    small = jnp.concatenate(
        after(
            [
                query_bias,
                value_bias,
                out_bias,
                norm_gain,
                norm_shift,
                down_bias,
                final_gain,
                final_shift,
                up_bias,
            ],
            first,
        )
    )
    count = small.shape[0] // COLS
    small = jnp.pad(small.reshape(count, COLS), ((0, 16 - count), (0, 0)))
    (second,) = cut(
        cut_more,
        ((n2 + 16, COLS),),
        (out_weight, up_weight, small),
        [
            square,
            pl.BlockSpec((depth // 2, 2 * COLS), lambda i, at: (at[4] % 2, at[4] // 2)),
            pl.BlockSpec((16, COLS), lambda i, at: (0, 0)),
        ],
    )
    z1 = after(z1, second)

    def near(mine):
        return [mine, *(to_rep(mine, bit) for bit in (2, 4, 6))]

    def other_core(held):
        return [to_rep(part, 1) for part in held]

    mine1 = jnp.concatenate(z1, axis=0)
    from_x, from_y = to_rep(mine1, 2), to_rep(mine1, 4)
    second = after(second, z1)
    far = [to_grp(second, 2), to_grp(second, 3)]
    cut_at = (mine1.shape[0] // 2 + 15) // 16 * 16
    low, high = to_rep(from_x[:cut_at], 4), to_rep(from_y[cut_at:], 2)
    parts = [second, to_grp(after(second, (from_x, from_y)), 1), *far]
    parts[1:] = after(parts[1:], (low, high))
    mine2 = jnp.concatenate([part[:n2] for part in parts[1:]], axis=0)
    held2 = near(mine2)
    held1 = jnp.concatenate([mine1, from_x, from_y, low, high], axis=0)
    held1 = [held1, to_rep(held1, 1)]
    flat = jnp.stack([part[n2 : n2 + count].reshape(-1) for part in parts])
    by_zone = jnp.stack([flat[pos[0] ^ zone] for zone in range(groups)]).astype(f32)
    vectors = by_zone[:, : 8 * depth].reshape(groups, 8, depth).transpose(1, 0, 2).reshape(8, width)
    up_vector = by_zone[:, 8 * depth :].reshape(1, wide)
    third, close = after((third, close), mine2)
    far = [to_grp(third, 2), to_grp(third, 3)]

    mat = shape((rows, width), bf16)
    mat32 = shape((rows, width), f32)
    dense = 2 * rows * width * width
    by_pair = pl.BlockSpec((seqlen, width), lambda i: (i, 0))
    q, k, v, mixed, logsum, w_all = call(
        attend,
        (mat, mat, mat, mat, shape((pairs, 16, seqlen), f32), shape((width, 3 * width), bf16)),
        (pos, lengths, after(inputs, (mine2, close)), query_weight, key_weight, value_weight, vectors, *held1),
        [SMEM, SMEM, by_pair, ANY, ANY, ANY, VMEM] + [ANY] * 2,
        (by_pair,) * 4 + (pl.BlockSpec((1, 16, seqlen), lambda i: (i, 0, 0)), ANY),
        scratch=[
            pltpu.VMEM((width, 3 * width), bf16),
            pltpu.SemaphoreType.DMA((12 + 8 * (groups - 1),)),
        ],
        grid=(pairs,),
        flops=12 * dense,
        moved=12 * rows * width,
    )
    held2, far = after((held2, far), w_all)
    held2 += other_core(held2)
    (mine3,) = joined((close, *far))
    held3 = near(mine3)
    held3 += other_core(held3[:1])
    halves = rows // 512
    act, slope, normed, inverse, wu_all, wo_all = call(
        expand,
        (
            shape((rows, wide), bf16),
            shape((rows, wide), bf16),
            mat32,
            shape((rows, 128), f32),
            shape((width, wide), bf16),
            shape((width, width), bf16),
        ),
        (pos, after(inputs, held3[0]), mixed, up_weight, out_weight, vectors, up_vector, *held2),
        [SMEM, ANY, ANY, ANY, ANY, VMEM, VMEM] + [ANY] * 8,
        (ANY,) * 6,
        scratch=[
            pltpu.VMEM((width, wide), bf16),
            pltpu.VMEM((width, width), bf16),
            pltpu.VMEM((rows, width), bf16),
            pltpu.VMEM((rows, width), bf16),
            pltpu.VMEM((rows, wide), bf16),
            pltpu.VMEM((rows, wide), bf16),
            pltpu.VMEM((rows, width), f32),
            pltpu.VMEM((rows, 128), f32),
            pltpu.SemaphoreType.DMA((halves, 2)),
            pltpu.SemaphoreType.DMA((1 + 8 * (groups - 1),)),
            pltpu.SemaphoreType.DMA((1 + 8 * (groups - 1) * 2,)),
            pltpu.SemaphoreType.DMA((2 + 2 * halves + 2 * halves * wide // 768,)),
        ],
        flops=8 * dense,
        moved=18 * rows * width,
    )
    held3 = after(held3, wo_all)
    held3 += other_core(held3[1:4])

    vec = shape((8, width), f32)

    def travelling(n):
        return (shape((groups, 4, n, COLS), bf16),) * 2

    n_up = depth + depth // 4 + 16
    output, grad_first, grad_mixed, down_send, down_keep, send, keep = call(
        feed_forward,
        (mat, mat32, mat, *travelling(n3), *travelling(n_up)),
        (pos, lengths, act, slope, normed, inverse, upstream, mixed, down_weight, wu_all, wo_all, vectors)
        + tuple(held3),
        [SMEM, SMEM] + [ANY] * 9 + [VMEM] + [ANY] * 8,
        (ANY,) * 7,
        scratch=[
            pltpu.VMEM((wide, width), bf16),
            pltpu.VMEM((width, wide), bf16),
            pltpu.VMEM((width, width), bf16),
            pltpu.VMEM((rows, wide), bf16),
            pltpu.VMEM((rows, wide), bf16),
            pltpu.VMEM((rows, width), f32),
            pltpu.VMEM((rows, 128), f32),
            pltpu.VMEM((rows, width), bf16),
            pltpu.VMEM((rows, width), bf16),
            pltpu.VMEM((rows, width), bf16),
            pltpu.VMEM((rows, width), bf16),
            pltpu.VMEM((rows, width), bf16),
            pltpu.VMEM((rows, width), bf16),
            pltpu.VMEM((width, width), bf16),
            pltpu.VMEM((LOCAL, 16, COLS), bf16),
            pltpu.SemaphoreType.DMA((1 + 8 * (groups - 1),)),
            pltpu.SemaphoreType.DMA((4, halves)),
            pltpu.SemaphoreType.DMA((4,)),
            pltpu.SemaphoreType.DMA((3 * halves,)),
            pltpu.SemaphoreType.DMA((groups * 4 * 2 * 6,)),
        ],
        flops=22 * dense,
        moved=50 * rows * width,
    )
    down = Reduce(pos, down_send, down_keep)
    up = Reduce(pos, after(send, down.got), keep)
    done = down.one()
    done = up.one(done)

    n_heads = n1 + 16
    grads = sums = None
    for pair in range(pairs):
        grads, sums = call(
            pair_back,
            (shape((rows, 3 * width), bf16), vec),
            (lengths, q, k, v, mixed, grad_mixed, after(logsum, done))
            + ((sums, grads) if pair else ()),
            [SMEM] + [ANY] * 5 + [VMEM] + ([VMEM, ANY] if pair else []),
            (ANY, VMEM),
            scratch=[
                pltpu.VMEM((5, seqlen, width), bf16),
                pltpu.VMEM((seqlen, 3 * width), bf16),
                pltpu.VMEM((16, seqlen), f32),
                pltpu.SemaphoreType.DMA((2, 5)),
                pltpu.SemaphoreType.DMA((6,)),
            ],
            flops=12 * dense // pairs,
            moved=12 * rows * width,
            aliases={8: 0} if pair else None,
            limit=MIDDLE_LIMIT,
            pair=pair,
        )
        if pair == 0:
            done = down.two(grads, near=(True, True))
    done = up.two(grads, near=(True, True))
    done = down.three(done, near=(True, True))
    send, keep = call(
        heads_weights,
        travelling(n_heads),
        (pos, after(inputs, done), grads, sums),
        [SMEM, ANY, ANY, VMEM],
        (ANY, ANY),
        scratch=[
            pltpu.VMEM((rows, width), bf16),
            pltpu.VMEM((rows, 3 * width), bf16),
            pltpu.VMEM((width, 3 * width), bf16),
            pltpu.VMEM((LOCAL, 16, COLS), bf16),
            pltpu.SemaphoreType.DMA((4,)),
            pltpu.SemaphoreType.DMA((groups * 4 * 2 * 4,)),
        ],
        flops=3 * dense,
        moved=12 * rows * width,
        limit=MIDDLE_LIMIT,
    )
    heads = Reduce(pos, after(send, (up.ra, up.rb, down.arrived)), keep)
    done = up.three(down.arrived, near=(True, True))
    done = heads.one(done)
    row_block = rows // halves
    by_row = pl.BlockSpec((row_block, width), lambda i: (i, 0))
    grad_inputs = call(
        inputs_back,
        mat,
        (after(grad_first, done), grads, w_all),
        [by_row, pl.BlockSpec((row_block, 3 * width), lambda i: (i, 0)), VMEM],
        by_row,
        grid=(halves,),
        flops=3 * dense,
        moved=16 * rows * width,
        limit=MIDDLE_LIMIT,
    )
    done = heads.two(grad_inputs, up.arrived, near=(True, True))
    down_total = down.four(done, near=(True, True))
    up_total = up.four(down_total, near=(True, True))
    down_total, up_total = after((down_total, up_total), (heads.ra, heads.rb))
    heads.three(near=(True, True))
    near_down, near_up = after((to_rep(down_total, 2), to_rep(up_total, 4)), heads.blocks[0])
    down_pair, up_pair = joined((down_total, near_down), (up_total, near_up), near=(True, True))
    (both,) = joined(
        (down_pair, to_rep(down_pair, 4), up_pair, to_rep(up_pair, 2)), near=(True, True)
    )
    heads.four(near=(True, True))
    heads.around()
    both = both, to_rep(after(both, heads.arrived), 1)
    vector = shape((1, depth), f32)
    square = shape((depth, width), f32)
    gd, gu, go, g2, s2, bd, bu, g1, s1, bo = call(
        place_ffn,
        (shape((wide // groups, width), f32), shape((depth, wide), f32), square)
        + (vector,) * 3
        + (shape((1, wide // groups), f32),)
        + (vector,) * 3,
        (pos, *both),
        [SMEM, VMEM, VMEM],
        (VMEM,) * 10,
        scratch=[pltpu.VMEM((LOCAL, 16, COLS), f32)],
        moved=24 * depth * width,
        near=(True, False),
    )
    heads.five(gd)
    gq, gk, gv, bq, bv = call(
        place_heads,
        (square,) * 3 + (vector,) * 2,
        (pos, *heads.both),
        [SMEM] + [VMEM] * 2,
        (VMEM,) * 5,
        scratch=[pltpu.VMEM((LOCAL, 8, COLS), f32)],
        moved=24 * depth * width,
        near=(True, False),
    )
    bq, bv, bo, g1, s1, bu, bd, g2, s2 = (
        row.reshape(-1) for row in (bq, bv, bo, g1, s1, bu, bd, g2, s2)
    )
    return (
        output.reshape(pairs, seqlen, width),
        grad_inputs.reshape(pairs, seqlen, width),
        gq,
        bq,
        gk,
        gv,
        bv,
        go,
        bo,
        g1,
        s1,
        gu,
        bu,
        gd,
        bd,
        g2,
        s2,
    )


def solution(mesh):
    pairs = P(("grp", "rep"), None, None)
    matrix = P("grp", None)
    vector = P("grp")
    placed = (pairs, P(("grp", "rep")), pairs, matrix, vector, matrix, matrix, vector, matrix, vector)
    placed += (vector, vector, matrix, vector, matrix, vector, vector, vector)
    results = (pairs, pairs, matrix, vector, matrix, matrix, vector, matrix, vector, vector, vector)
    results += (matrix, vector, matrix, vector, vector, vector)
    return jax.shard_map(shards, mesh=mesh, in_specs=placed, out_specs=results, check_vma=False)
```

```python
import functools

import jax
import jax.numpy as jnp
from jax import lax
from jax.experimental import pallas as pl
from jax.experimental.pallas import tpu as pltpu
from jax.sharding import PartitionSpec as P

H = 12
HD = 64
EPSILON = 1e-06
MASKED = -1e30
DENSITY = 0.3989422804014327
ROOT_HALF = 0.7071067811865476

f32 = jnp.float32
bf16 = jnp.bfloat16
VMEM = pl.BlockSpec(memory_space=pltpu.VMEM)
SMEM = pl.BlockSpec(memory_space=pltpu.SMEM)
ANY = pl.BlockSpec(memory_space=pl.ANY)
VMEM_LIMIT = 63 * 2**20
MIDDLE_LIMIT = 36 * 2**20
SMALL_LIMIT = 20 * 2**20
COLS = 384
WEIGHT = 20
LOCAL = 8


def dot(a, b):
    return jnp.dot(a, b, preferred_element_type=f32)


def nt(a, b):
    return lax.dot_general(a, b, (((1,), (1,)), ((), ())), preferred_element_type=f32)


def tn(a, b):
    return lax.dot_general(a, b, (((0,), (0,)), ((), ())), preferred_element_type=f32)


def shape(dims, dtype):
    return jax.ShapeDtypeStruct(dims, dtype)


def al(value, by):
    return pl.multiple_of(value, by)


def inside(out):
    return pltpu.VMEM(out.shape, out.dtype)


def call(
    kernel, outs, args, specs, out_specs, scratch=(), grid=(), flops=0, moved=0, aliases=None, near=None, limit=VMEM_LIMIT, **fixed
):
    if near is not None:
        limit = SMALL_LIMIT
        if near[0]:
            args = [
                pltpu.with_memory_space_constraint(arg, pltpu.VMEM) if spec is VMEM else arg
                for arg, spec in zip(args, specs)
            ]
        if near[1]:
            outs = jax.tree.map(inside, outs)
    return pl.pallas_call(
        functools.partial(kernel, **fixed) if fixed else kernel,
        grid=grid,
        out_shape=outs,
        in_specs=specs,
        out_specs=out_specs,
        scratch_shapes=scratch,
        input_output_aliases=aliases or {},
        compiler_params=pltpu.CompilerParams(vmem_limit_bytes=limit),
        cost_estimate=pl.CostEstimate(
            flops=WEIGHT * flops, bytes_accessed=WEIGHT * moved if flops else 0, transcendentals=0
        ),
        name=kernel.__name__,
    )(*args)


def after(values, *events):
    return lax.optimization_barrier((values, events))[0]


def to_rep(array, bit):
    size = lax.axis_size("rep")
    return lax.ppermute(array, "rep", [(i, i ^ bit) for i in range(size)])


def to_grp(array, bit):
    size = lax.axis_size("grp")
    return lax.ppermute(array, "grp", [(i, i ^ bit) for i in range(size)])


def position():
    z = lax.axis_index("grp").astype(jnp.int32)
    p = lax.axis_index("rep").astype(jnp.int32) % LOCAL
    return jnp.stack([z, (p // 2) % 2, p // 4, p % 2, p])


class Copies:
    def __init__(self, sems):
        self.sems, self.held = sems, []

    def add(self, src, dst):
        copy = pltpu.make_async_copy(src, dst, self.sems.at[len(self.held)])
        copy.start()
        self.held.append(copy)

    def wait(self):
        for copy in self.held:
            copy.wait()


def piece_refs(kind, ref, zone, p, depth):
    if kind == "slab":
        rows = depth // LOCAL
        return [(ref.at[pl.ds(al(zone * depth + p * rows, 16), rows), :], rows)]
    if kind == "halves":
        rows, cols = depth // 4, ref.shape[1] // 2
        start = al(zone * depth + (p // 2) * rows, 16)
        return [(ref.at[pl.ds(start, rows), pl.ds(al((p % 2) * cols, 128), cols)], rows)]
    if kind == "tall":
        rows = depth // LOCAL
        start = al(zone * depth + p * rows, 16)
        return [
            (ref.at[pl.ds(start, rows), pl.ds(half * COLS, COLS)], rows) for half in range(2)
        ]
    if kind == "wide":
        rows = depth // 2
        start = al(zone * depth + (p % 2) * rows, 16)
        return [
            (
                ref.at[pl.ds(start, rows), pl.ds(al((p // 2) * 2 * COLS + half * COLS, 128), COLS)],
                rows,
            )
            for half in range(2)
        ]
    if kind == "half":
        rows = depth // 2
        start = al(zone * depth + (p % 2) * rows, 16)
        return [(ref.at[pl.ds(start, rows), pl.ds(al((p // 2) * COLS, 128), COLS)], rows)]
    rows = depth // 4
    offset = int(kind)
    start = al(zone * depth + (p // 2) * rows, 16)
    return [(ref.at[pl.ds(start, rows), pl.ds(al(offset + (p % 2) * COLS, 128), COLS)], rows)]


def own_slab(ref, zone, depth, first=0, width=None):
    width = ref.shape[1] if width is None else width
    return ref.at[pl.ds(al(zone * depth, 16), depth), pl.ds(first, width)]


def block_rows(parts):
    return sum(rows for kind, ref, depth in parts for _, rows in piece_refs(kind, ref, 0, 0, depth))


def fetch(copies, pos, parts, held, only=None):
    zone, p = pos[0], pos[4]
    groups = lax.axis_size("grp")
    side = len(held) // 2
    n = held[0].shape[0] // (groups - 1) // (4 // side)
    for sib in range(2):
        for other in range(4):
            owner = p ^ (other * 2) ^ sib
            part = held[side * sib + other % side]
            at = 0 if side == 4 else other * (groups - 1) * n
            for step in range(1, groups):
                source = zone ^ step
                skip = at + n
                for index, (kind, ref, depth) in enumerate(parts):
                    for place, rows in piece_refs(kind, ref, source, owner, depth):
                        if only in (None, index):
                            copies.add(part.at[pl.ds(at, rows), :], place)
                        at += rows
                at = skip


def emit(copies, pos, parts, send, keep, quads=range(4), base=0, zones=None):
    core = pos[3]
    zones = range(lax.axis_size("grp")) if zones is None else zones
    for held, flip in ((send, 1), (keep, 0)):
        for zone in zones:
            for q in quads:
                owner = q * 2 + (core ^ flip)
                at = base
                for kind, ref, depth in parts:
                    for place, rows in piece_refs(kind, ref, zone, owner, depth):
                        copies.add(place, held.at[zone, q, pl.ds(at, rows), :])
                        at += rows


def add_first(pos, keep, got, sa, ka, sb, kb):
    x, y = pos[1], pos[2]
    half = keep.shape[0] // 2
    for zone in range(half):
        for j in range(2):
            for ref, q in ((sa, j * 2 + (1 - x)), (ka, j * 2 + x)):
                ref[zone, j] = keep[zone, q] + got[zone, q]
            for ref, q in ((sb, (1 - y) * 2 + j), (kb, y * 2 + j)):
                ref[zone, j] = keep[half + zone, q] + got[half + zone, q]


def add_second(pos, ka, ra, kb, rb, sa, ja, sb, jb):
    x, y = pos[1], pos[2]
    for zone in range(ka.shape[0]):
        for kept, got, send, hold, at in ((ka, ra, sa, ja, y), (kb, rb, sb, jb, x)):
            send[zone] = kept[zone, 1 - at] + got[zone, 1 - at]
            hold[zone] = kept[zone, at] + got[zone, at]


def add_third(pos, ka, ra, kb, rb, *rest):
    outs, total = rest[:-1], rest[-1]
    half = ka.shape[0]
    for zone in range(half):
        total[zone] = ka[zone] + ra[zone]
        total[half + zone] = kb[zone] + rb[zone]
    for step, out in enumerate(outs):
        out[...] = total[pos[0] ^ step]


def add_fourth(*refs):
    total = refs[0][...].astype(f32)
    for ref in refs[1:-1]:
        total = total + ref[...].astype(f32)
    refs[-1][...] = total.astype(bf16)


def over_blocks(total):
    bit = LOCAL
    while bit < lax.axis_size("rep"):
        other = to_rep(total, bit)
        total = call(add_fourth, shape(total.shape, bf16), (total, other), [VMEM] * 2, VMEM)
        bit *= 2
    return total


class Reduce:
    def __init__(self, pos, send, keep):
        self.pos, self.keep = pos, keep
        self.n = keep.shape[2]
        self.size = keep.shape[0] * 4 * self.n * COLS * 2
        self.got = to_rep(send, 1)

    def one(self, *events):
        groups = self.keep.shape[0]
        quad = shape((groups // 2, 2, self.n, COLS), bf16)
        got = after(self.got, *events)
        sa, self.ka, sb, self.kb = call(
            add_first,
            (quad,) * 4,
            (self.pos, self.keep, got),
            [SMEM, VMEM, VMEM],
            (VMEM,) * 4,
            moved=3 * self.size,
            near=(True, True),
        )
        self.ra, self.rb = to_rep(sa, 2), to_rep(sb, 4)
        return self.ka

    def two(self, *events, near=None):
        pair = shape((self.ka.shape[0], self.n, COLS), bf16)
        ra, rb = after((self.ra, self.rb), *events)
        sa, self.ja, sb, self.jb = call(
            add_second,
            (pair,) * 4,
            (self.pos, self.ka, ra, self.kb, rb),
            [SMEM] + [VMEM] * 4,
            (VMEM,) * 4,
            moved=3 * self.size // 2,
            near=near,
        )
        self.ra, self.rb = to_rep(sa, 4), to_rep(sb, 2)
        return self.ja

    def three(self, *events, near=None):
        groups = self.keep.shape[0]
        ra, rb = after((self.ra, self.rb), *events)
        self.blocks = call(
            add_third,
            (shape((self.n, COLS), bf16),) * groups,
            (self.pos, self.ja, ra, self.jb, rb),
            [SMEM] + [VMEM] * 4,
            (VMEM,) * groups,
            scratch=[pltpu.VMEM((groups, self.n, COLS), bf16)],
            moved=3 * self.size // 4,
            near=near,
        )
        self.arrived = [to_grp(self.blocks[step], step) for step in range(1, groups)]
        return self.blocks[0]

    def four(self, *events, near=None):
        arrived = after(self.arrived, *events)
        total = call(
            add_fourth,
            shape((self.n, COLS), bf16),
            (self.blocks[0], *arrived),
            [VMEM] * (1 + len(arrived)),
            VMEM,
            moved=self.size // 3,
            near=near,
        )
        self.total = over_blocks(total)
        return self.total

    def around(self):
        self.near = [to_rep(self.total, bit) for bit in (2, 4, 6)]

    def five(self, *events):
        near = after(self.near, *events)
        held = jnp.concatenate([self.total, *near], axis=0)
        self.both = held, to_rep(held, 1)
        return held


def cut_first(pos, wq, wk, wv, wd, first, third):
    for m, ref in enumerate((wq, wk, wv)):
        first[:, m * COLS : (m + 1) * COLS] = ref[...]
    third[...] = wd[...]


def cut_more(pos, wo, wu, small, second):
    half, quarter = wu.shape[0], wo.shape[0]
    for j in range(2):
        second[j * half : (j + 1) * half, :] = wu[:, j * COLS : (j + 1) * COLS]
    second[2 * half : 2 * half + quarter, :] = wo[...]
    second[2 * half + quarter :, :] = small[...]


def join(*refs, counts):
    first = 0
    for count, out in zip(counts, refs[-len(counts) :]):
        at = 0
        for ref in refs[first : first + count]:
            out[at : at + ref.shape[0], :] = ref[...]
            at += ref.shape[0]
        first += count


def joined(*lists, near=None):
    blocks = [block for one in lists for block in one]
    return call(
        join,
        tuple(shape((sum(block.shape[0] for block in one), one[0].shape[1]), bf16) for one in lists),
        blocks,
        [VMEM] * len(blocks),
        (VMEM,) * len(lists),
        moved=sum(block.shape[0] for block in blocks) * COLS * 4,
        counts=tuple(len(one) for one in lists),
        near=near,
    )


def layer_norm(values):
    centred = values - jnp.mean(values, axis=-1, keepdims=True)
    spread_of = jnp.mean(centred * centred, axis=-1, keepdims=True)
    inverse = lax.rsqrt(spread_of + EPSILON)
    return centred * inverse, inverse


def norm_back(upstream, normed, inverse, gain):
    scaled = upstream * gain
    return inverse * (
        scaled
        - jnp.mean(scaled, axis=-1, keepdims=True)
        - normed * jnp.mean(scaled * normed, axis=-1, keepdims=True)
    )


def attend_heads(lengths, x, vectors, weight, q_out, k_out, v_out, mixed, logsum, pair):
    width = x.shape[1]
    rows = x[...]
    scaling = HD ** (-0.5)
    for half in range(2):
        c = slice(half * COLS, (half + 1) * COLS)
        part = dot(rows, weight[:, half * 3 * COLS : (half + 1) * 3 * COLS])
        q_out[:, c] = (
            (part[:, :COLS] + vectors[0:1, c]).astype(bf16).astype(f32) * scaling
        ).astype(bf16)
        k_out[:, c] = part[:, COLS : 2 * COLS].astype(bf16)
        v_out[:, c] = (part[:, 2 * COLS :] + vectors[1:2, c]).astype(bf16)
    slots = rows.shape[0]
    lane = lax.broadcasted_iota(jnp.int32, (slots, 128), 1)
    low = lane < HD
    slot = lax.broadcasted_iota(jnp.int32, (1, slots), 1)
    bias = jnp.where(slot < lengths[pair], 0.0, MASKED).astype(f32)

    def heads(h, sums):
        s = pl.ds(al(h * 128, 128), 128)
        q1, k1, v1 = q_out[:, s], k_out[:, s], v_out[:, s]
        results, peaks = [], []
        for e in range(2):
            mask = low if e == 0 else ~low
            scores = nt(jnp.where(mask, q1, 0).astype(bf16), k1) + bias
            peak = jnp.max(scores, axis=1, keepdims=True)
            expo = jnp.exp(scores - peak).astype(bf16)
            results.append(dot(expo, jnp.where(mask, v1, 1).astype(bf16)))
            peaks.append(peak)
        total = pltpu.roll(jnp.where(low, results[1], results[0]), HD, 1)
        mixed[:, s] = (jnp.where(low, results[0], results[1]) / total).astype(bf16)
        sums = jnp.where(lane % HD == h, jnp.where(low, peaks[0], peaks[1]) + jnp.log(total), sums)
        return sums

    sums = lax.fori_loop(0, H // 2, heads, jnp.zeros((slots, 128), f32), unroll=True)
    turned = sums.T
    logsum[0, :8] = turned[:8]
    logsum[0, 8:] = turned[HD : HD + 8]


def attend(pos, lengths, x, wq, wk, wv, vectors, *rest):
    held, (q_out, k_out, v_out, mixed, logsum, w_out, weight, sems) = rest[:2], rest[2:]
    depth, width = wq.shape
    pair = pl.program_id(0)
    places = [
        (weight.at[:, pl.ds((half * 3 + m) * COLS, COLS)], pl.ds(m * width + half * COLS, COLS))
        for half in range(2)
        for m in range(3)
    ]
    writes = [
        pltpu.make_async_copy(place, w_out.at[:, c], sems.at[sems.shape[0] - 1 - i])
        for i, (place, c) in enumerate(places)
    ]

    @pl.when(pair == 0)
    def _():
        copies = Copies(sems)
        for half in range(2):
            for m, ref in enumerate((wq, wk, wv)):
                copies.add(
                    ref.at[:, pl.ds(half * COLS, COLS)],
                    own_slab(weight, pos[0], depth, (half * 3 + m) * COLS, COLS),
                )
        fetch(copies, pos, [("halves", weight, depth)], held)
        copies.wait()
        for write in writes:
            write.start()

    attend_heads(lengths, x, vectors, weight, q_out, k_out, v_out, mixed, logsum, pair)

    @pl.when(pair == pl.num_programs(0) - 1)
    def _():
        for write in writes:
            write.wait()


def expand(pos, x, mixed, wu, wo, vectors, up_bias, *rest):
    held, rest = rest[:8], rest[8:]
    act, slope, normed, inverse, wu_out, wo_out, up, out_w, xs, mixes, acts, slopes, normals, scales = rest[:14]
    row_sems, near_sems, far_sems, store_sems = rest[14:]
    depth = wo.shape[0]
    count = row_sems.shape[0]
    rows = xs.shape[0] // count
    chunk = 768
    loads = [Copies(row_sems.at[i]) for i in range(count)]
    near, far, stores = Copies(near_sems), Copies(far_sems), Copies(store_sems)
    parts = [("wide", up, depth), ("0", out_w, depth)]
    for i, load in enumerate(loads):
        s = pl.ds(i * rows, rows)
        load.add(mixed.at[s, :], mixes.at[s, :])
        load.add(x.at[s, :], xs.at[s, :])
        if i == 0:
            near.add(wo, own_slab(out_w, pos[0], depth))
            fetch(near, pos, parts, held, 1)
    far.add(wu, own_slab(up, pos[0], depth))
    fetch(far, pos, parts, held, 0)
    near.wait()
    hidden = []
    for i, load in enumerate(loads):
        load.wait()
        s = pl.ds(i * rows, rows)
        first = xs[s, :].astype(f32) + dot(mixes[s, :], out_w[...]) + vectors[2:3, :]
        normal, scale = layer_norm(first)
        normals[s, :] = normal
        scales[s, :] = jnp.broadcast_to(scale, (rows, scales.shape[1]))
        stores.add(normals.at[s, :], normed.at[s, :])
        stores.add(scales.at[s, :], inverse.at[s, :])
        hidden.append((normal * vectors[3:4, :] + vectors[4:5, :]).astype(bf16))
    far.wait()
    stores.add(up, wu_out)
    stores.add(out_w, wo_out)
    for j in range(up.shape[1] // chunk):
        c = slice(j * chunk, (j + 1) * chunk)
        for i in range(count):
            s = pl.ds(i * rows, rows)
            u = dot(hidden[i], up[:, c]) + up_bias[:, c]
            cdf, pdf = gaussian(u)
            acts[s, c] = (u * cdf).astype(bf16)
            slopes[s, c] = (cdf + u * pdf).astype(bf16)
            stores.add(acts.at[s, c], act.at[s, c])
            stores.add(slopes.at[s, c], slope.at[s, c])
    stores.wait()


def gaussian(u):
    return 0.5 + 0.5 * lax.erf(u * ROOT_HALF), jnp.exp(-0.5 * u * u) * DENSITY


def feed_forward(pos, lengths, act, slope, normed, inverse, cotangent, mixed, wd, wu, wo, vectors, *rest):
    held, rest = rest[:8], rest[8:]
    output, grad_first, grad_mixed, down_send, down_keep, send, keep = rest[:7]
    down, up, out_w, acts, slopes, normals, scales, cots, mixes, hiddens, lows, lows_first = rest[7:19]
    mixed_grads, grad_out, blocks, sems, block_sems, late_sems, store_sems, out_sems = rest[19:]
    total, width = mixes.shape
    wide = acts.shape[1]
    depth = wd.shape[0]
    count = block_sems.shape[1]
    rows = total // count
    chunk = 768

    def at(i):
        return pl.ds(i * rows, rows)

    def load(k, i):
        source, held_at = ((act, acts), (normed, normals), (cotangent, cots), (slope, slopes))[k]
        return pltpu.make_async_copy(source.at[at(i), :], held_at.at[at(i), :], block_sems.at[k, i])

    weights = Copies(sems)
    weights.add(wd, own_slab(down, pos[0], depth))
    fetch(weights, pos, [("slab", down, depth)], held)
    for k in range(3):
        load(k, 0).start()
    late = Copies(late_sems)
    weights.wait()
    load(3, 0).start()
    stores = Copies(store_sems)
    sums = [jnp.zeros((1, width), f32)] * 6
    up_sums = [jnp.zeros((1, chunk), f32)] * (wide // chunk)
    first_gain, gain = vectors[3:4, :], vectors[6:7, :]

    def column_sums(values):
        return jnp.sum(values, axis=0, keepdims=True)

    def begin(i):
        for k in range(3):
            load(k, i).wait()
        if i == 0:
            for source, place in ((wu, up), (wo, out_w), (inverse, scales)):
                late.add(source, place)
        if i + 1 < count:
            for k in range(3):
                load(k, i + 1).start()
        else:
            late.add(mixed, mixes)
        return dot(acts[at(i), :], down[...])

    def middle(i, product):
        s = at(i)
        per_pair = count // lengths.shape[0]
        slot = lax.broadcasted_iota(jnp.int32, (rows, 1), 0) + (i % per_pair) * rows
        mask = (slot < lengths[i // per_pair]).astype(f32)
        hidden = normals[s, :] * first_gain + vectors[4:5, :]
        hiddens[s, :] = hidden.astype(bf16)
        normal, scale = layer_norm(hidden + product + vectors[5:6, :])
        upstream = cots[s, :].astype(f32) * mask
        cots[s, :] = ((normal * gain + vectors[7:8, :]) * mask).astype(bf16)
        stores.add(cots.at[s, :], output.at[s, :])
        grad_second = norm_back(upstream, normal, scale, gain)
        low = grad_second.astype(bf16)
        lows[s, :] = low
        for k, value in enumerate((upstream * normal, upstream, low.astype(f32))):
            sums[k] = sums[k] + column_sums(value)
        return grad_second, low

    def grow(i, low):
        s = at(i)
        load(3, i).wait()
        if i + 1 < count:
            load(3, i + 1).start()
        for j in range(wide // chunk):
            c = slice(j * chunk, (j + 1) * chunk)
            grown = (nt(low, down[c, :]) * slopes[s, c].astype(f32)).astype(bf16)
            slopes[s, c] = grown
            up_sums[j] = up_sums[j] + column_sums(grown.astype(f32))

    def shrink(i):
        if i == 0:
            for copy in late.held[:3]:
                copy.wait()
        return nt(slopes[at(i), :], up[...])

    def end(i, grad_second, product):
        s = at(i)
        normal = normals[s, :]
        upstream = grad_second + product
        result = norm_back(upstream, normal, scales[s, 0:1], first_gain)
        normals[s, :] = result
        stores.add(normals.at[s, :], grad_first.at[s, :])
        low = result.astype(bf16)
        lows_first[s, :] = low
        mixed_grads[s, :] = nt(low, out_w[...]).astype(bf16)
        stores.add(mixed_grads.at[s, :], grad_mixed.at[s, :])
        for k, value in enumerate((upstream * normal, upstream, low.astype(f32))):
            sums[3 + k] = sums[3 + k] + column_sums(value)

    pieces = Copies(out_sems)

    def down_zone(zone):
        s = slice(zone * depth, (zone + 1) * depth)
        down[s, :] = tn(acts[:, s], lows[...]).astype(bf16)
        emit(pieces, pos, [("tall", down, depth)], down_send, down_keep, zones=(zone,))

    for a in range(0, count, 2):
        b = a + 1
        product_a = begin(a)
        second_a, low_a = middle(a, product_a)
        product_b = begin(b)
        grow(a, low_a)
        second_b, low_b = middle(b, product_b)
        grow(b, low_b)
        product_a = shrink(a)
        product_b = shrink(b)
        end(a, second_a, product_a)
        if b == count - 1:
            down_zone(0)
        end(b, second_b, product_b)
    for zone in range(1, wide // depth):
        down_zone(zone)
    up_depth = width // lax.axis_size("grp")
    grad_up = acts.at[pl.ds(0, width), :]
    late.held[3].wait()
    grad_out[...] = tn(mixes[...], lows_first[...]).astype(bf16)
    emit(pieces, pos, [("0", grad_out, up_depth)], send, keep, base=up_depth)
    vector_blocks(blocks, sums[:3] + up_sums + sums[3:])
    emit_vectors(pieces, pos, blocks, up_depth + up_depth // 4, send, keep)
    for j in range(wide // chunk):
        c = slice(j * chunk, (j + 1) * chunk)
        acts[:width, c] = tn(hiddens[...], slopes[:, c]).astype(bf16)
        emit(pieces, pos, [("wide", grad_up, up_depth)], send, keep, (j,))
    stores.wait()
    pieces.wait()


def vector_blocks(blocks, rows):
    blocks[...] = jnp.zeros_like(blocks)
    for p in range(min(LOCAL, len(rows))):
        here = rows[p::LOCAL]
        half = here[0].shape[1] // 2
        stacked = [part for row in here for part in (row[:, :half], row[:, half:])]
        stacked.append(jnp.zeros((16 - 2 * len(here), half), f32))
        blocks[p] = jnp.concatenate(stacked, axis=0).astype(bf16)


def vector_of(block, i):
    at = 2 * (i // LOCAL)
    return jnp.concatenate([block[at : at + 1, :], block[at + 1 : at + 2, :]], axis=1)


def emit_vectors(copies, pos, blocks, base, send, keep):
    for held, flip in ((send, 1), (keep, 0)):
        for zone in range(send.shape[0]):
            for q in range(4):
                owner = q * 2 + (pos[3] ^ flip)
                copies.add(blocks.at[owner], held.at[zone, q, pl.ds(base, 16), :])


def pair_back(lengths, q, k, v, mixed, grad_mixed, logsum, *rest, pair):
    if pair:
        old_sums, rest = rest[0], rest[2:]
    grads, sums, rows_of, held, deltas, in_sems, out_sem = rest
    slots, width = held.shape[0], q.shape[1]
    here = pl.ds(pair * slots, slots)
    spans = 2
    span = width // spans
    loads = [Copies(in_sems.at[i]) for i in range(spans)]
    for part, load in enumerate(loads):
        c = pl.ds(part * span, span)
        for i, ref in enumerate((mixed, grad_mixed, q, k, v)):
            load.add(ref.at[here, c], rows_of.at[i, :, c])
    stores = Copies(out_sem)
    sums[...] = old_sums[...] if pair else jnp.zeros_like(sums)
    low = lax.broadcasted_iota(jnp.int32, (slots, 128), 1) < HD
    slot = lax.broadcasted_iota(jnp.int32, (slots, 1), 0)
    scaling = HD ** (-0.5)
    bias = jnp.where(slot < lengths[pair], 0.0, MASKED).astype(f32)

    def heads(h, carry):
        s = pl.ds(al(h * 128, 128), 128)
        g1, q1, k1, v1 = (rows_of[i, :, s] for i in (1, 2, 3, 4))
        probs, scores_back, qs, gs, ks = [], [], [], [], []
        for e in range(2):
            mask = low if e == 0 else ~low
            qm = jnp.where(mask, q1, 0).astype(bf16)
            gm = jnp.where(mask, g1, 0).astype(bf16)
            prob = jnp.exp(nt(k1, qm) + bias - logsum[pair, pl.ds(h + 8 * e, 1), :])
            back = prob * (nt(v1, gm) - deltas[pl.ds(h * 2 + e, 1), :])
            probs.append(prob.astype(bf16))
            scores_back.append(back.astype(bf16))
            qs.append(qm)
            gs.append(gm)
            ks.append(jnp.where(mask, k1, 0).astype(bf16))
        grad_v = dot(jnp.concatenate(probs, 1), jnp.concatenate(gs, 0))
        grad_k = dot(jnp.concatenate(scores_back, 1), jnp.concatenate(qs, 0))
        grad_q = tn(jnp.concatenate(scores_back, 0), jnp.concatenate(ks, 0)) * scaling
        for m, value in enumerate((grad_q, grad_k, grad_v)):
            value = value.astype(bf16)
            held[:, pl.ds(al(m * width + h * 128, 128), 128)] = value
            if m != 1:
                sums[m : m + 1, s] += jnp.sum(value.astype(f32), axis=0, keepdims=True)
        return carry

    for part, load in enumerate(loads):
        load.wait()
        c = pl.ds(part * span, span)
        select = (
            lax.broadcasted_iota(jnp.int32, (16, span), 1) // HD + part * span // HD
            == lax.broadcasted_iota(jnp.int32, (16, span), 0)
        ).astype(bf16)
        product = rows_of[0, :, c].astype(f32) * rows_of[1, :, c].astype(f32)
        high = product.astype(bf16)
        rest_of = (product - high.astype(f32)).astype(bf16)
        delta = nt(select, high) + nt(select, rest_of)
        deltas[...] = delta if part == 0 else deltas[...] + delta
        lax.fori_loop(part * span // 128, (part + 1) * span // 128, heads, 0, unroll=True)
        for m in range(3):
            here_m = pl.ds(m * width + part * span, span)
            stores.add(held.at[:, here_m], grads.at[here, here_m])
    stores.wait()


def heads_weights(pos, x, grads, sums, send, keep, xs, held, weight_grads, blocks, sems, out_sems):
    width = xs.shape[1]
    depth = width // lax.axis_size("grp")
    copies = Copies(sems)

    def add(m):
        c = pl.ds(m * width, width)
        copies.add(grads.at[:, c], held.at[:, c])

    copies.add(x, xs)
    add(0)
    copies.wait()
    add(1)
    stores = Copies(out_sems)
    vector_blocks(blocks, [sums[m : m + 1, :] for m in (0, 2)])
    emit_vectors(stores, pos, blocks, 3 * depth // 4, send, keep)
    for m in range(3):
        c = slice(m * width, (m + 1) * width)
        if m:
            copies.held[1 + m].wait()
        if m == 1:
            add(2)
        weight_grads[:, c] = tn(xs[...], held[:, c]).astype(bf16)
        emit(stores, pos, [(str(m * width), weight_grads, depth)], send, keep, base=m * depth // 4)
    stores.wait()


def inputs_back(grad_first, grads, weight, out):
    out[...] = (grad_first[...] + nt(grads[...], weight[...])).astype(bf16)


def place_ffn(pos, mine, sibling, gd, gu, go, g2, s2, bd, bu, g1, s1, bo, small):
    tall, half, quarter = gd.shape[0] // LOCAL, gu.shape[0] // 2, go.shape[0] // 4
    n = mine.shape[0] // 4 - 2 * tall
    for sib, held in ((0, mine), (1, sibling)):
        for other in range(4):
            owner = pos[4] ^ (other * 2) ^ sib
            at = other * 2 * tall
            for j in range(2):
                gd[pl.ds(al(owner * tall, 16), tall), j * COLS : (j + 1) * COLS] = held[
                    at : at + tall, :
                ].astype(f32)
                at += tall
            at = 8 * tall + (0, 2, 1, 3)[other] * n
            for j in range(2):
                first = pl.ds(al((owner // 2) * 2 * COLS + j * COLS, 128), COLS)
                gu[pl.ds(al((owner % 2) * half, 16), half), first] = held[at : at + half, :].astype(f32)
                at += half
            rows = pl.ds(al((owner // 2) * quarter, 16), quarter)
            go[rows, pl.ds(al((owner % 2) * COLS, 128), COLS)] = held[at : at + quarter, :].astype(f32)
            at += quarter
            small[owner] = held[at : at + 16, :].astype(f32)

    for i, out in ((0, g2), (1, s2), (2, bd), (7, g1), (8, s1), (9, bo)):
        out[...] = own_part(pos, vector_of(small[i % LOCAL], i), out.shape[1])
    total = jnp.zeros(bu.shape, f32)
    for zone in range(4):
        total = jnp.where(pos[0] == zone, vector_of(small[3 + zone], 3 + zone), total)
    bu[...] = total


def own_part(pos, row, size):
    total = row[:, :size]
    for zone in range(1, row.shape[1] // size):
        total = jnp.where(pos[0] == zone, row[:, zone * size : (zone + 1) * size], total)
    return total


def place_heads(pos, mine, sibling, gq, gk, gv, bq, bv, small):
    quarter = gq.shape[0] // 4
    n = mine.shape[0] // 4
    for sib, held in ((0, mine), (1, sibling)):
        for other in range(4):
            owner = pos[4] ^ (other * 2) ^ sib
            row4 = pl.ds(al((owner // 2) * quarter, 16), quarter)
            col2 = pl.ds(al((owner % 2) * COLS, 128), COLS)
            at = other * n
            for out in (gq, gk, gv):
                out[row4, col2] = held[at : at + quarter, :].astype(f32)
                at += quarter
            small[owner] = held[at : at + 16, :].astype(f32)[:8]
    for i, out in enumerate((bq, bv)):
        out[...] = own_part(pos, vector_of(small[i], i), out.shape[1])


def shards(
    tokens,
    lengths,
    cotangent,
    query_weight,
    query_bias,
    key_weight,
    value_weight,
    value_bias,
    out_weight,
    out_bias,
    norm_gain,
    norm_shift,
    up_weight,
    up_bias,
    down_weight,
    down_bias,
    final_gain,
    final_shift,
):
    groups = lax.axis_size("grp")
    pairs, seqlen, width = tokens.shape
    rows = pairs * seqlen
    depth = width // groups
    wide = up_weight.shape[1]
    inputs = tokens.reshape(rows, width)
    upstream = cotangent.reshape(rows, width)
    pos = position()
    n1 = 3 * depth // 4
    n2 = depth + depth // 4
    n3 = depth

    def cut(kernel, sizes, args, specs):
        return pl.pallas_call(
            kernel,
            grid_spec=pltpu.PrefetchScalarGridSpec(
                num_scalar_prefetch=1,
                grid=(1,),
                in_specs=specs,
                out_specs=[pl.BlockSpec(size, lambda i, at: (0, 0)) for size in sizes],
            ),
            out_shape=[shape(size, bf16) for size in sizes],
            name=kernel.__name__,
        )(pos, *args)

    square = pl.BlockSpec((depth // 4, COLS), lambda i, at: (at[4] // 2, at[4] % 2))
    tall = pl.BlockSpec((down_weight.shape[0] // LOCAL, width), lambda i, at: (at[4], 0))
    first, third = cut(
        cut_first,
        ((depth // 4, 3 * COLS), (n3 // 2, width)),
        (query_weight, key_weight, value_weight, down_weight),
        [square] * 3 + [tall],
    )
    z1 = [to_grp(first, step) for step in range(1, groups)]
    close = to_grp(third, 1)
    small = jnp.concatenate(
        after(
            [
                query_bias,
                value_bias,
                out_bias,
                norm_gain,
                norm_shift,
                down_bias,
                final_gain,
                final_shift,
                up_bias,
            ],
            first,
        )
    )
    count = small.shape[0] // COLS
    small = jnp.pad(small.reshape(count, COLS), ((0, 16 - count), (0, 0)))
    (second,) = cut(
        cut_more,
        ((n2 + 16, COLS),),
        (out_weight, up_weight, small),
        [
            square,
            pl.BlockSpec((depth // 2, 2 * COLS), lambda i, at: (at[4] % 2, at[4] // 2)),
            pl.BlockSpec((16, COLS), lambda i, at: (0, 0)),
        ],
    )
    z1 = after(z1, second)

    def near(mine):
        return [mine, *(to_rep(mine, bit) for bit in (2, 4, 6))]

    def other_core(held):
        return [to_rep(part, 1) for part in held]

    mine1 = jnp.concatenate(z1, axis=0)
    from_x, from_y = to_rep(mine1, 2), to_rep(mine1, 4)
    far = [to_grp(second, 2), to_grp(second, 3)]
    cut_at = (mine1.shape[0] // 2 + 15) // 16 * 16
    low, high = to_rep(from_x[:cut_at], 4), to_rep(from_y[cut_at:], 2)
    parts = [second, to_grp(after(second, (from_x, from_y)), 1), *far]
    parts[1:] = after(parts[1:], (low, high))
    mine2 = jnp.concatenate([part[:n2] for part in parts[1:]], axis=0)
    held2 = near(mine2)
    held1 = jnp.concatenate([mine1, from_x, from_y, low, high], axis=0)
    held1 = [held1, to_rep(held1, 1)]
    flat = jnp.stack([part[n2 : n2 + count].reshape(-1) for part in parts])
    by_zone = jnp.stack([flat[pos[0] ^ zone] for zone in range(groups)]).astype(f32)
    vectors = by_zone[:, : 8 * depth].reshape(groups, 8, depth).transpose(1, 0, 2).reshape(8, width)
    up_vector = by_zone[:, 8 * depth :].reshape(1, wide)
    third, close = after((third, close), mine2)
    far = [to_grp(third, 2), to_grp(third, 3)]

    mat = shape((rows, width), bf16)
    mat32 = shape((rows, width), f32)
    dense = 2 * rows * width * width
    by_pair = pl.BlockSpec((seqlen, width), lambda i: (i, 0))
    q, k, v, mixed, logsum, w_all = call(
        attend,
        (mat, mat, mat, mat, shape((pairs, 16, seqlen), f32), shape((width, 3 * width), bf16)),
        (pos, lengths, after(inputs, (mine2, close)), query_weight, key_weight, value_weight, vectors, *held1),
        [SMEM, SMEM, by_pair, ANY, ANY, ANY, VMEM] + [ANY] * 2,
        (by_pair,) * 4 + (pl.BlockSpec((1, 16, seqlen), lambda i: (i, 0, 0)), ANY),
        scratch=[
            pltpu.VMEM((width, 3 * width), bf16),
            pltpu.SemaphoreType.DMA((12 + 8 * (groups - 1),)),
        ],
        grid=(pairs,),
        flops=12 * dense,
        moved=12 * rows * width,
    )
    held2, far = after((held2, far), w_all)
    held2 += other_core(held2)
    (mine3,) = joined((close, *far))
    held3 = near(mine3)
    held3 += other_core(held3[:1])
    halves = rows // 512
    act, slope, normed, inverse, wu_all, wo_all = call(
        expand,
        (
            shape((rows, wide), bf16),
            shape((rows, wide), bf16),
            mat32,
            shape((rows, 128), f32),
            shape((width, wide), bf16),
            shape((width, width), bf16),
        ),
        (pos, after(inputs, held3[0]), mixed, up_weight, out_weight, vectors, up_vector, *held2),
        [SMEM, ANY, ANY, ANY, ANY, VMEM, VMEM] + [ANY] * 8,
        (ANY,) * 6,
        scratch=[
            pltpu.VMEM((width, wide), bf16),
            pltpu.VMEM((width, width), bf16),
            pltpu.VMEM((rows, width), bf16),
            pltpu.VMEM((rows, width), bf16),
            pltpu.VMEM((rows, wide), bf16),
            pltpu.VMEM((rows, wide), bf16),
            pltpu.VMEM((rows, width), f32),
            pltpu.VMEM((rows, 128), f32),
            pltpu.SemaphoreType.DMA((halves, 2)),
            pltpu.SemaphoreType.DMA((1 + 8 * (groups - 1),)),
            pltpu.SemaphoreType.DMA((1 + 8 * (groups - 1) * 2,)),
            pltpu.SemaphoreType.DMA((2 + 2 * halves + 2 * halves * wide // 768,)),
        ],
        flops=8 * dense,
        moved=18 * rows * width,
    )
    held3 = after(held3, wo_all)
    held3 += other_core(held3[1:4])

    vec = shape((8, width), f32)

    def travelling(n):
        return (shape((groups, 4, n, COLS), bf16),) * 2

    n_up = depth + depth // 4 + 16
    output, grad_first, grad_mixed, down_send, down_keep, send, keep = call(
        feed_forward,
        (mat, mat32, mat, *travelling(n3), *travelling(n_up)),
        (pos, lengths, act, slope, normed, inverse, upstream, mixed, down_weight, wu_all, wo_all, vectors)
        + tuple(held3),
        [SMEM, SMEM] + [ANY] * 9 + [VMEM] + [ANY] * 8,
        (ANY,) * 7,
        scratch=[
            pltpu.VMEM((wide, width), bf16),
            pltpu.VMEM((width, wide), bf16),
            pltpu.VMEM((width, width), bf16),
            pltpu.VMEM((rows, wide), bf16),
            pltpu.VMEM((rows, wide), bf16),
            pltpu.VMEM((rows, width), f32),
            pltpu.VMEM((rows, 128), f32),
            pltpu.VMEM((rows, width), bf16),
            pltpu.VMEM((rows, width), bf16),
            pltpu.VMEM((rows, width), bf16),
            pltpu.VMEM((rows, width), bf16),
            pltpu.VMEM((rows, width), bf16),
            pltpu.VMEM((rows, width), bf16),
            pltpu.VMEM((width, width), bf16),
            pltpu.VMEM((LOCAL, 16, COLS), bf16),
            pltpu.SemaphoreType.DMA((1 + 8 * (groups - 1),)),
            pltpu.SemaphoreType.DMA((4, halves)),
            pltpu.SemaphoreType.DMA((4,)),
            pltpu.SemaphoreType.DMA((3 * halves,)),
            pltpu.SemaphoreType.DMA((groups * 4 * 2 * 6,)),
        ],
        flops=22 * dense,
        moved=50 * rows * width,
    )
    down = Reduce(pos, down_send, down_keep)
    up = Reduce(pos, after(send, down.got), keep)
    done = down.one()
    done = up.one(done)

    n_heads = n1 + 16
    grads = sums = None
    for pair in range(pairs):
        grads, sums = call(
            pair_back,
            (shape((rows, 3 * width), bf16), vec),
            (lengths, q, k, v, mixed, grad_mixed, after(logsum, done))
            + ((sums, grads) if pair else ()),
            [SMEM] + [ANY] * 5 + [VMEM] + ([VMEM, ANY] if pair else []),
            (ANY, VMEM),
            scratch=[
                pltpu.VMEM((5, seqlen, width), bf16),
                pltpu.VMEM((seqlen, 3 * width), bf16),
                pltpu.VMEM((16, seqlen), f32),
                pltpu.SemaphoreType.DMA((2, 5)),
                pltpu.SemaphoreType.DMA((6,)),
            ],
            flops=12 * dense // pairs,
            moved=12 * rows * width,
            aliases={8: 0} if pair else None,
            limit=MIDDLE_LIMIT,
            pair=pair,
        )
        if pair == 0:
            done = down.two(grads, near=(True, True))
    done = up.two(grads, near=(True, True))
    done = down.three(done, near=(True, True))
    send, keep = call(
        heads_weights,
        travelling(n_heads),
        (pos, after(inputs, done), grads, sums),
        [SMEM, ANY, ANY, VMEM],
        (ANY, ANY),
        scratch=[
            pltpu.VMEM((rows, width), bf16),
            pltpu.VMEM((rows, 3 * width), bf16),
            pltpu.VMEM((width, 3 * width), bf16),
            pltpu.VMEM((LOCAL, 16, COLS), bf16),
            pltpu.SemaphoreType.DMA((4,)),
            pltpu.SemaphoreType.DMA((groups * 4 * 2 * 4,)),
        ],
        flops=3 * dense,
        moved=12 * rows * width,
        limit=MIDDLE_LIMIT,
    )
    heads = Reduce(pos, after(send, (up.ra, up.rb, down.arrived)), keep)
    done = up.three(down.arrived, near=(True, True))
    done = heads.one(done)
    row_block = rows // halves
    by_row = pl.BlockSpec((row_block, width), lambda i: (i, 0))
    grad_inputs = call(
        inputs_back,
        mat,
        (after(grad_first, done), grads, w_all),
        [by_row, pl.BlockSpec((row_block, 3 * width), lambda i: (i, 0)), VMEM],
        by_row,
        grid=(halves,),
        flops=3 * dense,
        moved=16 * rows * width,
        limit=MIDDLE_LIMIT,
    )
    done = heads.two(grad_inputs, up.arrived, near=(True, True))
    down_total = down.four(done, near=(True, True))
    up_total = up.four(down_total, near=(True, True))
    down_total, up_total = after((down_total, up_total), heads.ja)
    heads.three(near=(True, True))
    near_down, near_up = after((to_rep(down_total, 2), to_rep(up_total, 4)), heads.blocks[0])
    down_pair, up_pair = joined((down_total, near_down), (up_total, near_up), near=(True, True))
    (both,) = joined(
        (down_pair, to_rep(down_pair, 4), up_pair, to_rep(up_pair, 2)), near=(True, True)
    )
    heads.four(near=(True, True))
    heads.around()
    both = both, to_rep(after(both, heads.arrived), 1)
    vector = shape((1, depth), f32)
    square = shape((depth, width), f32)
    gd, gu, go, g2, s2, bd, bu, g1, s1, bo = call(
        place_ffn,
        (shape((wide // groups, width), f32), shape((depth, wide), f32), square)
        + (vector,) * 3
        + (shape((1, wide // groups), f32),)
        + (vector,) * 3,
        (pos, *both),
        [SMEM, VMEM, VMEM],
        (VMEM,) * 10,
        scratch=[pltpu.VMEM((LOCAL, 16, COLS), f32)],
        moved=24 * depth * width,
        near=(True, False),
    )
    heads.five(gd)
    gq, gk, gv, bq, bv = call(
        place_heads,
        (square,) * 3 + (vector,) * 2,
        (pos, *heads.both),
        [SMEM] + [VMEM] * 2,
        (VMEM,) * 5,
        scratch=[pltpu.VMEM((LOCAL, 8, COLS), f32)],
        moved=24 * depth * width,
        near=(True, False),
    )
    bq, bv, bo, g1, s1, bu, bd, g2, s2 = (
        row.reshape(-1) for row in (bq, bv, bo, g1, s1, bu, bd, g2, s2)
    )
    return (
        output.reshape(pairs, seqlen, width),
        grad_inputs.reshape(pairs, seqlen, width),
        gq,
        bq,
        gk,
        gv,
        bv,
        go,
        bo,
        g1,
        s1,
        gu,
        bu,
        gd,
        bd,
        g2,
        s2,
    )


def solution(mesh):
    pairs = P(("grp", "rep"), None, None)
    matrix = P("grp", None)
    vector = P("grp")
    placed = (pairs, P(("grp", "rep")), pairs, matrix, vector, matrix, matrix, vector, matrix, vector)
    placed += (vector, vector, matrix, vector, matrix, vector, vector, vector)
    results = (pairs, pairs, matrix, vector, matrix, matrix, vector, matrix, vector, vector, vector)
    results += (matrix, vector, matrix, vector, vector, vector)
    return jax.shard_map(shards, mesh=mesh, in_specs=placed, out_specs=results, check_vma=False)
```

```python
import functools

import jax
import jax.numpy as jnp
from jax import lax
from jax.experimental import pallas as pl
from jax.experimental.pallas import tpu as pltpu
from jax.sharding import PartitionSpec as P

H = 12
HD = 64
EPSILON = 1e-06
MASKED = -1e30
DENSITY = 0.3989422804014327
ROOT_HALF = 0.7071067811865476

f32 = jnp.float32
bf16 = jnp.bfloat16
VMEM = pl.BlockSpec(memory_space=pltpu.VMEM)
SMEM = pl.BlockSpec(memory_space=pltpu.SMEM)
ANY = pl.BlockSpec(memory_space=pl.ANY)
VMEM_LIMIT = 63 * 2**20
MIDDLE_LIMIT = 36 * 2**20
SMALL_LIMIT = 20 * 2**20
COLS = 384
WEIGHT = 8
LOCAL = 8


def dot(a, b):
    return jnp.dot(a, b, preferred_element_type=f32)


def nt(a, b):
    return lax.dot_general(a, b, (((1,), (1,)), ((), ())), preferred_element_type=f32)


def tn(a, b):
    return lax.dot_general(a, b, (((0,), (0,)), ((), ())), preferred_element_type=f32)


def shape(dims, dtype):
    return jax.ShapeDtypeStruct(dims, dtype)


def al(value, by):
    return pl.multiple_of(value, by)


def inside(out):
    return pltpu.VMEM(out.shape, out.dtype)


def call(
    kernel, outs, args, specs, out_specs, scratch=(), grid=(), flops=0, moved=0, aliases=None, near=None, limit=VMEM_LIMIT, **fixed
):
    if near is not None:
        limit = SMALL_LIMIT
        if near[0]:
            args = [
                pltpu.with_memory_space_constraint(arg, pltpu.VMEM) if spec is VMEM else arg
                for arg, spec in zip(args, specs)
            ]
        if near[1]:
            outs = jax.tree.map(inside, outs)
    return pl.pallas_call(
        functools.partial(kernel, **fixed) if fixed else kernel,
        grid=grid,
        out_shape=outs,
        in_specs=specs,
        out_specs=out_specs,
        scratch_shapes=scratch,
        input_output_aliases=aliases or {},
        compiler_params=pltpu.CompilerParams(vmem_limit_bytes=limit),
        cost_estimate=pl.CostEstimate(
            flops=WEIGHT * flops, bytes_accessed=WEIGHT * moved if flops else 0, transcendentals=0
        ),
        name=kernel.__name__,
    )(*args)


def after(values, *events):
    return lax.optimization_barrier((values, events))[0]


def to_rep(array, bit):
    size = lax.axis_size("rep")
    return lax.ppermute(array, "rep", [(i, i ^ bit) for i in range(size)])


def to_grp(array, bit):
    size = lax.axis_size("grp")
    return lax.ppermute(array, "grp", [(i, i ^ bit) for i in range(size)])


def position():
    z = lax.axis_index("grp").astype(jnp.int32)
    p = lax.axis_index("rep").astype(jnp.int32) % LOCAL
    return jnp.stack([z, (p // 2) % 2, p // 4, p % 2, p])


class Copies:
    def __init__(self, sems):
        self.sems, self.held = sems, []

    def add(self, src, dst):
        copy = pltpu.make_async_copy(src, dst, self.sems.at[len(self.held)])
        copy.start()
        self.held.append(copy)

    def wait(self):
        for copy in self.held:
            copy.wait()


def piece_refs(kind, ref, zone, p, depth):
    if kind == "slab":
        rows = depth // LOCAL
        return [(ref.at[pl.ds(al(zone * depth + p * rows, 16), rows), :], rows)]
    if kind == "halves":
        rows, cols = depth // 4, ref.shape[1] // 2
        start = al(zone * depth + (p // 2) * rows, 16)
        return [(ref.at[pl.ds(start, rows), pl.ds(al((p % 2) * cols, 128), cols)], rows)]
    if kind == "tall":
        rows = depth // LOCAL
        start = al(zone * depth + p * rows, 16)
        return [
            (ref.at[pl.ds(start, rows), pl.ds(half * COLS, COLS)], rows) for half in range(2)
        ]
    if kind == "wide":
        rows = depth // 2
        start = al(zone * depth + (p % 2) * rows, 16)
        return [
            (
                ref.at[pl.ds(start, rows), pl.ds(al((p // 2) * 2 * COLS + half * COLS, 128), COLS)],
                rows,
            )
            for half in range(2)
        ]
    if kind == "half":
        rows = depth // 2
        start = al(zone * depth + (p % 2) * rows, 16)
        return [(ref.at[pl.ds(start, rows), pl.ds(al((p // 2) * COLS, 128), COLS)], rows)]
    rows = depth // 4
    offset = int(kind)
    start = al(zone * depth + (p // 2) * rows, 16)
    return [(ref.at[pl.ds(start, rows), pl.ds(al(offset + (p % 2) * COLS, 128), COLS)], rows)]


def own_slab(ref, zone, depth, first=0, width=None):
    width = ref.shape[1] if width is None else width
    return ref.at[pl.ds(al(zone * depth, 16), depth), pl.ds(first, width)]


def block_rows(parts):
    return sum(rows for kind, ref, depth in parts for _, rows in piece_refs(kind, ref, 0, 0, depth))


def fetch(copies, pos, parts, held, only=None):
    zone, p = pos[0], pos[4]
    groups = lax.axis_size("grp")
    side = len(held) // 2
    n = held[0].shape[0] // (groups - 1) // (4 // side)
    for sib in range(2):
        for other in range(4):
            owner = p ^ (other * 2) ^ sib
            part = held[side * sib + other % side]
            at = 0 if side == 4 else other * (groups - 1) * n
            for step in range(1, groups):
                source = zone ^ step
                skip = at + n
                for index, (kind, ref, depth) in enumerate(parts):
                    for place, rows in piece_refs(kind, ref, source, owner, depth):
                        if only in (None, index):
                            copies.add(part.at[pl.ds(at, rows), :], place)
                        at += rows
                at = skip


def emit(copies, pos, parts, send, keep, quads=range(4), base=0, zones=None):
    core = pos[3]
    zones = range(lax.axis_size("grp")) if zones is None else zones
    for held, flip in ((send, 1), (keep, 0)):
        for zone in zones:
            for q in quads:
                owner = q * 2 + (core ^ flip)
                at = base
                for kind, ref, depth in parts:
                    for place, rows in piece_refs(kind, ref, zone, owner, depth):
                        copies.add(place, held.at[zone, q, pl.ds(at, rows), :])
                        at += rows


def add_first(pos, keep, got, sa, ka, sb, kb):
    x, y = pos[1], pos[2]
    half = keep.shape[0] // 2
    for zone in range(half):
        for j in range(2):
            for ref, q in ((sa, j * 2 + (1 - x)), (ka, j * 2 + x)):
                ref[zone, j] = keep[zone, q] + got[zone, q]
            for ref, q in ((sb, (1 - y) * 2 + j), (kb, y * 2 + j)):
                ref[zone, j] = keep[half + zone, q] + got[half + zone, q]


def add_second(pos, ka, ra, kb, rb, sa, ja, sb, jb):
    x, y = pos[1], pos[2]
    for zone in range(ka.shape[0]):
        for kept, got, send, hold, at in ((ka, ra, sa, ja, y), (kb, rb, sb, jb, x)):
            send[zone] = kept[zone, 1 - at] + got[zone, 1 - at]
            hold[zone] = kept[zone, at] + got[zone, at]


def add_third(pos, ka, ra, kb, rb, *rest):
    outs, total = rest[:-1], rest[-1]
    half = ka.shape[0]
    for zone in range(half):
        total[zone] = ka[zone] + ra[zone]
        total[half + zone] = kb[zone] + rb[zone]
    for step, out in enumerate(outs):
        out[...] = total[pos[0] ^ step]


def add_fourth(*refs):
    total = refs[0][...].astype(f32)
    for ref in refs[1:-1]:
        total = total + ref[...].astype(f32)
    refs[-1][...] = total.astype(bf16)


def over_blocks(total):
    bit = LOCAL
    while bit < lax.axis_size("rep"):
        other = to_rep(total, bit)
        total = call(add_fourth, shape(total.shape, bf16), (total, other), [VMEM] * 2, VMEM)
        bit *= 2
    return total


class Reduce:
    def __init__(self, pos, send, keep):
        self.pos, self.keep = pos, keep
        self.n = keep.shape[2]
        self.size = keep.shape[0] * 4 * self.n * COLS * 2
        self.got = to_rep(send, 1)

    def one(self, *events):
        groups = self.keep.shape[0]
        quad = shape((groups // 2, 2, self.n, COLS), bf16)
        got = after(self.got, *events)
        sa, self.ka, sb, self.kb = call(
            add_first,
            (quad,) * 4,
            (self.pos, self.keep, got),
            [SMEM, VMEM, VMEM],
            (VMEM,) * 4,
            moved=3 * self.size,
            near=(True, True),
        )
        self.ra, self.rb = to_rep(sa, 2), to_rep(sb, 4)
        return self.ka

    def two(self, *events, near=None):
        pair = shape((self.ka.shape[0], self.n, COLS), bf16)
        ra, rb = after((self.ra, self.rb), *events)
        sa, self.ja, sb, self.jb = call(
            add_second,
            (pair,) * 4,
            (self.pos, self.ka, ra, self.kb, rb),
            [SMEM] + [VMEM] * 4,
            (VMEM,) * 4,
            moved=3 * self.size // 2,
            near=near,
        )
        self.ra, self.rb = to_rep(sa, 4), to_rep(sb, 2)
        return self.ja

    def three(self, *events, near=None):
        groups = self.keep.shape[0]
        ra, rb = after((self.ra, self.rb), *events)
        self.blocks = call(
            add_third,
            (shape((self.n, COLS), bf16),) * groups,
            (self.pos, self.ja, ra, self.jb, rb),
            [SMEM] + [VMEM] * 4,
            (VMEM,) * groups,
            scratch=[pltpu.VMEM((groups, self.n, COLS), bf16)],
            moved=3 * self.size // 4,
            near=near,
        )
        self.arrived = [to_grp(self.blocks[step], step) for step in range(1, groups)]
        return self.blocks[0]

    def four(self, *events, near=None):
        arrived = after(self.arrived, *events)
        total = call(
            add_fourth,
            shape((self.n, COLS), bf16),
            (self.blocks[0], *arrived),
            [VMEM] * (1 + len(arrived)),
            VMEM,
            moved=self.size // 3,
            near=near,
        )
        self.total = over_blocks(total)
        return self.total

    def around(self):
        self.near = [to_rep(self.total, bit) for bit in (2, 4, 6)]

    def five(self, *events):
        near = after(self.near, *events)
        held = jnp.concatenate([self.total, *near], axis=0)
        self.both = held, to_rep(held, 1)
        return held


def cut_first(pos, wq, wk, wv, wd, first, third):
    for m, ref in enumerate((wq, wk, wv)):
        first[:, m * COLS : (m + 1) * COLS] = ref[...]
    third[...] = wd[...]


def cut_more(pos, wo, wu, small, second):
    half, quarter = wu.shape[0], wo.shape[0]
    for j in range(2):
        second[j * half : (j + 1) * half, :] = wu[:, j * COLS : (j + 1) * COLS]
    second[2 * half : 2 * half + quarter, :] = wo[...]
    second[2 * half + quarter :, :] = small[...]


def join(*refs, counts):
    first = 0
    for count, out in zip(counts, refs[-len(counts) :]):
        at = 0
        for ref in refs[first : first + count]:
            out[at : at + ref.shape[0], :] = ref[...]
            at += ref.shape[0]
        first += count


def joined(*lists, near=None):
    blocks = [block for one in lists for block in one]
    return call(
        join,
        tuple(shape((sum(block.shape[0] for block in one), one[0].shape[1]), bf16) for one in lists),
        blocks,
        [VMEM] * len(blocks),
        (VMEM,) * len(lists),
        moved=sum(block.shape[0] for block in blocks) * COLS * 4,
        counts=tuple(len(one) for one in lists),
        near=near,
    )


def layer_norm(values):
    centred = values - jnp.mean(values, axis=-1, keepdims=True)
    spread_of = jnp.mean(centred * centred, axis=-1, keepdims=True)
    inverse = lax.rsqrt(spread_of + EPSILON)
    return centred * inverse, inverse


def norm_back(upstream, normed, inverse, gain):
    scaled = upstream * gain
    return inverse * (
        scaled
        - jnp.mean(scaled, axis=-1, keepdims=True)
        - normed * jnp.mean(scaled * normed, axis=-1, keepdims=True)
    )


def attend_heads(lengths, x, vectors, weight, q_out, k_out, v_out, mixed, logsum, pair):
    width = x.shape[1]
    rows = x[...]
    scaling = HD ** (-0.5)
    for half in range(2):
        c = slice(half * COLS, (half + 1) * COLS)
        part = dot(rows, weight[:, half * 3 * COLS : (half + 1) * 3 * COLS])
        q_out[:, c] = (
            (part[:, :COLS] + vectors[0:1, c]).astype(bf16).astype(f32) * scaling
        ).astype(bf16)
        k_out[:, c] = part[:, COLS : 2 * COLS].astype(bf16)
        v_out[:, c] = (part[:, 2 * COLS :] + vectors[1:2, c]).astype(bf16)
    slots = rows.shape[0]
    lane = lax.broadcasted_iota(jnp.int32, (slots, 128), 1)
    low = lane < HD
    slot = lax.broadcasted_iota(jnp.int32, (1, slots), 1)
    bias = jnp.where(slot < lengths[pair], 0.0, MASKED).astype(f32)

    def heads(h, sums):
        s = pl.ds(al(h * 128, 128), 128)
        q1, k1, v1 = q_out[:, s], k_out[:, s], v_out[:, s]
        results, peaks = [], []
        for e in range(2):
            mask = low if e == 0 else ~low
            scores = nt(jnp.where(mask, q1, 0).astype(bf16), k1) + bias
            peak = jnp.max(scores, axis=1, keepdims=True)
            expo = jnp.exp(scores - peak).astype(bf16)
            results.append(dot(expo, jnp.where(mask, v1, 1).astype(bf16)))
            peaks.append(peak)
        total = pltpu.roll(jnp.where(low, results[1], results[0]), HD, 1)
        mixed[:, s] = (jnp.where(low, results[0], results[1]) / total).astype(bf16)
        sums = jnp.where(lane % HD == h, jnp.where(low, peaks[0], peaks[1]) + jnp.log(total), sums)
        return sums

    sums = lax.fori_loop(0, H // 2, heads, jnp.zeros((slots, 128), f32), unroll=True)
    turned = sums.T
    logsum[0, :8] = turned[:8]
    logsum[0, 8:] = turned[HD : HD + 8]


def attend(pos, lengths, x, wq, wk, wv, vectors, *rest):
    held, (q_out, k_out, v_out, mixed, logsum, w_out, weight, sems) = rest[:2], rest[2:]
    depth, width = wq.shape
    pair = pl.program_id(0)
    places = [
        (weight.at[:, pl.ds((half * 3 + m) * COLS, COLS)], pl.ds(m * width + half * COLS, COLS))
        for half in range(2)
        for m in range(3)
    ]
    writes = [
        pltpu.make_async_copy(place, w_out.at[:, c], sems.at[sems.shape[0] - 1 - i])
        for i, (place, c) in enumerate(places)
    ]

    @pl.when(pair == 0)
    def _():
        copies = Copies(sems)
        for half in range(2):
            for m, ref in enumerate((wq, wk, wv)):
                copies.add(
                    ref.at[:, pl.ds(half * COLS, COLS)],
                    own_slab(weight, pos[0], depth, (half * 3 + m) * COLS, COLS),
                )
        fetch(copies, pos, [("halves", weight, depth)], held)
        copies.wait()
        for write in writes:
            write.start()

    attend_heads(lengths, x, vectors, weight, q_out, k_out, v_out, mixed, logsum, pair)

    @pl.when(pair == pl.num_programs(0) - 1)
    def _():
        for write in writes:
            write.wait()


def expand(pos, x, mixed, wu, wo, vectors, up_bias, *rest):
    held, rest = rest[:8], rest[8:]
    act, slope, normed, inverse, wu_out, wo_out, up, out_w, xs, mixes, acts, slopes, normals, scales = rest[:14]
    row_sems, near_sems, far_sems, store_sems = rest[14:]
    depth = wo.shape[0]
    count = row_sems.shape[0]
    rows = xs.shape[0] // count
    chunk = 768
    loads = [Copies(row_sems.at[i]) for i in range(count)]
    near, far, stores = Copies(near_sems), Copies(far_sems), Copies(store_sems)
    parts = [("wide", up, depth), ("0", out_w, depth)]
    for i, load in enumerate(loads):
        s = pl.ds(i * rows, rows)
        load.add(mixed.at[s, :], mixes.at[s, :])
        load.add(x.at[s, :], xs.at[s, :])
        if i == 0:
            near.add(wo, own_slab(out_w, pos[0], depth))
            fetch(near, pos, parts, held, 1)
    far.add(wu, own_slab(up, pos[0], depth))
    fetch(far, pos, parts, held, 0)
    near.wait()
    hidden = []
    for i, load in enumerate(loads):
        load.wait()
        s = pl.ds(i * rows, rows)
        first = xs[s, :].astype(f32) + dot(mixes[s, :], out_w[...]) + vectors[2:3, :]
        normal, scale = layer_norm(first)
        normals[s, :] = normal
        scales[s, :] = jnp.broadcast_to(scale, (rows, scales.shape[1]))
        stores.add(normals.at[s, :], normed.at[s, :])
        stores.add(scales.at[s, :], inverse.at[s, :])
        hidden.append((normal * vectors[3:4, :] + vectors[4:5, :]).astype(bf16))
    far.wait()
    stores.add(up, wu_out)
    stores.add(out_w, wo_out)
    for j in range(up.shape[1] // chunk):
        c = slice(j * chunk, (j + 1) * chunk)
        for i in range(count):
            s = pl.ds(i * rows, rows)
            u = dot(hidden[i], up[:, c]) + up_bias[:, c]
            cdf, pdf = gaussian(u)
            acts[s, c] = (u * cdf).astype(bf16)
            slopes[s, c] = (cdf + u * pdf).astype(bf16)
            stores.add(acts.at[s, c], act.at[s, c])
            stores.add(slopes.at[s, c], slope.at[s, c])
    stores.wait()


def gaussian(u):
    return 0.5 + 0.5 * lax.erf(u * ROOT_HALF), jnp.exp(-0.5 * u * u) * DENSITY


def feed_forward(pos, lengths, act, slope, normed, inverse, cotangent, mixed, wd, wu, wo, vectors, *rest):
    held, rest = rest[:8], rest[8:]
    output, grad_first, grad_mixed, down_send, down_keep, send, keep = rest[:7]
    down, up, out_w, acts, slopes, normals, scales, cots, mixes, hiddens, lows, lows_first = rest[7:19]
    mixed_grads, grad_out, blocks, sems, block_sems, late_sems, store_sems, out_sems = rest[19:]
    total, width = mixes.shape
    wide = acts.shape[1]
    depth = wd.shape[0]
    count = block_sems.shape[1]
    rows = total // count
    chunk = 768

    def at(i):
        return pl.ds(i * rows, rows)

    def load(k, i):
        source, held_at = ((act, acts), (normed, normals), (cotangent, cots), (slope, slopes))[k]
        return pltpu.make_async_copy(source.at[at(i), :], held_at.at[at(i), :], block_sems.at[k, i])

    weights = Copies(sems)
    weights.add(wd, own_slab(down, pos[0], depth))
    fetch(weights, pos, [("slab", down, depth)], held)
    for k in range(3):
        load(k, 0).start()
    late = Copies(late_sems)
    weights.wait()
    load(3, 0).start()
    stores = Copies(store_sems)
    sums = [jnp.zeros((1, width), f32)] * 6
    up_sums = [jnp.zeros((1, chunk), f32)] * (wide // chunk)
    first_gain, gain = vectors[3:4, :], vectors[6:7, :]

    def column_sums(values):
        return jnp.sum(values, axis=0, keepdims=True)

    def begin(i):
        for k in range(3):
            load(k, i).wait()
        if i == 0:
            for source, place in ((wu, up), (wo, out_w), (inverse, scales)):
                late.add(source, place)
        if i + 1 < count:
            for k in range(3):
                load(k, i + 1).start()
        else:
            late.add(mixed, mixes)
        return dot(acts[at(i), :], down[...])

    def middle(i, product):
        s = at(i)
        per_pair = count // lengths.shape[0]
        slot = lax.broadcasted_iota(jnp.int32, (rows, 1), 0) + (i % per_pair) * rows
        mask = (slot < lengths[i // per_pair]).astype(f32)
        hidden = normals[s, :] * first_gain + vectors[4:5, :]
        hiddens[s, :] = hidden.astype(bf16)
        normal, scale = layer_norm(hidden + product + vectors[5:6, :])
        upstream = cots[s, :].astype(f32) * mask
        cots[s, :] = ((normal * gain + vectors[7:8, :]) * mask).astype(bf16)
        stores.add(cots.at[s, :], output.at[s, :])
        grad_second = norm_back(upstream, normal, scale, gain)
        low = grad_second.astype(bf16)
        lows[s, :] = low
        for k, value in enumerate((upstream * normal, upstream, low.astype(f32))):
            sums[k] = sums[k] + column_sums(value)
        return grad_second, low

    def grow(i, low):
        s = at(i)
        load(3, i).wait()
        if i + 1 < count:
            load(3, i + 1).start()
        for j in range(wide // chunk):
            c = slice(j * chunk, (j + 1) * chunk)
            grown = (nt(low, down[c, :]) * slopes[s, c].astype(f32)).astype(bf16)
            slopes[s, c] = grown
            up_sums[j] = up_sums[j] + column_sums(grown.astype(f32))

    def shrink(i):
        if i == 0:
            for copy in late.held[:3]:
                copy.wait()
        return nt(slopes[at(i), :], up[...])

    def end(i, grad_second, product):
        s = at(i)
        normal = normals[s, :]
        upstream = grad_second + product
        result = norm_back(upstream, normal, scales[s, 0:1], first_gain)
        normals[s, :] = result
        stores.add(normals.at[s, :], grad_first.at[s, :])
        low = result.astype(bf16)
        lows_first[s, :] = low
        mixed_grads[s, :] = nt(low, out_w[...]).astype(bf16)
        stores.add(mixed_grads.at[s, :], grad_mixed.at[s, :])
        for k, value in enumerate((upstream * normal, upstream, low.astype(f32))):
            sums[3 + k] = sums[3 + k] + column_sums(value)

    pieces = Copies(out_sems)

    def down_zone(zone):
        s = slice(zone * depth, (zone + 1) * depth)
        down[s, :] = tn(acts[:, s], lows[...]).astype(bf16)
        emit(pieces, pos, [("tall", down, depth)], down_send, down_keep, zones=(zone,))

    for a in range(0, count, 2):
        b = a + 1
        product_a = begin(a)
        second_a, low_a = middle(a, product_a)
        product_b = begin(b)
        grow(a, low_a)
        second_b, low_b = middle(b, product_b)
        grow(b, low_b)
        product_a = shrink(a)
        product_b = shrink(b)
        end(a, second_a, product_a)
        if b == count - 1:
            down_zone(0)
        end(b, second_b, product_b)
    for zone in range(1, wide // depth):
        down_zone(zone)
    up_depth = width // lax.axis_size("grp")
    grad_up = acts.at[pl.ds(0, width), :]
    late.held[3].wait()
    grad_out[...] = tn(mixes[...], lows_first[...]).astype(bf16)
    emit(pieces, pos, [("0", grad_out, up_depth)], send, keep, base=up_depth)
    vector_blocks(blocks, sums[:3] + up_sums + sums[3:])
    emit_vectors(pieces, pos, blocks, up_depth + up_depth // 4, send, keep)
    for j in range(wide // chunk):
        c = slice(j * chunk, (j + 1) * chunk)
        acts[:width, c] = tn(hiddens[...], slopes[:, c]).astype(bf16)
        emit(pieces, pos, [("wide", grad_up, up_depth)], send, keep, (j,))
    stores.wait()
    pieces.wait()


def vector_blocks(blocks, rows):
    blocks[...] = jnp.zeros_like(blocks)
    for p in range(min(LOCAL, len(rows))):
        here = rows[p::LOCAL]
        half = here[0].shape[1] // 2
        stacked = [part for row in here for part in (row[:, :half], row[:, half:])]
        stacked.append(jnp.zeros((16 - 2 * len(here), half), f32))
        blocks[p] = jnp.concatenate(stacked, axis=0).astype(bf16)


def vector_of(block, i):
    at = 2 * (i // LOCAL)
    return jnp.concatenate([block[at : at + 1, :], block[at + 1 : at + 2, :]], axis=1)


def emit_vectors(copies, pos, blocks, base, send, keep):
    for held, flip in ((send, 1), (keep, 0)):
        for zone in range(send.shape[0]):
            for q in range(4):
                owner = q * 2 + (pos[3] ^ flip)
                copies.add(blocks.at[owner], held.at[zone, q, pl.ds(base, 16), :])


def pair_back(lengths, q, k, v, mixed, grad_mixed, logsum, *rest, pair):
    if pair:
        old_sums, rest = rest[0], rest[2:]
    grads, sums, rows_of, held, deltas, in_sems, out_sem = rest
    slots, width = held.shape[0], q.shape[1]
    here = pl.ds(pair * slots, slots)
    spans = 2
    span = width // spans
    loads = [Copies(in_sems.at[i]) for i in range(spans)]
    for part, load in enumerate(loads):
        c = pl.ds(part * span, span)
        for i, ref in enumerate((mixed, grad_mixed, q, k, v)):
            load.add(ref.at[here, c], rows_of.at[i, :, c])
    stores = Copies(out_sem)
    sums[...] = old_sums[...] if pair else jnp.zeros_like(sums)
    low = lax.broadcasted_iota(jnp.int32, (slots, 128), 1) < HD
    slot = lax.broadcasted_iota(jnp.int32, (slots, 1), 0)
    scaling = HD ** (-0.5)
    bias = jnp.where(slot < lengths[pair], 0.0, MASKED).astype(f32)

    def heads(h, carry):
        s = pl.ds(al(h * 128, 128), 128)
        g1, q1, k1, v1 = (rows_of[i, :, s] for i in (1, 2, 3, 4))
        probs, scores_back, qs, gs, ks = [], [], [], [], []
        for e in range(2):
            mask = low if e == 0 else ~low
            qm = jnp.where(mask, q1, 0).astype(bf16)
            gm = jnp.where(mask, g1, 0).astype(bf16)
            prob = jnp.exp(nt(k1, qm) + bias - logsum[pair, pl.ds(h + 8 * e, 1), :])
            back = prob * (nt(v1, gm) - deltas[pl.ds(h * 2 + e, 1), :])
            probs.append(prob.astype(bf16))
            scores_back.append(back.astype(bf16))
            qs.append(qm)
            gs.append(gm)
            ks.append(jnp.where(mask, k1, 0).astype(bf16))
        grad_v = dot(jnp.concatenate(probs, 1), jnp.concatenate(gs, 0))
        grad_k = dot(jnp.concatenate(scores_back, 1), jnp.concatenate(qs, 0))
        grad_q = tn(jnp.concatenate(scores_back, 0), jnp.concatenate(ks, 0)) * scaling
        for m, value in enumerate((grad_q, grad_k, grad_v)):
            value = value.astype(bf16)
            held[:, pl.ds(al(m * width + h * 128, 128), 128)] = value
            if m != 1:
                sums[m : m + 1, s] += jnp.sum(value.astype(f32), axis=0, keepdims=True)
        return carry

    for part, load in enumerate(loads):
        load.wait()
        c = pl.ds(part * span, span)
        select = (
            lax.broadcasted_iota(jnp.int32, (16, span), 1) // HD + part * span // HD
            == lax.broadcasted_iota(jnp.int32, (16, span), 0)
        ).astype(bf16)
        product = rows_of[0, :, c].astype(f32) * rows_of[1, :, c].astype(f32)
        high = product.astype(bf16)
        rest_of = (product - high.astype(f32)).astype(bf16)
        delta = nt(select, high) + nt(select, rest_of)
        deltas[...] = delta if part == 0 else deltas[...] + delta
        lax.fori_loop(part * span // 128, (part + 1) * span // 128, heads, 0, unroll=True)
        for m in range(3):
            here_m = pl.ds(m * width + part * span, span)
            stores.add(held.at[:, here_m], grads.at[here, here_m])
    stores.wait()


def heads_weights(pos, x, grads, sums, send, keep, xs, held, weight_grads, blocks, sems, out_sems):
    width = xs.shape[1]
    depth = width // lax.axis_size("grp")
    copies = Copies(sems)

    def add(m):
        c = pl.ds(m * width, width)
        copies.add(grads.at[:, c], held.at[:, c])

    copies.add(x, xs)
    add(0)
    copies.wait()
    add(1)
    stores = Copies(out_sems)
    vector_blocks(blocks, [sums[m : m + 1, :] for m in (0, 2)])
    emit_vectors(stores, pos, blocks, 3 * depth // 4, send, keep)
    for m in range(3):
        c = slice(m * width, (m + 1) * width)
        if m:
            copies.held[1 + m].wait()
        if m == 1:
            add(2)
        weight_grads[:, c] = tn(xs[...], held[:, c]).astype(bf16)
        emit(stores, pos, [(str(m * width), weight_grads, depth)], send, keep, base=m * depth // 4)
    stores.wait()


def inputs_back(grad_first, grads, weight, out):
    out[...] = (grad_first[...] + nt(grads[...], weight[...])).astype(bf16)


def place_ffn(pos, mine, sibling, gd, gu, go, g2, s2, bd, bu, g1, s1, bo, small):
    tall, half, quarter = gd.shape[0] // LOCAL, gu.shape[0] // 2, go.shape[0] // 4
    n = mine.shape[0] // 4 - 2 * tall
    for sib, held in ((0, mine), (1, sibling)):
        for other in range(4):
            owner = pos[4] ^ (other * 2) ^ sib
            at = other * 2 * tall
            for j in range(2):
                gd[pl.ds(al(owner * tall, 16), tall), j * COLS : (j + 1) * COLS] = held[
                    at : at + tall, :
                ].astype(f32)
                at += tall
            at = 8 * tall + (0, 2, 1, 3)[other] * n
            for j in range(2):
                first = pl.ds(al((owner // 2) * 2 * COLS + j * COLS, 128), COLS)
                gu[pl.ds(al((owner % 2) * half, 16), half), first] = held[at : at + half, :].astype(f32)
                at += half
            rows = pl.ds(al((owner // 2) * quarter, 16), quarter)
            go[rows, pl.ds(al((owner % 2) * COLS, 128), COLS)] = held[at : at + quarter, :].astype(f32)
            at += quarter
            small[owner] = held[at : at + 16, :].astype(f32)

    for i, out in ((0, g2), (1, s2), (2, bd), (7, g1), (8, s1), (9, bo)):
        out[...] = own_part(pos, vector_of(small[i % LOCAL], i), out.shape[1])
    total = jnp.zeros(bu.shape, f32)
    for zone in range(4):
        total = jnp.where(pos[0] == zone, vector_of(small[3 + zone], 3 + zone), total)
    bu[...] = total


def own_part(pos, row, size):
    total = row[:, :size]
    for zone in range(1, row.shape[1] // size):
        total = jnp.where(pos[0] == zone, row[:, zone * size : (zone + 1) * size], total)
    return total


def place_heads(pos, mine, sibling, gq, gk, gv, bq, bv, small):
    quarter = gq.shape[0] // 4
    n = mine.shape[0] // 4
    for sib, held in ((0, mine), (1, sibling)):
        for other in range(4):
            owner = pos[4] ^ (other * 2) ^ sib
            row4 = pl.ds(al((owner // 2) * quarter, 16), quarter)
            col2 = pl.ds(al((owner % 2) * COLS, 128), COLS)
            at = other * n
            for out in (gq, gk, gv):
                out[row4, col2] = held[at : at + quarter, :].astype(f32)
                at += quarter
            small[owner] = held[at : at + 16, :].astype(f32)[:8]
    for i, out in enumerate((bq, bv)):
        out[...] = own_part(pos, vector_of(small[i], i), out.shape[1])


def shards(
    tokens,
    lengths,
    cotangent,
    query_weight,
    query_bias,
    key_weight,
    value_weight,
    value_bias,
    out_weight,
    out_bias,
    norm_gain,
    norm_shift,
    up_weight,
    up_bias,
    down_weight,
    down_bias,
    final_gain,
    final_shift,
):
    groups = lax.axis_size("grp")
    pairs, seqlen, width = tokens.shape
    rows = pairs * seqlen
    depth = width // groups
    wide = up_weight.shape[1]
    inputs = tokens.reshape(rows, width)
    upstream = cotangent.reshape(rows, width)
    pos = position()
    n1 = 3 * depth // 4
    n2 = depth + depth // 4
    n3 = depth

    def cut(kernel, sizes, args, specs):
        return pl.pallas_call(
            kernel,
            grid_spec=pltpu.PrefetchScalarGridSpec(
                num_scalar_prefetch=1,
                grid=(1,),
                in_specs=specs,
                out_specs=[pl.BlockSpec(size, lambda i, at: (0, 0)) for size in sizes],
            ),
            out_shape=[shape(size, bf16) for size in sizes],
            name=kernel.__name__,
        )(pos, *args)

    square = pl.BlockSpec((depth // 4, COLS), lambda i, at: (at[4] // 2, at[4] % 2))
    tall = pl.BlockSpec((down_weight.shape[0] // LOCAL, width), lambda i, at: (at[4], 0))
    first, third = cut(
        cut_first,
        ((depth // 4, 3 * COLS), (n3 // 2, width)),
        (query_weight, key_weight, value_weight, down_weight),
        [square] * 3 + [tall],
    )
    z1 = [to_grp(first, step) for step in range(1, groups)]
    close = to_grp(third, 1)
    small = jnp.concatenate(
        after(
            [
                query_bias,
                value_bias,
                out_bias,
                norm_gain,
                norm_shift,
                down_bias,
                final_gain,
                final_shift,
                up_bias,
            ],
            first,
        )
    )
    count = small.shape[0] // COLS
    small = jnp.pad(small.reshape(count, COLS), ((0, 16 - count), (0, 0)))
    (second,) = cut(
        cut_more,
        ((n2 + 16, COLS),),
        (out_weight, up_weight, small),
        [
            square,
            pl.BlockSpec((depth // 2, 2 * COLS), lambda i, at: (at[4] % 2, at[4] // 2)),
            pl.BlockSpec((16, COLS), lambda i, at: (0, 0)),
        ],
    )
    z1 = after(z1, second)

    def near(mine):
        return [mine, *(to_rep(mine, bit) for bit in (2, 4, 6))]

    def other_core(held):
        return [to_rep(part, 1) for part in held]

    mine1 = jnp.concatenate(z1, axis=0)
    from_x, from_y = to_rep(mine1, 2), to_rep(mine1, 4)
    far = [to_grp(second, 2), to_grp(second, 3)]
    cut_at = (mine1.shape[0] // 2 + 15) // 16 * 16
    low, high = to_rep(from_x[:cut_at], 4), to_rep(from_y[cut_at:], 2)
    parts = [second, to_grp(after(second, (from_x, from_y)), 1), *far]
    parts[1:] = after(parts[1:], (low, high))
    mine2 = jnp.concatenate([part[:n2] for part in parts[1:]], axis=0)
    held2 = near(mine2)
    held1 = jnp.concatenate([mine1, from_x, from_y, low, high], axis=0)
    held1 = [held1, to_rep(held1, 1)]
    flat = jnp.stack([part[n2 : n2 + count].reshape(-1) for part in parts])
    by_zone = jnp.stack([flat[pos[0] ^ zone] for zone in range(groups)]).astype(f32)
    vectors = by_zone[:, : 8 * depth].reshape(groups, 8, depth).transpose(1, 0, 2).reshape(8, width)
    up_vector = by_zone[:, 8 * depth :].reshape(1, wide)
    third, close = after((third, close), mine2)
    far = [to_grp(third, 2), to_grp(third, 3)]

    mat = shape((rows, width), bf16)
    mat32 = shape((rows, width), f32)
    dense = 2 * rows * width * width
    by_pair = pl.BlockSpec((seqlen, width), lambda i: (i, 0))
    q, k, v, mixed, logsum, w_all = call(
        attend,
        (mat, mat, mat, mat, shape((pairs, 16, seqlen), f32), shape((width, 3 * width), bf16)),
        (pos, lengths, after(inputs, (mine2, close)), query_weight, key_weight, value_weight, vectors, *held1),
        [SMEM, SMEM, by_pair, ANY, ANY, ANY, VMEM] + [ANY] * 2,
        (by_pair,) * 4 + (pl.BlockSpec((1, 16, seqlen), lambda i: (i, 0, 0)), ANY),
        scratch=[
            pltpu.VMEM((width, 3 * width), bf16),
            pltpu.SemaphoreType.DMA((12 + 8 * (groups - 1),)),
        ],
        grid=(pairs,),
        flops=12 * dense,
        moved=12 * rows * width,
    )
    held2, far = after((held2, far), w_all)
    held2 += other_core(held2)
    (mine3,) = joined((close, *far))
    held3 = near(mine3)
    held3 += other_core(held3[:1])
    halves = rows // 512
    act, slope, normed, inverse, wu_all, wo_all = call(
        expand,
        (
            shape((rows, wide), bf16),
            shape((rows, wide), bf16),
            mat32,
            shape((rows, 128), f32),
            shape((width, wide), bf16),
            shape((width, width), bf16),
        ),
        (pos, after(inputs, held3[0]), mixed, up_weight, out_weight, vectors, up_vector, *held2),
        [SMEM, ANY, ANY, ANY, ANY, VMEM, VMEM] + [ANY] * 8,
        (ANY,) * 6,
        scratch=[
            pltpu.VMEM((width, wide), bf16),
            pltpu.VMEM((width, width), bf16),
            pltpu.VMEM((rows, width), bf16),
            pltpu.VMEM((rows, width), bf16),
            pltpu.VMEM((rows, wide), bf16),
            pltpu.VMEM((rows, wide), bf16),
            pltpu.VMEM((rows, width), f32),
            pltpu.VMEM((rows, 128), f32),
            pltpu.SemaphoreType.DMA((halves, 2)),
            pltpu.SemaphoreType.DMA((1 + 8 * (groups - 1),)),
            pltpu.SemaphoreType.DMA((1 + 8 * (groups - 1) * 2,)),
            pltpu.SemaphoreType.DMA((2 + 2 * halves + 2 * halves * wide // 768,)),
        ],
        flops=8 * dense,
        moved=18 * rows * width,
    )
    held3 = after(held3, wo_all)
    held3 += other_core(held3[1:4])

    vec = shape((8, width), f32)

    def travelling(n):
        return (shape((groups, 4, n, COLS), bf16),) * 2

    n_up = depth + depth // 4 + 16
    output, grad_first, grad_mixed, down_send, down_keep, send, keep = call(
        feed_forward,
        (mat, mat32, mat, *travelling(n3), *travelling(n_up)),
        (pos, lengths, act, slope, normed, inverse, upstream, mixed, down_weight, wu_all, wo_all, vectors)
        + tuple(held3),
        [SMEM, SMEM] + [ANY] * 9 + [VMEM] + [ANY] * 8,
        (ANY,) * 7,
        scratch=[
            pltpu.VMEM((wide, width), bf16),
            pltpu.VMEM((width, wide), bf16),
            pltpu.VMEM((width, width), bf16),
            pltpu.VMEM((rows, wide), bf16),
            pltpu.VMEM((rows, wide), bf16),
            pltpu.VMEM((rows, width), f32),
            pltpu.VMEM((rows, 128), f32),
            pltpu.VMEM((rows, width), bf16),
            pltpu.VMEM((rows, width), bf16),
            pltpu.VMEM((rows, width), bf16),
            pltpu.VMEM((rows, width), bf16),
            pltpu.VMEM((rows, width), bf16),
            pltpu.VMEM((rows, width), bf16),
            pltpu.VMEM((width, width), bf16),
            pltpu.VMEM((LOCAL, 16, COLS), bf16),
            pltpu.SemaphoreType.DMA((1 + 8 * (groups - 1),)),
            pltpu.SemaphoreType.DMA((4, halves)),
            pltpu.SemaphoreType.DMA((4,)),
            pltpu.SemaphoreType.DMA((3 * halves,)),
            pltpu.SemaphoreType.DMA((groups * 4 * 2 * 6,)),
        ],
        flops=22 * dense,
        moved=50 * rows * width,
    )
    down = Reduce(pos, down_send, down_keep)
    up = Reduce(pos, after(send, down.got), keep)
    done = down.one()
    done = up.one(done)

    n_heads = n1 + 16
    grads = sums = None
    for pair in range(pairs):
        grads, sums = call(
            pair_back,
            (shape((rows, 3 * width), bf16), vec),
            (lengths, q, k, v, mixed, grad_mixed, after(logsum, done))
            + ((sums, grads) if pair else ()),
            [SMEM] + [ANY] * 5 + [VMEM] + ([VMEM, ANY] if pair else []),
            (ANY, VMEM),
            scratch=[
                pltpu.VMEM((5, seqlen, width), bf16),
                pltpu.VMEM((seqlen, 3 * width), bf16),
                pltpu.VMEM((16, seqlen), f32),
                pltpu.SemaphoreType.DMA((2, 5)),
                pltpu.SemaphoreType.DMA((6,)),
            ],
            flops=12 * dense // pairs,
            moved=12 * rows * width,
            aliases={8: 0} if pair else None,
            limit=MIDDLE_LIMIT,
            pair=pair,
        )
        if pair == 0:
            done = down.two(grads, near=(True, True))
    done = up.two(grads, near=(True, True))
    done = down.three(done, near=(True, True))
    send, keep = call(
        heads_weights,
        travelling(n_heads),
        (pos, after(inputs, done), grads, sums),
        [SMEM, ANY, ANY, VMEM],
        (ANY, ANY),
        scratch=[
            pltpu.VMEM((rows, width), bf16),
            pltpu.VMEM((rows, 3 * width), bf16),
            pltpu.VMEM((width, 3 * width), bf16),
            pltpu.VMEM((LOCAL, 16, COLS), bf16),
            pltpu.SemaphoreType.DMA((4,)),
            pltpu.SemaphoreType.DMA((groups * 4 * 2 * 4,)),
        ],
        flops=3 * dense,
        moved=12 * rows * width,
        limit=MIDDLE_LIMIT,
    )
    heads = Reduce(pos, after(send, (up.ra, up.rb, down.arrived)), keep)
    done = up.three(down.arrived, near=(True, True))
    done = heads.one(done)
    row_block = rows // halves
    by_row = pl.BlockSpec((row_block, width), lambda i: (i, 0))
    grad_inputs = call(
        inputs_back,
        mat,
        (after(grad_first, done), grads, w_all),
        [by_row, pl.BlockSpec((row_block, 3 * width), lambda i: (i, 0)), VMEM],
        by_row,
        grid=(halves,),
        flops=3 * dense,
        moved=16 * rows * width,
        limit=MIDDLE_LIMIT,
    )
    done = heads.two(grad_inputs, up.arrived, near=(True, True))
    down_total = down.four(done, near=(True, True))
    up_total = up.four(down_total, near=(True, True))
    down_total, up_total = after((down_total, up_total), heads.ja)
    heads.three(near=(True, True))
    near_down, near_up = after((to_rep(down_total, 2), to_rep(up_total, 4)), heads.blocks[0])
    down_pair, up_pair = joined((down_total, near_down), (up_total, near_up), near=(True, True))
    (both,) = joined(
        (down_pair, to_rep(down_pair, 4), up_pair, to_rep(up_pair, 2)), near=(True, True)
    )
    heads.four(near=(True, True))
    heads.around()
    both = both, to_rep(after(both, heads.arrived), 1)
    vector = shape((1, depth), f32)
    square = shape((depth, width), f32)
    gd, gu, go, g2, s2, bd, bu, g1, s1, bo = call(
        place_ffn,
        (shape((wide // groups, width), f32), shape((depth, wide), f32), square)
        + (vector,) * 3
        + (shape((1, wide // groups), f32),)
        + (vector,) * 3,
        (pos, *both),
        [SMEM, VMEM, VMEM],
        (VMEM,) * 10,
        scratch=[pltpu.VMEM((LOCAL, 16, COLS), f32)],
        moved=24 * depth * width,
        near=(True, False),
    )
    heads.five(gd)
    gq, gk, gv, bq, bv = call(
        place_heads,
        (square,) * 3 + (vector,) * 2,
        (pos, *heads.both),
        [SMEM] + [VMEM] * 2,
        (VMEM,) * 5,
        scratch=[pltpu.VMEM((LOCAL, 8, COLS), f32)],
        moved=24 * depth * width,
        near=(True, False),
    )
    bq, bv, bo, g1, s1, bu, bd, g2, s2 = (
        row.reshape(-1) for row in (bq, bv, bo, g1, s1, bu, bd, g2, s2)
    )
    return (
        output.reshape(pairs, seqlen, width),
        grad_inputs.reshape(pairs, seqlen, width),
        gq,
        bq,
        gk,
        gv,
        bv,
        go,
        bo,
        g1,
        s1,
        gu,
        bu,
        gd,
        bd,
        g2,
        s2,
    )


def solution(mesh):
    pairs = P(("grp", "rep"), None, None)
    matrix = P("grp", None)
    vector = P("grp")
    placed = (pairs, P(("grp", "rep")), pairs, matrix, vector, matrix, matrix, vector, matrix, vector)
    placed += (vector, vector, matrix, vector, matrix, vector, vector, vector)
    results = (pairs, pairs, matrix, vector, matrix, matrix, vector, matrix, vector, vector, vector)
    results += (matrix, vector, matrix, vector, vector, vector)
    return jax.shard_map(shards, mesh=mesh, in_specs=placed, out_specs=results, check_vma=False)
```
